32 devices in a mesh: gx: 8 (over z, x), gy: 4 (over y, core).
Axes of the slice: x: 2, y: 2, z: 4, core: 2. Of those that a mesh axis runs over, the one named last changes fastest.
Arguments:
- leaf_maps: float32 [1, 4096, 8192], P(None, 'gy', 'gx'), may hold values from -5 to 14, as said below
Outputs:
- quad_maps: float32 [1, 4096, 8192], P(None, 'gy', 'gx')
The draws below stay inside these ranges and needn't reach their ends.
Inputs may be any that keep to these rules, and one draw needn't show every extreme that they name: `leaf_maps`: every patch's block is symmetric and positive definite.
All inputs are finite; a program needn't handle non-finite values.
Results may differ from the reference program's by a relative error of at most 0.000067.
Values sent between devices are 32-bit elements; how exact they have to be, the bound alone decides.
No kernel may reach another device: no remote copies, remote signals or barrier semaphores. Data moves between devices by JAX's collectives and lax.ppermute only.
A program may use at most 128 MiB of HBM per device.

```python
import math
import jax
import jax.numpy as jnp
from jax import lax

E = 256
FIELDS = 1
ROWS = 4096
COLS = 8192
N_GX = 8
N_GY = 4


def draw_leaf_maps(key, part):
    side_cells = 4 * E
    blocks_y = ROWS // side_cells
    blocks_x = COLS // side_cells
    block_count = FIELDS * blocks_y * blocks_x

    def one_block(index):
        block_key = jax.random.fold_in(key, index)
        factor_key, scale_key = jax.random.split(block_key)
        factor = jnp.clip(jax.random.normal(factor_key, (side_cells, side_cells), jnp.float32), -6.0, 6.0)
        scales = jnp.exp(jax.random.uniform(scale_key, (side_cells,), jnp.float32, 0.0, math.log(1.5)))
        gram = jnp.dot(factor, factor.T, precision=lax.Precision.HIGHEST) / float(side_cells)
        gram = 0.5 * (gram + gram.T)
        shifted = scales[:, None] * gram * scales[None, :]
        return shifted + 0.25 * jnp.eye(side_cells, dtype=jnp.float32)
    blocks = lax.map(one_block, jnp.arange(block_count, dtype=jnp.int32))
    blocks = blocks.reshape(FIELDS, blocks_y, blocks_x, side_cells, side_cells).transpose(0, 1, 3, 2, 4)
    return blocks.reshape(FIELDS, ROWS, COLS).astype(jnp.float32)


def setup_inputs(seed: int = 0) -> dict:
    splits = jax.random.split(jax.random.key(seed), 2)
    leaf_maps = draw_leaf_maps(jax.random.fold_in(splits[1], 71), 0)
    return dict(leaf_maps=leaf_maps)


def pick_rows(matrix, labels, row_labels, edge_width):
    return jnp.concatenate([matrix[:, labels.index(label_id) * edge_width:(labels.index(label_id) + 1) * edge_width, :] for label_id in row_labels], axis=1)

def pick_cols(matrix, labels, col_labels, edge_width):
    return jnp.concatenate([matrix[:, :, labels.index(label_id) * edge_width:(labels.index(label_id) + 1) * edge_width] for label_id in col_labels], axis=2)

def merge(first_map, first_labels, second_map, second_labels, shared, out_order, edge_width):
    coupling = pick_cols(pick_rows(first_map, first_labels, shared, edge_width), first_labels, shared, edge_width)
    coupling = coupling + pick_cols(pick_rows(second_map, second_labels, shared, edge_width), second_labels, shared, edge_width)
    pieces = []
    direct_rows = []
    for label_id in out_order:
        if label_id in first_labels:
            source, source_labels = (first_map, first_labels)
        else:
            source, source_labels = (second_map, second_labels)
        row_band = pick_rows(source, source_labels, [label_id], edge_width)
        pieces.append(pick_cols(row_band, source_labels, shared, edge_width))
        blocks = []
        for other_id in out_order:
            if other_id in source_labels:
                blocks.append(pick_cols(row_band, source_labels, [other_id], edge_width))
            else:
                blocks.append(jnp.zeros((row_band.shape[0], edge_width, edge_width), jnp.float32))
        direct_rows.append(jnp.concatenate(blocks, axis=2))
    edge_rows = jnp.concatenate(pieces, axis=1)
    direct = jnp.concatenate(direct_rows, axis=1)
    factor = jnp.linalg.cholesky(coupling)
    half_way = jax.scipy.linalg.solve_triangular(factor, jnp.swapaxes(edge_rows, 1, 2), lower=True)
    solved = jax.scipy.linalg.solve_triangular(factor, half_way, lower=True, trans=1)
    return direct - jnp.einsum('fik,fkj->fij', edge_rows, solved, precision=lax.Precision.HIGHEST)

def quad_map(quad_block):
    patch_len = 4 * E

    def leaf_at(x_pos, y_pos):
        return quad_block[:, y_pos * patch_len:(y_pos + 1) * patch_len, x_pos * patch_len:(x_pos + 1) * patch_len]
    low_pair = merge(leaf_at(0, 0), [0, 9, 2, 3], leaf_at(1, 0), [9, 1, 4, 5], [9], [0, 1, 2, 4, 3, 5], E)
    high_pair = merge(leaf_at(0, 1), [0, 9, 2, 3], leaf_at(1, 1), [9, 1, 4, 5], [9], [0, 1, 2, 4, 3, 5], E)
    return merge(low_pair, [0, 2, 4, 5, 10, 11], high_pair, [1, 3, 10, 11, 6, 7], [10, 11], [0, 2, 4, 5, 1, 3, 6, 7], E)

def reference(leaf_maps):
    patch_len = 4 * E
    half_rows = N_GY // 2
    half_cols = N_GX // 2
    all_quads = leaf_maps.reshape(FIELDS, 2, half_rows, patch_len, 2, half_cols, patch_len)
    all_quads = all_quads.transpose(2, 5, 0, 1, 3, 4, 6).reshape(half_rows * half_cols, FIELDS, 2 * patch_len, 2 * patch_len)
    merged = lax.map(quad_map, all_quads)
    merged = merged.reshape(half_rows, half_cols, FIELDS, 2, patch_len, 2, patch_len).transpose(2, 3, 0, 4, 5, 1, 6)
    return merged.reshape(FIELDS, ROWS, COLS)
```

```python
import jax
import jax.numpy as jnp
from jax import lax
from jax.experimental import pallas as pl
from jax.experimental.pallas import tpu as pltpu
from jax.sharding import PartitionSpec as P

F32 = jnp.float32
BF16 = jnp.bfloat16
T = 128
HBM = pl.BlockSpec(memory_space=pl.ANY)
VMEM = pl.BlockSpec(memory_space=pltpu.VMEM)
SMEM = pl.BlockSpec(memory_space=pltpu.SMEM)
PARAMS = pltpu.CompilerParams(vmem_limit_bytes=56 * 2**20)


def dot(a, b, dims=((1,), (0,))):
    return lax.dot_general(
        a, b, (dims, ((), ())), precision=lax.Precision.HIGHEST, preferred_element_type=F32
    )


def dot16(a, b, dims=((1,), (0,))):
    return lax.dot_general(a, b, (dims, ((), ())), preferred_element_type=F32)


def split(a):
    high = a.astype(BF16)
    return high, (a - high.astype(F32)).astype(BF16)


def dot3(a, b, dims=((1,), (0,))):
    return dot16(a[0], b[0], dims) + (dot16(a[0], b[1], dims) + dot16(a[1], b[0], dims))


NT = ((1,), (1,))
TN = ((0,), (0,))


def upper(n):
    return [(i, j) for i in range(n) for j in range(i, n)]


def panel(rows, c0):
    n = rows.shape[1]
    sub = lax.broadcasted_iota(jnp.int32, (8, n), 0)
    lane = lax.broadcasted_iota(jnp.int32, (8, n), 1)
    cols = [jnp.broadcast_to(rows[:, c0 + k : c0 + k + 1], (8, n)) for k in range(8)]
    out = jnp.where((lane >= c0) & (lane < c0 + 8), (lane - c0 == sub).astype(F32), rows)
    for k in range(8):
        inv = 1.0 / cols[k][k : k + 1, :]
        here = sub == k
        mult = cols[k]
        pivot_row = out[k : k + 1, :] * inv
        out = jnp.where(here, pivot_row, out - mult * pivot_row)
        for j in range(k + 1, 8):
            pivot = cols[j][k : k + 1, :] * inv
            cols[j] = jnp.where(here, pivot, cols[j] - mult * pivot)
    return out


def put_rows(matrix, rows, r0):
    parts = [matrix[:r0]] if r0 else []
    parts.append(rows)
    if r0 + rows.shape[0] < matrix.shape[0]:
        parts.append(matrix[r0 + rows.shape[0] :])
    return jnp.concatenate(parts, axis=0)


def invert_tiles(mats):
    n = mats[0].shape[0]
    lane = lax.broadcasted_iota(jnp.int32, (n, n), 1)
    for c0 in range(0, n, 8):
        done = []
        for m in mats:
            rows = panel(m[c0 : c0 + 8, :], c0)
            wide = put_rows(jnp.zeros((n, n), F32), rows, c0)
            rest = jnp.where((lane >= c0) & (lane < c0 + 8), 0.0, m) - dot(m, wide)
            done.append(put_rows(rest, rows, c0))
        mats = done
    return mats


def invert_in_place(refs):
    n = refs[0].shape[0]
    for p in range(0, n, T):
        pivots = invert_tiles([ref[p : p + T, p : p + T] for ref in refs])
        for ref, pivot in zip(refs, pivots):
            rows = dot(pivot, ref[p : p + T, :])
            parts = ([rows[:, :p]] if p else []) + [pivot]
            if p + T < n:
                parts.append(rows[:, p + T :])
            rows = jnp.concatenate(parts, axis=1)
            for q in range(0, n, T):
                if q != p:
                    change = dot(ref[q : q + T, p : p + T], rows)
                    ref[q : q + T, p : p + T] = jnp.zeros((T, T), F32)
                    ref[q : q + T, :] = ref[q : q + T, :] - change
            ref[p : p + T, :] = rows


def cut_kernel(place, leaf, inner, cross, outer, sem):
    e = leaf.shape[1] // 4
    v, u = place[0], place[1]
    ext = [v, 2 + u]
    inn = [1 - v, 3 - u]

    def src(side_r, side_c, r, c, size):
        return leaf.at[
            0,
            pl.ds(pl.multiple_of(side_r * e + r * size, T), size),
            pl.ds(pl.multiple_of(side_c * e + c * size, T), size),
        ]

    copies = []

    def add(source, target):
        copies.append(pltpu.make_async_copy(source, target, sem.at[len(copies)]))
        copies[-1].start()

    tiles = e // T
    at = 0
    for side in (1, 0):
        for r, c in upper(tiles):
            add(src(inn[side], inn[side], r, c, T), inner.at[pl.ds(at, T)])
            at += T
    for r in range(tiles):
        for c in range(tiles):
            add(src(inn[0], inn[1], r, c, T), inner.at[pl.ds(at, T)])
            at += T
    for r in range(2):
        for c in range(2):
            add(src(ext[r], inn[c], 0, 0, e), cross.at[pl.ds(r * e, e), pl.ds(c * e, e)])
    at = 0
    for r, c in upper(2 * tiles):
        add(
            src(ext[r // tiles], ext[c // tiles], r % tiles, c % tiles, T),
            outer.at[pl.ds(at, T)],
        )
        at += T
    for copy in copies:
        copy.wait()


def cut(place, leaf):
    e = leaf.shape[1] // 4
    tiles = e // T
    n_inner = 2 * len(upper(tiles)) + tiles * tiles
    n_outer = len(upper(2 * tiles))
    n_copies = n_inner + 4 + n_outer
    return pl.pallas_call(
        cut_kernel,
        out_shape=[
            jax.ShapeDtypeStruct((n_inner * T, T), F32),
            jax.ShapeDtypeStruct((2 * e, 2 * e), F32),
            jax.ShapeDtypeStruct((n_outer * T, T), F32),
        ],
        in_specs=[SMEM, HBM],
        out_specs=[HBM, HBM, HBM],
        scratch_shapes=[pltpu.SemaphoreType.DMA((n_copies,))],
        compiler_params=PARAMS,
        name="cut_leaf",
    )(place, leaf)


def unpack(ref, at, tiles):
    held = {}
    for r, c in upper(tiles):
        held[r, c] = ref[pl.ds(at, T), :]
        if c > r:
            held[c, r] = held[r, c].T
        at += T
    return jnp.concatenate(
        [jnp.concatenate([held[r, c] for c in range(tiles)], axis=1) for r in range(tiles)], axis=0
    )


def unpack_full(ref, at, tiles):
    rows = []
    for r in range(tiles):
        rows.append(
            jnp.concatenate([ref[pl.ds(at + (r * tiles + c) * T, T), :] for c in range(tiles)], axis=1)
        )
    return jnp.concatenate(rows, axis=0)


def factor_kernel(place, mine, across, along, corner, high, low, h0, h1, side, coup, full, cols):
    e = h0.shape[0]
    tiles = e // T
    sym = len(upper(tiles)) * T
    h0[...] = unpack(mine, 0, tiles) + unpack(along, 0, tiles)
    h1[...] = unpack(across, 0, tiles) + unpack(corner, 0, tiles)
    invert_in_place([h0, h1])
    coup[:e, :e] = unpack_full(mine, 2 * sym, tiles)
    coup[:e, e:] = unpack_full(across, 2 * sym, tiles)
    coup[e:, :e] = unpack_full(along, 2 * sym, tiles)
    coup[e:, e:] = unpack_full(corner, 2 * sym, tiles)
    cols[:, :e] = dot(coup[:, :e], h0[...])
    cols[:, e:] = dot(coup[:, e:], h1[...])
    side[...] = -dot(cols[...], coup[...], NT)
    side[:e, :e] = side[:e, :e] + (unpack(mine, sym, tiles) + unpack(across, sym, tiles))
    side[e:, e:] = side[e:, e:] + (unpack(along, sym, tiles) + unpack(corner, sym, tiles))
    invert_in_place([side])
    flow = cols[...]
    flow16 = split(flow)
    away = dot3(split(side[...]), flow16)
    full[...] = dot3(flow16, split(away), TN)
    full[:e, :e] = full[:e, :e] + h0[...]
    full[e:, e:] = full[e:, e:] + h1[...]

    def emit(value, rows, columns):
        high[rows, columns], low[rows, columns] = split(value)

    first, rest = slice(0, e), slice(e, 3 * e)
    emit(full[...], rest, rest)
    emit(-away[:e, :], first, rest)
    same = place[0] == place[1]

    @pl.when(same)
    def _():
        emit(side[:e, :e], first, first)
        emit(-away[:e, :].T, rest, first)

    @pl.when(jnp.logical_not(same))
    def _():
        emit(side[:e, e:], first, first)
        emit(-away[e:, :].T, rest, first)


def factor(place, mine, across, along, corner, e):
    return pl.pallas_call(
        factor_kernel,
        out_shape=[jax.ShapeDtypeStruct((3 * e, 3 * e), BF16)] * 2,
        in_specs=[SMEM, VMEM, VMEM, VMEM, VMEM],
        out_specs=[VMEM, VMEM],
        scratch_shapes=[
            pltpu.VMEM((e, e), F32),
            pltpu.VMEM((e, e), F32),
            pltpu.VMEM((2 * e, 2 * e), F32),
            pltpu.VMEM((2 * e, 2 * e), F32),
            pltpu.VMEM((2 * e, 2 * e), F32),
            pltpu.VMEM((2 * e, 2 * e), F32),
        ],
        compiler_params=PARAMS,
        cost_estimate=pl.CostEstimate(flops=30 * 10**9, bytes_accessed=5 * 10**6, transcendentals=0),
        name="invert_coupling",
    )(place, mine, across, along, corner)


def rows_kernel(mine, across, high, low, top, bottom):
    e = mine.shape[1] // 2
    whole = (high[...], low[...])
    for at, leaf in enumerate((mine, across)):
        first = split(leaf[:, :e])
        second = split(leaf[:, e:])
        inner = slice((1 + at) * e, (2 + at) * e)
        value = dot3(first, (whole[0][:e], whole[1][:e])) + dot3(
            second, (whole[0][inner], whole[1][inner])
        )
        rows = slice(2 * e * at, 2 * e * (at + 1))
        top[rows, :], bottom[rows, :] = split(value)


def row_products(mine, across, high, low):
    e = mine.shape[1] // 2
    return pl.pallas_call(
        rows_kernel,
        out_shape=[jax.ShapeDtypeStruct((4 * e, 3 * e), BF16)] * 2,
        in_specs=[VMEM] * 4,
        out_specs=[VMEM] * 2,
        compiler_params=PARAMS,
        cost_estimate=pl.CostEstimate(flops=3 * 10**9, bytes_accessed=7 * 10**6, transcendentals=0),
        name="row_products",
    )(mine, across, high, low)


def result_kernel(
    place, leaf, mine, across, along, corner, top, bottom, outer0, outer1, out, own, col, sem
):
    e = mine.shape[1] // 2
    tiles = e // T
    v, u = place[0], place[1]
    same = u == v
    ext = [v, 2 + u]
    copies = []
    for r in range(2):
        for c in range(2):
            copies.append(
                pltpu.make_async_copy(
                    leaf.at[
                        0,
                        pl.ds(pl.multiple_of(ext[r] * e, T), e),
                        pl.ds(pl.multiple_of(ext[c] * e, T), e),
                    ],
                    own.at[pl.ds(r * e, e), pl.ds(c * e, e)],
                    sem.at[2 * r + c],
                )
            )
            copies[-1].start()

    @pl.when(same)
    def _():
        col[0] = mine[...]
        col[1] = across[...]

    @pl.when(jnp.logical_not(same))
    def _():
        col[0] = along[...]
        col[1] = corner[...]

    def spot(side, which):
        return pl.ds(pl.multiple_of((2 * side + (v if which == 0 else 1 - v)) * e, T), e)

    for b in range(2):
        right = split(col[b])
        for a in range(2):
            rows = slice(2 * e * a, 2 * e * (a + 1))
            inner = slice((1 + b) * e, (2 + b) * e)
            left = [
                jnp.concatenate([ref[rows, :e], ref[rows, inner]], axis=1) for ref in (top, bottom)
            ]
            value = -dot3(left, right, NT)
            for r in range(2):
                for c in range(2):
                    out[0, spot(r, a), spot(c, b)] = value[r * e : (r + 1) * e, c * e : (c + 1) * e]
    for copy in copies:
        copy.wait()

    @pl.when(same)
    def _():
        held = {}
        for at, (i, j) in enumerate(upper(2 * tiles)):
            ref = outer0 if at < outer0.shape[0] // T else outer1
            at -= 0 if ref is outer0 else outer0.shape[0] // T
            held[i, j] = ref[at * T : (at + 1) * T, :]
            held[j, i] = held[i, j] if i == j else held[i, j].T
        for r in range(2):
            for c in range(2):
                out[0, spot(r, 0), spot(c, 0)] = (
                    out[0, spot(r, 0), spot(c, 0)] + own[r * e : (r + 1) * e, c * e : (c + 1) * e]
                )
                block = jnp.concatenate(
                    [
                        jnp.concatenate(
                            [held[r * tiles + i, c * tiles + j] for j in range(tiles)], axis=1
                        )
                        for i in range(tiles)
                    ],
                    axis=0,
                )
                out[0, spot(r, 1), spot(c, 1)] = out[0, spot(r, 1), spot(c, 1)] + block


def result(place, leaf, mine, across, along, corner, top, bottom, outer0, outer1):
    e = mine.shape[1] // 2
    return pl.pallas_call(
        result_kernel,
        out_shape=jax.ShapeDtypeStruct((1, 4 * e, 4 * e), F32),
        in_specs=[SMEM, HBM] + [VMEM] * 8,
        out_specs=VMEM,
        scratch_shapes=[
            pltpu.VMEM((2 * e, 2 * e), F32),
            pltpu.VMEM((2, 2 * e, 2 * e), F32),
            pltpu.SemaphoreType.DMA((4,)),
        ],
        compiler_params=PARAMS,
        cost_estimate=pl.CostEstimate(flops=4 * 10**9, bytes_accessed=12 * 10**6, transcendentals=0),
        name="result",
    )(place, leaf, mine, across, along, corner, top, bottom, outer0, outer1)


def solution(mesh):
    nx, ny = mesh.shape["gx"], mesh.shape["gy"]
    devices = [(x, y) for x in range(nx) for y in range(ny)]

    def is_same(x, y):
        return x // (nx // 2) == y // (ny // 2)

    def send(value, along_y, only=None):
        pairs = []
        for x, y in devices:
            if only is None or is_same(x, y) == only:
                to = (x, (y + ny // 2) % ny) if along_y else ((x + nx // 2) % nx, y)
                pairs.append((x * ny + y, to[0] * ny + to[1]))
        return lax.ppermute(value, ("gx", "gy"), pairs)

    def body(leaf):
        e = leaf.shape[1] // 4
        v = lax.axis_index("gx") // (nx // 2)
        u = lax.axis_index("gy") // (ny // 2)
        place = jnp.stack([v, u]).astype(jnp.int32)
        inner, cross, outer = cut(place, leaf)
        half = outer.shape[0] // 2
        inner_x = send(inner, False)
        inner_y = send(inner, True)
        passed = send(outer[half:], True, only=False)
        inner_d = send(inner_x, True)
        cross_x = send(cross, False)
        cross_y = send(cross, True, only=True)
        cross_d = send(cross_x, True, only=True)
        outer0 = send(jnp.where(u == v, passed, outer[:half]), False)
        outer1 = send(outer0, True, only=False)
        high, low = factor(place, inner, inner_x, inner_y, inner_d, e)
        top, bottom = row_products(cross, cross_x, high, low)
        return result(place, leaf, cross, cross_x, cross_y, cross_d, top, bottom, outer0, outer1)

    return jax.shard_map(
        body,
        mesh=mesh,
        in_specs=(P(None, "gy", "gx"),),
        out_specs=P(None, "gy", "gx"),
        check_vma=False,
    )
```

```python
import functools

import jax
import jax.numpy as jnp
from jax import lax
from jax.experimental import pallas as pl
from jax.experimental.pallas import tpu as pltpu
from jax.sharding import PartitionSpec as P

F32 = jnp.float32
BF16 = jnp.bfloat16
T = 128
HBM = pl.BlockSpec(memory_space=pl.ANY)
VMEM = pl.BlockSpec(memory_space=pltpu.VMEM)
SMEM = pl.BlockSpec(memory_space=pltpu.SMEM)
PARAMS = pltpu.CompilerParams(vmem_limit_bytes=56 * 2**20)


def dot(a, b, dims=((1,), (0,))):
    return lax.dot_general(
        a, b, (dims, ((), ())), precision=lax.Precision.HIGHEST, preferred_element_type=F32
    )


def dot16(a, b, dims=((1,), (0,))):
    return lax.dot_general(a, b, (dims, ((), ())), preferred_element_type=F32)


def split(a):
    high = a.astype(BF16)
    return high, (a - high.astype(F32)).astype(BF16)


def dot3(a, b, dims=((1,), (0,))):
    return dot16(a[0], b[0], dims) + (dot16(a[0], b[1], dims) + dot16(a[1], b[0], dims))


NT = ((1,), (1,))
TN = ((0,), (0,))


def upper(n):
    return [(i, j) for i in range(n) for j in range(i, n)]


def panel(rows, c0):
    n = rows.shape[1]
    sub = lax.broadcasted_iota(jnp.int32, (8, n), 0)
    lane = lax.broadcasted_iota(jnp.int32, (8, n), 1)
    cols = [jnp.broadcast_to(rows[:, c0 + k : c0 + k + 1], (8, n)) for k in range(8)]
    out = jnp.where((lane >= c0) & (lane < c0 + 8), (lane - c0 == sub).astype(F32), rows)
    for k in range(8):
        inv = 1.0 / cols[k][k : k + 1, :]
        here = sub == k
        mult = cols[k]
        pivot_row = out[k : k + 1, :] * inv
        out = jnp.where(here, pivot_row, out - mult * pivot_row)
        for j in range(k + 1, 8):
            pivot = cols[j][k : k + 1, :] * inv
            cols[j] = jnp.where(here, pivot, cols[j] - mult * pivot)
    return out


def put_rows(matrix, rows, r0):
    parts = [matrix[:r0]] if r0 else []
    parts.append(rows)
    if r0 + rows.shape[0] < matrix.shape[0]:
        parts.append(matrix[r0 + rows.shape[0] :])
    return jnp.concatenate(parts, axis=0)


def invert_tiles(mats):
    n = mats[0].shape[0]
    lane = lax.broadcasted_iota(jnp.int32, (n, n), 1)
    for c0 in range(0, n, 8):
        done = []
        for m in mats:
            rows = panel(m[c0 : c0 + 8, :], c0)
            wide = put_rows(jnp.zeros((n, n), F32), rows, c0)
            rest = jnp.where((lane >= c0) & (lane < c0 + 8), 0.0, m) - dot(m, wide)
            done.append(put_rows(rest, rows, c0))
        mats = done
    return mats


def invert_in_place(refs, start=0, stop=None):
    n = refs[0].shape[0]
    for p in range(start, n if stop is None else stop, T):
        pivots = invert_tiles([ref[p : p + T, p : p + T] for ref in refs])
        for ref, pivot in zip(refs, pivots):
            rows = dot(pivot, ref[p : p + T, :])
            parts = ([rows[:, :p]] if p else []) + [pivot]
            if p + T < n:
                parts.append(rows[:, p + T :])
            rows = jnp.concatenate(parts, axis=1)
            for q in range(0, n, T):
                if q != p:
                    change = dot(ref[q : q + T, p : p + T], rows)
                    ref[q : q + T, p : p + T] = jnp.zeros((T, T), F32)
                    ref[q : q + T, :] = ref[q : q + T, :] - change
            ref[p : p + T, :] = rows


def leaf_block(leaf, side_r, side_c, r, c, size):
    e = leaf.shape[1] // 4
    return leaf.at[
        0,
        pl.ds(pl.multiple_of(side_r * e + r * size, T), size),
        pl.ds(pl.multiple_of(side_c * e + c * size, T), size),
    ]


def run_copies(pairs, sem):
    copies = [pltpu.make_async_copy(a, b, sem.at[i]) for i, (a, b) in enumerate(pairs)]
    for copy in copies:
        copy.start()
    for copy in copies:
        copy.wait()


def cut_inner_kernel(place, leaf, hh, sr, sem):
    tiles = leaf.shape[1] // 4 // T
    x_in, y_in = 1 - place[0], 3 - place[1]
    pairs = []
    for at, (r, c) in enumerate(upper(tiles)):
        pairs.append((leaf_block(leaf, y_in, y_in, r, c, T), hh.at[pl.ds(at * T, T)]))
    for at, (r, c) in enumerate(upper(tiles)):
        pairs.append((leaf_block(leaf, x_in, x_in, r, c, T), sr.at[pl.ds(at * T, T)]))
    for at in range(tiles * tiles):
        r, c = at // tiles, at % tiles
        spot = (len(upper(tiles)) + at) * T
        pairs.append((leaf_block(leaf, x_in, y_in, r, c, T), sr.at[pl.ds(spot, T)]))
    run_copies(pairs, sem)


def cut_inner(place, leaf):
    tiles = leaf.shape[1] // 4 // T
    n_sym, n_full = len(upper(tiles)), tiles * tiles
    return pl.pallas_call(
        cut_inner_kernel,
        out_shape=[
            jax.ShapeDtypeStruct((n_sym * T, T), F32),
            jax.ShapeDtypeStruct(((n_sym + n_full) * T, T), F32),
        ],
        in_specs=[SMEM, HBM],
        out_specs=[VMEM, VMEM],
        scratch_shapes=[pltpu.SemaphoreType.DMA((2 * n_sym + n_full,))],
        compiler_params=PARAMS,
        name="cut_inner",
    )(place, leaf)


def cut_outer_kernel(place, leaf, *refs):
    *cross, outer0, outer1, sem = refs
    e = leaf.shape[1] // 4
    tiles = e // T
    v, u = place[0], place[1]
    ext = [v, 2 + u]
    inn = [1 - v, 3 - u]
    pairs = []
    row = 0
    for ref in cross:
        for at in range(0, ref.shape[0], T):
            for c in range(2):
                source = leaf.at[
                    0,
                    pl.ds(pl.multiple_of(ext[row // e] * e + row % e, T), T),
                    pl.ds(pl.multiple_of(inn[c] * e, T), e),
                ]
                pairs.append((source, ref.at[pl.ds(at, T), pl.ds(c * e, e)]))
            row += T
    for at, (r, c) in enumerate(upper(2 * tiles)):
        half = outer0.shape[0]
        ref, spot = (outer0, at * T) if at * T < half else (outer1, at * T - half)
        source = leaf_block(leaf, ext[r // tiles], ext[c // tiles], r % tiles, c % tiles, T)
        pairs.append((source, ref.at[pl.ds(spot, T)]))
    run_copies(pairs, sem)


def cut_outer(place, leaf, chunks):
    e = leaf.shape[1] // 4
    n_outer = len(upper(2 * (e // T)))
    return pl.pallas_call(
        cut_outer_kernel,
        out_shape=[jax.ShapeDtypeStruct((rows, 2 * e), F32) for rows in chunks]
        + [jax.ShapeDtypeStruct((n_outer // 2 * T, T), F32)] * 2,
        in_specs=[SMEM, HBM],
        out_specs=[VMEM] * (len(chunks) + 2),
        scratch_shapes=[pltpu.SemaphoreType.DMA((n_outer + 4 * e // T,))],
        compiler_params=PARAMS,
        name="cut_outer",
    )(place, leaf)


def unpack(ref, at, tiles):
    held = {}
    for r, c in upper(tiles):
        held[r, c] = ref[pl.ds(at, T), :]
        if c > r:
            held[c, r] = held[r, c].T
        at += T
    return jnp.concatenate(
        [jnp.concatenate([held[r, c] for c in range(tiles)], axis=1) for r in range(tiles)], axis=0
    )


def unpack_full(ref, at, tiles):
    rows = []
    for r in range(tiles):
        rows.append(
            jnp.concatenate([ref[pl.ds(at + (r * tiles + c) * T, T), :] for c in range(tiles)], axis=1)
        )
    return jnp.concatenate(rows, axis=0)


def pack(ref, value, tiles):
    for at, (r, c) in enumerate(upper(tiles)):
        ref[at * T : (at + 1) * T, :] = value[r * T : (r + 1) * T, c * T : (c + 1) * T]


def invert_side_kernel(mine, along, whole, packed, held):
    tiles = whole.shape[0] // T
    held[...] = unpack(mine, 0, tiles) + unpack(along, 0, tiles)
    invert_in_place([held])
    whole[...] = held[...]
    pack(packed, held[...], tiles)


def invert_side(mine, along, e):
    return pl.pallas_call(
        invert_side_kernel,
        out_shape=[jax.ShapeDtypeStruct((e, e), F32), jax.ShapeDtypeStruct(mine.shape, F32)],
        in_specs=[VMEM, VMEM],
        out_specs=[VMEM, VMEM],
        scratch_shapes=[pltpu.VMEM((e, e), F32)],
        compiler_params=PARAMS,
        cost_estimate=pl.CostEstimate(flops=10**10, bytes_accessed=10**6, transcendentals=0),
        name="invert_side",
    )(mine, along)


def factor_start_kernel(h0, h1_tiles, mine, across, along, corner, side, cols, h1, coup):
    e = h0.shape[0]
    tiles = e // T
    sym = len(upper(tiles)) * T
    h1[...] = unpack(h1_tiles, 0, tiles)
    coup[:e, :e] = unpack_full(mine, sym, tiles)
    coup[:e, e:] = unpack_full(across, sym, tiles)
    coup[e:, :e] = unpack_full(along, sym, tiles)
    coup[e:, e:] = unpack_full(corner, sym, tiles)
    cols[:, :e] = dot(coup[:, :e], h0[...])
    cols[:, e:] = dot(coup[:, e:], h1[...])
    side[...] = -dot(cols[...], coup[...], NT)
    side[:e, :e] = side[:e, :e] + (unpack(mine, 0, tiles) + unpack(across, 0, tiles))
    side[e:, e:] = side[e:, e:] + (unpack(along, 0, tiles) + unpack(corner, 0, tiles))
    invert_in_place([side], 0, e)


def factor_start(h0, h1_tiles, mine, across, along, corner):
    e = h0.shape[0]
    return pl.pallas_call(
        factor_start_kernel,
        out_shape=[
            jax.ShapeDtypeStruct((2 * e, 2 * e), F32),
            jax.ShapeDtypeStruct((2 * e, 2 * e), F32),
            jax.ShapeDtypeStruct((e, e), F32),
        ],
        in_specs=[VMEM] * 6,
        out_specs=[VMEM] * 3,
        scratch_shapes=[pltpu.VMEM((2 * e, 2 * e), F32)],
        compiler_params=PARAMS,
        cost_estimate=pl.CostEstimate(flops=12 * 10**9, bytes_accessed=5 * 10**6, transcendentals=0),
        name="factor_start",
    )(h0, h1_tiles, mine, across, along, corner)


def factor_end_kernel(place, side_in, cols, h0, h1, high, low, side, full):
    e = h0.shape[0]
    side[...] = side_in[...]
    invert_in_place([side], e, 2 * e)
    flow16 = split(cols[...])
    away = dot3(split(side[...]), flow16)
    full[...] = dot3(flow16, split(away), TN)
    full[:e, :e] = full[:e, :e] + h0[...]
    full[e:, e:] = full[e:, e:] + h1[...]

    def emit(value, rows, columns):
        high[rows, columns], low[rows, columns] = split(value)

    first, rest = slice(0, e), slice(e, 3 * e)
    emit(full[...], rest, rest)
    emit(-away[:e, :], first, rest)
    same = place[0] == place[1]

    @pl.when(same)
    def _():
        emit(side[:e, :e], first, first)
        emit(-away[:e, :].T, rest, first)

    @pl.when(jnp.logical_not(same))
    def _():
        emit(side[:e, e:], first, first)
        emit(-away[e:, :].T, rest, first)


def factor_end(place, side, cols, h0, h1):
    e = h0.shape[0]
    return pl.pallas_call(
        factor_end_kernel,
        out_shape=[jax.ShapeDtypeStruct((3 * e, 3 * e), BF16)] * 2,
        in_specs=[SMEM] + [VMEM] * 4,
        out_specs=[VMEM, VMEM],
        scratch_shapes=[pltpu.VMEM((2 * e, 2 * e), F32), pltpu.VMEM((2 * e, 2 * e), F32)],
        compiler_params=PARAMS,
        cost_estimate=pl.CostEstimate(flops=12 * 10**9, bytes_accessed=5 * 10**6, transcendentals=0),
        name="factor_end",
    )(place, side, cols, h0, h1)


def join(refs):
    return jnp.concatenate([ref[...] for ref in refs], axis=0)


def rows_kernel(high, low, *refs):
    *leaves, top, bottom = refs
    n = len(leaves) // 2
    e = leaves[0].shape[1] // 2
    whole = (high[...], low[...])
    for at, leaf in enumerate((join(leaves[:n]), join(leaves[n:]))):
        first = split(leaf[:, :e])
        second = split(leaf[:, e:])
        inner = slice((1 + at) * e, (2 + at) * e)
        value = dot3(first, (whole[0][:e], whole[1][:e])) + dot3(
            second, (whole[0][inner], whole[1][inner])
        )
        rows = slice(2 * e * at, 2 * e * (at + 1))
        top[rows, :], bottom[rows, :] = split(value)


def row_products(high, low, mine, across):
    e = mine[0].shape[1] // 2
    return pl.pallas_call(
        rows_kernel,
        out_shape=[jax.ShapeDtypeStruct((4 * e, 3 * e), BF16)] * 2,
        in_specs=[VMEM] * (2 + 2 * len(mine)),
        out_specs=[VMEM] * 2,
        compiler_params=PARAMS,
        cost_estimate=pl.CostEstimate(flops=3 * 10**9, bytes_accessed=7 * 10**6, transcendentals=0),
        name="row_products",
    )(high, low, *mine, *across)


def result_kernel(n, place, leaf, top, bottom, outer0, outer1, *refs):
    mine, across, along, corner = (refs[i * n : (i + 1) * n] for i in range(4))
    out, own, col, sem = refs[4 * n :]
    e = mine[0].shape[1] // 2
    tiles = e // T
    v, u = place[0], place[1]
    same = u == v
    ext = [v, 2 + u]
    copies = []
    for r in range(2):
        for c in range(2):
            copies.append(
                pltpu.make_async_copy(
                    leaf_block(leaf, ext[r], ext[c], 0, 0, e),
                    own.at[pl.ds(r * e, e), pl.ds(c * e, e)],
                    sem.at[2 * r + c],
                )
            )
            copies[-1].start()

    @pl.when(same)
    def _():
        col[0] = join(mine)
        col[1] = join(across)

    @pl.when(jnp.logical_not(same))
    def _():
        col[0] = join(along)
        col[1] = join(corner)

    def spot(side, which):
        return pl.ds(pl.multiple_of((2 * side + (v if which == 0 else 1 - v)) * e, T), e)

    for b in range(2):
        right = split(col[b])
        for a in range(2):
            rows = slice(2 * e * a, 2 * e * (a + 1))
            inner = slice((1 + b) * e, (2 + b) * e)
            left = [
                jnp.concatenate([ref[rows, :e], ref[rows, inner]], axis=1) for ref in (top, bottom)
            ]
            value = -dot3(left, right, NT)
            for r in range(2):
                for c in range(2):
                    out[0, spot(r, a), spot(c, b)] = value[r * e : (r + 1) * e, c * e : (c + 1) * e]
    for copy in copies:
        copy.wait()

    @pl.when(same)
    def _():
        held = {}
        for at, (i, j) in enumerate(upper(2 * tiles)):
            ref = outer0 if at < outer0.shape[0] // T else outer1
            at -= 0 if ref is outer0 else outer0.shape[0] // T
            held[i, j] = ref[at * T : (at + 1) * T, :]
            held[j, i] = held[i, j] if i == j else held[i, j].T
        for r in range(2):
            for c in range(2):
                out[0, spot(r, 0), spot(c, 0)] = (
                    out[0, spot(r, 0), spot(c, 0)] + own[r * e : (r + 1) * e, c * e : (c + 1) * e]
                )
                block = jnp.concatenate(
                    [
                        jnp.concatenate(
                            [held[r * tiles + i, c * tiles + j] for j in range(tiles)], axis=1
                        )
                        for i in range(tiles)
                    ],
                    axis=0,
                )
                out[0, spot(r, 1), spot(c, 1)] = out[0, spot(r, 1), spot(c, 1)] + block


def result(place, leaf, top, bottom, outer0, outer1, mine, across, along, corner):
    e = leaf.shape[1] // 4
    n = len(mine)
    return pl.pallas_call(
        functools.partial(result_kernel, n),
        out_shape=jax.ShapeDtypeStruct((1, 4 * e, 4 * e), F32),
        in_specs=[SMEM, HBM] + [VMEM] * (4 + 4 * n),
        out_specs=VMEM,
        scratch_shapes=[
            pltpu.VMEM((2 * e, 2 * e), F32),
            pltpu.VMEM((2, 2 * e, 2 * e), F32),
            pltpu.SemaphoreType.DMA((4,)),
        ],
        compiler_params=PARAMS,
        cost_estimate=pl.CostEstimate(flops=4 * 10**9, bytes_accessed=12 * 10**6, transcendentals=0),
        name="result",
    )(place, leaf, top, bottom, outer0, outer1, *mine, *across, *along, *corner)


def tie(*values):
    return lax.optimization_barrier(values)


def solution(mesh):
    nx, ny = mesh.shape["gx"], mesh.shape["gy"]
    devices = [(x, y) for x in range(nx) for y in range(ny)]

    def is_same(x, y):
        return x // (nx // 2) == y // (ny // 2)

    def send(value, along_y, only=None):
        pairs = []
        for x, y in devices:
            if only is None or is_same(x, y) == only:
                to = (x, (y + ny // 2) % ny) if along_y else ((x + nx // 2) % nx, y)
                pairs.append((x * ny + y, to[0] * ny + to[1]))
        return lax.ppermute(value, ("gx", "gy"), pairs)

    def body(leaf):
        e = leaf.shape[1] // 4
        v = lax.axis_index("gx") // (nx // 2)
        u = lax.axis_index("gy") // (ny // 2)
        place = jnp.stack([v, u]).astype(jnp.int32)
        hh, sr = cut_inner(place, leaf)
        hh_y = send(hh, True)
        sr_x = send(sr, False)
        sr_y = send(sr, True)
        ca, cb, cc, outer0, outer1 = cut_outer(place, leaf, (e // 2, e // 2, e))
        passed = send(outer1, True, only=False)
        ca_x = send(ca, False)
        ca_y = send(ca, True, only=True)
        h0, h0_tiles = invert_side(hh, hh_y, e)
        h1_tiles = send(h0_tiles, False)
        sr_d = send(sr_x, True)
        cb, cc, sr_d, h1_tiles, ca_x = tie(cb, cc, sr_d, h1_tiles, ca_x)
        cb_x = send(cb, False)
        ca_d = send(ca_x, True, only=True)
        cb_y = send(cb, True, only=True)
        side, cols, h1 = factor_start(h0, h1_tiles, sr, sr_x, sr_y, sr_d)
        cc, cb_x, side, passed = tie(cc, cb_x, side, passed)
        cb_d = send(cb_x, True, only=True)
        outer0 = send(jnp.where(u == v, passed, outer0), False)
        cc_x = send(cc, False)
        cc_y = send(cc, True, only=True)
        high, low = factor_end(place, side, cols, h0, h1)
        cc_x, outer0, high = tie(cc_x, outer0, high)
        cc_d = send(cc_x, True, only=True)
        outer1 = send(outer0, True, only=False)
        mine, across = (ca, cb, cc), (ca_x, cb_x, cc_x)
        along, corner = (ca_y, cb_y, cc_y), (ca_d, cb_d, cc_d)
        top, bottom = row_products(high, low, mine, across)
        return result(place, leaf, top, bottom, outer0, outer1, mine, across, along, corner)

    return jax.shard_map(
        body,
        mesh=mesh,
        in_specs=(P(None, "gy", "gx"),),
        out_specs=P(None, "gy", "gx"),
        check_vma=False,
    )
```

```python
import functools

import jax
import jax.numpy as jnp
from jax import lax
from jax.experimental import pallas as pl
from jax.experimental.pallas import tpu as pltpu
from jax.sharding import PartitionSpec as P

F32 = jnp.float32
BF16 = jnp.bfloat16
T = 128
R = 16
HBM = pl.BlockSpec(memory_space=pl.ANY)
VMEM = pl.BlockSpec(memory_space=pltpu.VMEM)
SMEM = pl.BlockSpec(memory_space=pltpu.SMEM)
PARAMS = pltpu.CompilerParams(vmem_limit_bytes=32 * 2**20)


def dot(a, b, dims=((1,), (0,))):
    return lax.dot_general(
        a, b, (dims, ((), ())), precision=lax.Precision.HIGHEST, preferred_element_type=F32
    )


def dot16(a, b, dims=((1,), (0,))):
    return lax.dot_general(a, b, (dims, ((), ())), preferred_element_type=F32)


def split(a):
    high = a.astype(BF16)
    return high, (a - high.astype(F32)).astype(BF16)


def dot3(a, b, dims=((1,), (0,))):
    return dot16(a[0], b[0], dims) + (dot16(a[0], b[1], dims) + dot16(a[1], b[0], dims))


NT = ((1,), (1,))
TN = ((0,), (0,))


def upper(n):
    return [(i, j) for i in range(n) for j in range(i, n)]


def across_lanes(x, k):
    return jnp.broadcast_to(x[:, k : k + 1], x.shape)


def across_rows(x, k):
    return jnp.broadcast_to(x[k : k + 1, :], x.shape)


def panel(rows, c0, lower):
    sub = lax.broadcasted_iota(jnp.int32, rows.shape, 0)
    lane = lax.broadcasted_iota(jnp.int32, rows.shape, 1)
    cols = [across_lanes(rows, c0 + k) for k in range(R)]
    out = jnp.where((lane >= c0) & (lane < c0 + R), (lane - c0 == sub).astype(F32), rows)
    half = out
    scale = jnp.ones_like(rows)
    for k in range(R):
        pivot = across_rows(cols[k], k)
        inv = 1.0 / pivot
        here = sub == k
        mult = cols[k]

        def step(x):
            row = across_rows(x, k) * inv
            return jnp.where(here, row, x - mult * row)

        if lower:
            scale = jnp.where(here, pivot, scale)
            half = half - jnp.where(sub > k, mult, 0.0) * (across_rows(half, k) * inv)
        out = step(out)
        for j in range(k + 1, R):
            cols[j] = step(cols[j])
    return out, half * lax.rsqrt(scale) if lower else None


def put_rows(matrix, rows, r0):
    parts = [matrix[:r0]] if r0 else []
    parts.append(rows)
    if r0 + rows.shape[0] < matrix.shape[0]:
        parts.append(matrix[r0 + rows.shape[0] :])
    return jnp.concatenate(parts, axis=0)


def invert_tile(m, lower=False):
    lane = lax.broadcasted_iota(jnp.int32, (T, T), 1)
    sub = lax.broadcasted_iota(jnp.int32, (T, T), 0)
    rows = m[:R]
    for c0 in range(0, T, R):
        swept, half = panel(rows, c0, lower)
        if c0 + R < T:
            old = m[c0 + R : c0 + 2 * R]
            inside = (lane[:R] >= c0) & (lane[:R] < c0 + R)
            rows = jnp.where(inside, 0.0, old)
            for k in range(R):
                rows = rows - across_lanes(old, c0 + k) * across_rows(swept, k)
        wide = put_rows(jnp.zeros((T, T), F32), swept, c0)
        rest = jnp.where((lane >= c0) & (lane < c0 + R), 0.0, m) - dot(m, wide)
        if lower:
            rest = jnp.where(sub < c0, m, rest)
        m = put_rows(rest, half if lower else swept, c0)
    return jnp.where(lane > sub, 0.0, m) if lower else m


def sweep(ref, start, stop):
    n = ref.shape[0]
    for p in range(start, stop, T):
        pivot = invert_tile(ref[p : p + T, p : p + T])
        rows = dot(pivot, ref[p : p + T, :])
        parts = ([rows[:, :p]] if p else []) + [pivot]
        if p + T < n:
            parts.append(rows[:, p + T :])
        rows = jnp.concatenate(parts, axis=1)
        for q in range(0, n, T):
            if q != p:
                change = dot(ref[q : q + T, p : p + T], rows)
                ref[q : q + T, p : p + T] = jnp.zeros((T, T), F32)
                ref[q : q + T, :] = ref[q : q + T, :] - change
        ref[p : p + T, :] = rows


def inverse_factor(ref):
    n = ref.shape[0]
    for p in range(0, n, T):
        pivot = invert_tile(ref[p : p + T, p : p + T], lower=True)
        scaled = dot(pivot, ref[p : p + T, :])
        for q in range(p + T, n, T):
            weight = scaled[:, q : q + T]
            ref[q : q + T, :] = ref[q : q + T, :] - dot(weight, scaled, TN)
            ref[q : q + T, p : p + T] = -dot(weight, pivot, TN)
        for q in range(0, n, T):
            if q < p:
                ref[p : p + T, q : q + T] = scaled[:, q : q + T]
            else:
                ref[p : p + T, q : q + T] = pivot if q == p else jnp.zeros((T, T), F32)


def leaf_block(leaf, side_r, side_c, r, c, size):
    e = leaf.shape[1] // 4
    return leaf.at[
        0,
        pl.ds(pl.multiple_of(side_r * e + r * size, T), size),
        pl.ds(pl.multiple_of(side_c * e + c * size, T), size),
    ]


def run_copies(pairs, sem):
    copies = [pltpu.make_async_copy(a, b, sem.at[i]) for i, (a, b) in enumerate(pairs)]
    for copy in copies:
        copy.start()
    for copy in copies:
        copy.wait()


def sides(place):
    v, u = place[0], place[1]
    return [v, 2 + u], [1 - v, 3 - u]


def unpack(ref, at, tiles):
    held = {}
    for r, c in upper(tiles):
        held[r, c] = ref[at : at + T, :]
        if c > r:
            held[c, r] = held[r, c].T
        at += T
    return jnp.concatenate(
        [jnp.concatenate([held[r, c] for c in range(tiles)], axis=1) for r in range(tiles)], axis=0
    )


def unpack_full(ref, at, tiles):
    rows = []
    for r in range(tiles):
        spots = [at + (r * tiles + c) * T for c in range(tiles)]
        rows.append(jnp.concatenate([ref[x : x + T, :] for x in spots], axis=1))
    return jnp.concatenate(rows, axis=0)


def call(kernel, name, outs, ins, scratch, flops, **more):
    return pl.pallas_call(
        kernel,
        out_shape=[jax.ShapeDtypeStruct(shape, dtype) for shape, dtype in outs],
        in_specs=[spec for spec, _ in ins],
        out_specs=more.pop("out_specs", [VMEM] * len(outs)),
        scratch_shapes=scratch,
        compiler_params=PARAMS,
        cost_estimate=pl.CostEstimate(flops=flops, bytes_accessed=10**6, transcendentals=0),
        name=name,
        **more,
    )(*[value for _, value in ins])


def cut_first_kernel(place, leaf, hh, a, sem):
    tiles = leaf.shape[1] // 4 // T
    ext, inn = sides(place)
    n_sym = len(upper(tiles))
    pairs = []
    for at, (r, c) in enumerate(upper(tiles)):
        pairs.append((leaf_block(leaf, inn[1], inn[1], r, c, T), hh.at[pl.ds(at * T, T)]))
        pairs.append((leaf_block(leaf, inn[0], inn[0], r, c, T), a.at[pl.ds(at * T, T)]))
    for at in range(tiles * tiles):
        source = leaf_block(leaf, ext[0], inn[0], at // tiles, at % tiles, T)
        pairs.append((source, a.at[pl.ds((n_sym + at) * T, T)]))
    run_copies(pairs, sem)


def cut_first(place, leaf):
    tiles = leaf.shape[1] // 4 // T
    n_sym, n_full = len(upper(tiles)), tiles * tiles
    return call(
        cut_first_kernel,
        "cut_first",
        [((n_sym * T, T), F32), (((n_sym + n_full) * T, T), F32)],
        [(SMEM, place), (HBM, leaf)],
        [pltpu.SemaphoreType.DMA((2 * n_sym + n_full,))],
        10**8,
    )


def cut_second_kernel(place, leaf, b, c1, c2, outer0, outer1, sem):
    e = leaf.shape[1] // 4
    tiles = e // T
    ext, inn = sides(place)
    pairs = [
        (leaf_block(leaf, inn[0], inn[1], 0, 0, e), b),
        (leaf_block(leaf, ext[1], inn[0], 0, 0, e), c1.at[pl.ds(0, e)]),
        (leaf_block(leaf, ext[0], inn[1], 0, 0, e), c1.at[pl.ds(e, e)]),
        (leaf_block(leaf, ext[1], inn[1], 0, 0, e), c2),
    ]
    half = outer0.shape[0]
    for at, (r, c) in enumerate(upper(2 * tiles)):
        ref, spot = (outer0, at * T) if at * T < half else (outer1, at * T - half)
        source = leaf_block(leaf, ext[r // tiles], ext[c // tiles], r % tiles, c % tiles, T)
        pairs.append((source, ref.at[pl.ds(spot, T)]))
    run_copies(pairs, sem)


def cut_second(place, leaf):
    e = leaf.shape[1] // 4
    n_outer = len(upper(2 * (e // T)))
    return call(
        cut_second_kernel,
        "cut_second",
        [((e, e), F32), ((2 * e, e), F32), ((e, e), F32)] + [((n_outer // 2 * T, T), F32)] * 2,
        [(SMEM, place), (HBM, leaf)],
        [pltpu.SemaphoreType.DMA((n_outer + 4,))],
        10**8,
    )


def gauge_kernel(place, mine, along, b, c1, c2, outer1, b_out, c1_out, c2_out, swap, held):
    e = held.shape[0]
    held[...] = unpack(mine, 0, e // T) + unpack(along, 0, e // T)
    inverse_factor(held)
    b_out[...] = dot(b[...], held[...], NT)
    factor = split(held[...])
    c1_out[:e, :] = c1[:e, :]
    c1_out[e:, :] = dot3(split(c1[e:, :]), factor, NT)
    c2_out[...] = dot3(split(c2[...]), factor, NT)
    same = place[0] == place[1]

    @pl.when(same)
    def _():
        swap[: 2 * e, :] = c1_out[...]
        swap[2 * e :, :] = c2_out[...]

    @pl.when(jnp.logical_not(same))
    def _():
        swap[: outer1.shape[0], :T] = outer1[...]


def gauge(place, mine, along, b, c1, c2, outer1):
    e = b.shape[0]
    return call(
        gauge_kernel,
        "gauge_side",
        [((e, e), F32), ((2 * e, e), F32), ((e, e), F32), ((3 * e, e), F32)],
        [(SMEM, place)] + [(VMEM, x) for x in (mine, along, b, c1, c2, outer1)],
        [pltpu.VMEM((e, e), F32)],
        5 * 10**9,
    )


def couple(b):
    mine, across, along, corner = (ref[...] for ref in b)
    return jnp.concatenate(
        [jnp.concatenate([mine, across], axis=1), jnp.concatenate([along, corner], axis=1)], axis=0
    )


def factor_start_kernel(a0, a1, a2, a3, b0, b1, b2, b3, side):
    e = b0.shape[0]
    tiles = e // T
    coup = couple((b0, b1, b2, b3))
    side[...] = -dot(coup, coup, NT)
    side[:e, :e] = side[:e, :e] + (unpack(a0, 0, tiles) + unpack(a1, 0, tiles))
    side[e:, e:] = side[e:, e:] + (unpack(a2, 0, tiles) + unpack(a3, 0, tiles))
    sweep(side, 0, e)


def factor_start(a, b):
    e = b[0].shape[0]
    return call(
        factor_start_kernel,
        "factor_start",
        [((2 * e, 2 * e), F32)],
        [(VMEM, x) for x in (*a, *b)],
        [],
        8 * 10**9,
    )[0]


def factor_end_kernel(place, side_in, b0, b1, b2, b3, high, low, side, full):
    e = b0.shape[0]
    side[...] = side_in[...]
    sweep(side, e, 2 * e)
    coup = split(couple((b0, b1, b2, b3)))
    away = dot3(split(side[...]), coup)
    shape = full.shape
    unit = lax.broadcasted_iota(jnp.int32, shape, 0) == lax.broadcasted_iota(jnp.int32, shape, 1)
    full[...] = dot3(coup, split(away), TN) + unit.astype(F32)

    def emit(value, rows, columns):
        high[rows, columns], low[rows, columns] = split(value)

    first, rest = slice(0, e), slice(e, 3 * e)
    emit(full[...], rest, rest)
    emit(-away[:e, :], first, rest)
    same = place[0] == place[1]

    @pl.when(same)
    def _():
        emit(side[:e, :e], first, first)
        emit(-away[:e, :].T, rest, first)

    @pl.when(jnp.logical_not(same))
    def _():
        emit(side[:e, e:], first, first)
        emit(-away[e:, :].T, rest, first)


def factor_end(place, side, b):
    e = b[0].shape[0]
    return call(
        factor_end_kernel,
        "factor_end",
        [((3 * e, 3 * e), BF16)] * 2,
        [(SMEM, place), (VMEM, side)] + [(VMEM, x) for x in b],
        [pltpu.VMEM((2 * e, 2 * e), F32), pltpu.VMEM((2 * e, 2 * e), F32)],
        8 * 10**9,
    )


def cross_block(a, c):
    e = c[0].shape[1]
    n_sym = len(upper(e // T)) * T
    c = jnp.concatenate([ref[...] for ref in c], axis=0)
    return jnp.concatenate(
        [
            jnp.concatenate([unpack_full(a, n_sym, e // T), c[e : 2 * e]], axis=1),
            jnp.concatenate([c[:e], c[2 * e :]], axis=1),
        ],
        axis=0,
    )


def times_inverse(cross, high, low, inner):
    e = cross.shape[1] // 2
    return dot3(split(cross[:, :e]), (high[:e], low[:e])) + dot3(
        split(cross[:, e:]), (high[inner], low[inner])
    )


def rows_kernel(place, leaf, high, low, a0, c01, c02, a2, swapped, top, bottom, block, col, own, sem):
    e = c02.shape[0]
    ext, _ = sides(place)
    copies = []
    for r in range(2):
        for c in range(2):
            target = own.at[pl.ds(r * e, e), pl.ds(c * e, e)]
            source = leaf_block(leaf, ext[r], ext[c], 0, 0, e)
            copies.append(pltpu.make_async_copy(source, target, sem.at[2 * r + c]))
            copies[-1].start()
    same = place[0] == place[1]
    mine = cross_block(a0, (c01, c02))

    @pl.when(same)
    def _():
        col[...] = mine

    @pl.when(jnp.logical_not(same))
    def _():
        col[...] = cross_block(a2, (swapped,))

    left = split(times_inverse(mine, high[...], low[...], slice(e, 2 * e)))
    top[...], bottom[...] = left
    left = [x[:, : 2 * e] for x in left]
    block[...] = -dot3(left, split(col[...]), NT)
    for copy in copies:
        copy.wait()

    @pl.when(same)
    def _():
        block[...] = block[...] + own[...]


def own_rows(place, leaf, high, low, a0, c0, a2, swapped):
    e = leaf.shape[1] // 4
    return call(
        rows_kernel,
        "own_rows",
        [((2 * e, 3 * e), BF16)] * 2 + [((2 * e, 2 * e), F32)],
        [(SMEM, place), (HBM, leaf)] + [(VMEM, x) for x in (high, low, a0, *c0, a2, swapped)],
        [
            pltpu.VMEM((2 * e, 2 * e), F32),
            pltpu.VMEM((2 * e, 2 * e), F32),
            pltpu.SemaphoreType.DMA((4,)),
        ],
        3 * 10**9,
    )


def spot(place, e, side, which):
    x = place[0] if which == 0 else 1 - place[0]
    return pl.ds(pl.multiple_of((2 * side + x) * e, T), e)


def products_kernel(
    place, high, low, top, bottom, block, a0, c01, c02, a1, c11, c12, a2, swapped, a3, c31, c32, out, col
):
    e = c02.shape[0]
    same = place[0] == place[1]
    across = cross_block(a1, (c11, c12))

    @pl.when(same)
    def _():
        col[0] = cross_block(a0, (c01, c02))
        col[1] = across

    @pl.when(jnp.logical_not(same))
    def _():
        col[0] = cross_block(a2, (swapped,))
        col[1] = cross_block(a3, (c31, c32))

    def write(value, a, b):
        for r in range(2):
            for c in range(2):
                out[0, spot(place, e, r, a), spot(place, e, c, b)] = value[
                    r * e : (r + 1) * e, c * e : (c + 1) * e
                ]

    write(block[...], 0, 0)
    rows = [
        (top[...], bottom[...]),
        split(times_inverse(across, high[...], low[...], slice(2 * e, 3 * e))),
    ]
    for a, b in ((1, 0), (0, 1), (1, 1)):
        inner = slice((1 + b) * e, (2 + b) * e)
        left = [jnp.concatenate([x[:, :e], x[:, inner]], axis=1) for x in rows[a]]
        write(-dot3(left, split(col[b]), NT), a, b)


def products(place, high, low, top, bottom, block, a, c0, c1, swapped, c3):
    e = swapped.shape[1]
    return call(
        products_kernel,
        "products",
        [((1, 4 * e, 4 * e), F32)],
        [(SMEM, place)]
        + [(VMEM, x) for x in (high, low, top, bottom, block)]
        + [(VMEM, x) for x in (a[0], *c0, a[1], *c1, a[2], swapped, a[3], *c3)],
        [pltpu.VMEM((2, 2 * e, 2 * e), F32)],
        4 * 10**9,
    )[0]


def add_outer_kernel(place, before, outer0, outer1, out, held, sem):
    e = out.shape[1] // 4
    tiles = e // T
    spots = [
        (
            out.at[0, spot(place, e, r, 1), spot(place, e, c, 1)],
            held.at[pl.ds(r * e, e), pl.ds(c * e, e)],
        )
        for r in range(2)
        for c in range(2)
    ]

    @pl.when(place[0] == place[1])
    def _():
        run_copies(spots, sem)
        half = outer0.shape[0]
        for at, (i, j) in enumerate(upper(2 * tiles)):
            ref, at = (outer0, at * T) if at * T < half else (outer1, at * T - half)
            piece = ref[at : at + T, :]
            r, c = slice(i * T, (i + 1) * T), slice(j * T, (j + 1) * T)
            held[r, c] = held[r, c] + piece
            if i != j:
                held[c, r] = held[c, r] + piece.T
        run_copies([(b, a) for a, b in spots], sem)


def add_outer(place, before, outer0, outer1):
    e = before.shape[1] // 4
    return call(
        add_outer_kernel,
        "add_outer",
        [(before.shape, F32)],
        [(SMEM, place), (HBM, before), (VMEM, outer0), (VMEM, outer1)],
        [pltpu.VMEM((2 * e, 2 * e), F32), pltpu.SemaphoreType.DMA((4,))],
        10**8,
        out_specs=[HBM],
        input_output_aliases={1: 0},
    )[0]


def tie(*values):
    return lax.optimization_barrier(values)


def solution(mesh):
    nx, ny = mesh.shape["gx"], mesh.shape["gy"]
    devices = [(x, y) for x in range(nx) for y in range(ny)]

    def is_same(x, y):
        return x // (nx // 2) == y // (ny // 2)

    def send(value, along_y, only=None):
        pairs = []
        for x, y in devices:
            if only is None or is_same(x, y) == only:
                to = (x, (y + ny // 2) % ny) if along_y else ((x + nx // 2) % nx, y)
                pairs.append((x * ny + y, to[0] * ny + to[1]))
        return lax.ppermute(value, ("gx", "gy"), pairs)

    def body(leaf):
        e = leaf.shape[1] // 4
        v = lax.axis_index("gx") // (nx // 2)
        u = lax.axis_index("gy") // (ny // 2)
        place = jnp.stack([v, u]).astype(jnp.int32)
        hh, a = cut_first(place, leaf)
        hh_y = send(hh, True)
        a_x = send(a, False)
        a_y = send(a, True)
        b, c1, c2, outer0, outer1 = cut_second(place, leaf)
        b, c1, c2, swap = gauge(place, hh, hh_y, b, c1, c2, outer1)
        b_x = send(b, False)
        b_y = send(b, True)
        a_x, b = tie(a_x, b)
        a_d = send(a_x, True)
        b_d = send(b_x, True)
        c1, swap, b_x = tie(c1, swap, b_x)
        c1_x = send(c1, False)
        swapped = send(swap, True)
        side = factor_start((a, a_x, a_y, a_d), (b, b_x, b_y, b_d))
        c2, c1_x, side = tie(c2, c1_x, side)
        c2_x = send(c2, False)
        c1_d = send(c1_x, True, only=True)
        high, low = factor_end(place, side, (b, b_x, b_y, b_d))
        passed = swapped[: outer0.shape[0], :T]
        outer0, high = tie(jnp.where(u == v, passed, outer0), high)
        outer0 = send(outer0, False)
        c2_d = send(c2_x, True, only=True)
        top, bottom, block = own_rows(place, leaf, high, low, a, (c1, c2), a_y, swapped)
        outer1 = send(outer0, True, only=False)
        out = products(
            place, high, low, top, bottom, block, (a, a_x, a_y, a_d), (c1, c2), (c1_x, c2_x), swapped, (c1_d, c2_d)
        )
        return add_outer(place, out, outer0, outer1)

    return jax.shard_map(
        body,
        mesh=mesh,
        in_specs=(P(None, "gy", "gx"),),
        out_specs=P(None, "gy", "gx"),
        check_vma=False,
    )
```

```python
import math

import jax
import jax.numpy as jnp
from jax import lax
from jax.experimental import pallas as pl
from jax.experimental.pallas import tpu as pltpu
from jax.sharding import PartitionSpec as P

F32 = jnp.float32
BF16 = jnp.bfloat16
T = 128
R = 16
COST = 1000
HBM = pl.BlockSpec(memory_space=pl.ANY)
VMEM = pl.BlockSpec(memory_space=pltpu.VMEM)
SMEM = pl.BlockSpec(memory_space=pltpu.SMEM)
PARAMS = pltpu.CompilerParams(vmem_limit_bytes=32 * 2**20)


def dot(a, b, dims=((1,), (0,))):
    return lax.dot_general(
        a, b, (dims, ((), ())), precision=lax.Precision.HIGHEST, preferred_element_type=F32
    )


def dot16(a, b, dims=((1,), (0,))):
    return lax.dot_general(a, b, (dims, ((), ())), preferred_element_type=F32)


def split(a):
    high = a.astype(BF16)
    return high, (a - high.astype(F32)).astype(BF16)


def dot3(a, b, dims=((1,), (0,))):
    return dot16(a[0], b[0], dims) + (dot16(a[0], b[1], dims) + dot16(a[1], b[0], dims))


NT = ((1,), (1,))
TN = ((0,), (0,))


def upper(n):
    return [(i, j) for i in range(n) for j in range(i, n)]


def across_lanes(x, k):
    return jnp.broadcast_to(x[:, k : k + 1], x.shape)


def across_rows(x, k):
    return jnp.broadcast_to(x[k : k + 1, :], x.shape)


def panel(rows, c0, lower):
    sub = lax.broadcasted_iota(jnp.int32, rows.shape, 0)
    lane = lax.broadcasted_iota(jnp.int32, rows.shape, 1)
    cols = [across_lanes(rows, c0 + k) for k in range(R)]
    out = jnp.where((lane >= c0) & (lane < c0 + R), (lane - c0 == sub).astype(F32), rows)
    half = out
    scale = jnp.ones_like(rows)
    for k in range(R):
        pivot = across_rows(cols[k], k)
        inv = 1.0 / pivot
        here = sub == k
        mult = cols[k]

        def step(x):
            row = across_rows(x, k) * inv
            return jnp.where(here, row, x - mult * row)

        if lower:
            scale = jnp.where(here, pivot, scale)
            half = half - jnp.where(sub > k, mult, 0.0) * (across_rows(half, k) * inv)
        out = step(out)
        for j in range(k + 1, R):
            cols[j] = step(cols[j])
    return out, half * lax.rsqrt(scale) if lower else None


def put_rows(matrix, rows, r0):
    parts = [matrix[:r0]] if r0 else []
    parts.append(rows)
    if r0 + rows.shape[0] < matrix.shape[0]:
        parts.append(matrix[r0 + rows.shape[0] :])
    return jnp.concatenate(parts, axis=0)


def invert_tile(m, lower=False):
    lane = lax.broadcasted_iota(jnp.int32, (T, T), 1)
    sub = lax.broadcasted_iota(jnp.int32, (T, T), 0)
    rows = m[:R]
    for c0 in range(0, T, R):
        swept, half = panel(rows, c0, lower)
        if c0 + R < T:
            old = m[c0 + R : c0 + 2 * R]
            inside = (lane[:R] >= c0) & (lane[:R] < c0 + R)
            rows = jnp.where(inside, 0.0, old)
            for k in range(R):
                rows = rows - across_lanes(old, c0 + k) * across_rows(swept, k)
        wide = put_rows(jnp.zeros((T, T), F32), swept, c0)
        rest = jnp.where((lane >= c0) & (lane < c0 + R), 0.0, m) - dot(m, wide)
        if lower:
            rest = jnp.where(sub < c0, m, rest)
        m = put_rows(rest, half if lower else swept, c0)
    return jnp.where(lane > sub, 0.0, m) if lower else m


def sweep(ref, start, stop):
    n = ref.shape[0]
    for p in range(start, stop, T):
        pivot = invert_tile(ref[p : p + T, p : p + T])
        rows = dot(pivot, ref[p : p + T, :])
        parts = ([rows[:, :p]] if p else []) + [pivot]
        if p + T < n:
            parts.append(rows[:, p + T :])
        rows = jnp.concatenate(parts, axis=1)
        for q in range(0, n, T):
            if q != p:
                change = dot(ref[q : q + T, p : p + T], rows)
                ref[q : q + T, p : p + T] = jnp.zeros((T, T), F32)
                ref[q : q + T, :] = ref[q : q + T, :] - change
        ref[p : p + T, :] = rows


def inverse_factor(ref):
    n = ref.shape[0]
    for p in range(0, n, T):
        pivot = invert_tile(ref[p : p + T, p : p + T], lower=True)
        scaled = dot(pivot, ref[p : p + T, :])
        for q in range(p + T, n, T):
            weight = scaled[:, q : q + T]
            ref[q : q + T, :] = ref[q : q + T, :] - dot(weight, scaled, TN)
            ref[q : q + T, p : p + T] = -dot(weight, pivot, TN)
        for q in range(0, n, T):
            if q < p:
                ref[p : p + T, q : q + T] = scaled[:, q : q + T]
            else:
                ref[p : p + T, q : q + T] = pivot if q == p else jnp.zeros((T, T), F32)


def leaf_block(leaf, side_r, side_c, r, c, size):
    e = leaf.shape[1] // 4
    return leaf.at[
        0,
        pl.ds(pl.multiple_of(side_r * e + r * size, T), size),
        pl.ds(pl.multiple_of(side_c * e + c * size, T), size),
    ]


def run_copies(pairs, sem):
    copies = [pltpu.make_async_copy(a, b, sem.at[i]) for i, (a, b) in enumerate(pairs)]
    for copy in copies:
        copy.start()
    for copy in copies:
        copy.wait()


def sides(place):
    v, u = place[0], place[1]
    return [v, 2 + u], [1 - v, 3 - u]


def unpack(ref, at, tiles):
    held = {}
    for r, c in upper(tiles):
        held[r, c] = ref[at : at + T, :]
        if c > r:
            held[c, r] = held[r, c].T
        at += T
    return jnp.concatenate(
        [jnp.concatenate([held[r, c] for c in range(tiles)], axis=1) for r in range(tiles)], axis=0
    )


def unpack_full(ref, at, tiles):
    rows = []
    for r in range(tiles):
        spots = [at + (r * tiles + c) * T for c in range(tiles)]
        rows.append(jnp.concatenate([ref[x : x + T, :] for x in spots], axis=1))
    return jnp.concatenate(rows, axis=0)


def call(kernel, name, outs, ins, scratch, **more):
    return pl.pallas_call(
        kernel,
        out_shape=[jax.ShapeDtypeStruct(shape, dtype) for shape, dtype in outs],
        in_specs=[spec for spec, _ in ins],
        out_specs=more.pop("out_specs", [VMEM] * len(outs)),
        scratch_shapes=scratch,
        compiler_params=PARAMS,
        cost_estimate=pl.CostEstimate(flops=COST, bytes_accessed=COST, transcendentals=0),
        name=name,
        **more,
    )(*[value for _, value in ins])


def block_tiles(leaf, side_r, side_c, at):
    tiles = leaf.shape[1] // 4 // T
    return leaf_block(leaf, side_r, side_c, at // tiles, at % tiles, T)


def cut_first_kernel(place, leaf, a, hs, sem):
    tiles = leaf.shape[1] // 4 // T
    ext, inn = sides(place)
    n_sym = len(upper(tiles))
    pairs = []
    for at, (r, c) in enumerate(upper(tiles)):
        source = leaf_block(leaf, inn[0], inn[0], r, c, T)
        pairs.append((source, a.at[pl.ds(at * T, T)]))
        pairs.append((source, hs.at[pl.ds((n_sym + at) * T, T)]))
        pairs.append((leaf_block(leaf, inn[1], inn[1], r, c, T), hs.at[pl.ds(at * T, T)]))
    for at in range(tiles * tiles):
        pairs.append(
            (block_tiles(leaf, ext[0], inn[0], at), a.at[pl.ds((n_sym + at) * T, T)])
        )
    run_copies(pairs, sem)


def cut_first(place, leaf):
    tiles = leaf.shape[1] // 4 // T
    n_sym, n_full = len(upper(tiles)), tiles * tiles
    return call(
        cut_first_kernel,
        "cut_first",
        [(((n_sym + n_full) * T, T), F32), ((2 * n_sym * T, T), F32)],
        [(SMEM, place), (HBM, leaf)],
        [pltpu.SemaphoreType.DMA((3 * n_sym + n_full,))],
    )


def cut_second_kernel(place, leaf, outer0, swap, b, c, sem):
    e = leaf.shape[1] // 4
    tiles = e // T
    ext, inn = sides(place)
    pairs = [
        (leaf_block(leaf, inn[0], inn[1], 0, 0, e), b),
        (leaf_block(leaf, ext[1], inn[0], 0, 0, e), c.at[pl.ds(0, e)]),
        (leaf_block(leaf, ext[0], inn[1], 0, 0, e), c.at[pl.ds(e, e)]),
        (leaf_block(leaf, ext[1], inn[1], 0, 0, e), c.at[pl.ds(2 * e, e)]),
    ]
    half = outer0.shape[0] // T
    second = []
    for at, (r, c) in enumerate(upper(2 * tiles)):
        source = leaf_block(leaf, ext[r // tiles], ext[c // tiles], r % tiles, c % tiles, T)
        if at < half:
            pairs.append((source, outer0.at[pl.ds(at * T, T)]))
        else:
            second.append((source, swap.at[pl.ds((at - half) * T, T)]))
    run_copies(pairs, sem)
    same = place[0] == place[1]

    @pl.when(same)
    def _():
        cross = [
            (block_tiles(leaf, ext[0], inn[0], at), swap.at[pl.ds(at * T, T)])
            for at in range(tiles * tiles)
        ]
        run_copies(cross, sem)

    @pl.when(jnp.logical_not(same))
    def _():
        run_copies(second, sem)


def cut_second(place, leaf):
    e = leaf.shape[1] // 4
    n_outer = len(upper(2 * (e // T)))
    return call(
        cut_second_kernel,
        "cut_second",
        [((n_outer // 2 * T, T), F32)] * 2 + [((e, e), F32), ((3 * e, e), F32)],
        [(SMEM, place), (HBM, leaf)],
        [pltpu.SemaphoreType.DMA((n_outer // 2 + 4,))],
    )


def gauge_kernel(mine, along, b, c, b_out, c1, c2, held):
    e = held.shape[0]
    tiles = e // T
    held[...] = unpack(mine, 0, tiles) + unpack(along, 0, tiles)
    inverse_factor(held)
    b_out[...] = dot(b[...], held[...], NT)
    scaled = dot3(split(c[e:, :]), split(held[...]), NT)
    for at in range(3 * tiles * tiles):
        r, k = at // tiles * T, at % tiles * T
        tile = c[r : r + T, k : k + T] if r < e else scaled[r - e : r - e + T, k : k + T]
        ref, spot = (c1, at * T) if at * T < c1.shape[0] else (c2, at * T - c1.shape[0])
        ref[spot : spot + T, :] = tile


def gauge(mine, along, b, c, last):
    e = b.shape[0]
    return call(
        gauge_kernel,
        "gauge_side",
        [((e, e), F32), ((3 * e * e // T - last, T), F32), ((last, T), F32)],
        [(VMEM, x) for x in (mine, along, b, c)],
        [pltpu.VMEM((e, e), F32)],
    )


def couple(b):
    mine, across, along, corner = (ref[...] for ref in b)
    return jnp.concatenate(
        [jnp.concatenate([mine, across], axis=1), jnp.concatenate([along, corner], axis=1)], axis=0
    )


def factor_start_kernel(a0, a1, hs, a3, b0, b1, b2, b3, side):
    e = b0.shape[0]
    tiles = e // T
    coup = couple((b0, b1, b2, b3))
    side[...] = -dot(coup, coup, NT)
    side[:e, :e] = side[:e, :e] + (unpack(a0, 0, tiles) + unpack(a1, 0, tiles))
    side[e:, e:] = side[e:, e:] + (
        unpack(hs, len(upper(tiles)) * T, tiles) + unpack(a3, 0, tiles)
    )
    sweep(side, 0, e)


def factor_start(a, b):
    e = b[0].shape[0]
    return call(
        factor_start_kernel,
        "factor_start",
        [((2 * e, 2 * e), F32)],
        [(VMEM, x) for x in (*a, *b)],
        [],
    )[0]


def factor_end_kernel(place, side_in, b0, b1, b2, b3, high, low, side, full):
    e = b0.shape[0]
    side[...] = side_in[...]
    sweep(side, e, 2 * e)
    coup = split(couple((b0, b1, b2, b3)))
    away = dot3(split(side[...]), coup)
    shape = full.shape
    unit = lax.broadcasted_iota(jnp.int32, shape, 0) == lax.broadcasted_iota(jnp.int32, shape, 1)
    full[...] = dot3(coup, split(away), TN) + unit.astype(F32)

    def emit(value, rows, columns):
        high[rows, columns], low[rows, columns] = split(value)

    first, rest = slice(0, e), slice(e, 3 * e)
    emit(full[...], rest, rest)
    emit(-away[:e, :], first, rest)
    same = place[0] == place[1]

    @pl.when(same)
    def _():
        emit(side[:e, :e], first, first)
        emit(-away[:e, :].T, rest, first)

    @pl.when(jnp.logical_not(same))
    def _():
        emit(side[:e, e:], first, first)
        emit(-away[e:, :].T, rest, first)


def factor_end(place, side, b):
    e = b[0].shape[0]
    return call(
        factor_end_kernel,
        "factor_end",
        [((3 * e, 3 * e), BF16)] * 2,
        [(SMEM, place), (VMEM, side)] + [(VMEM, x) for x in b],
        [pltpu.VMEM((2 * e, 2 * e), F32), pltpu.VMEM((2 * e, 2 * e), F32)],
    )


def cross_block(first, at, c1, c2):
    rest = jnp.concatenate([c1[...], c2[...]], axis=0)
    e = math.isqrt(rest.shape[0] * T // 3)
    n = e * e // T
    tiles = e // T
    return jnp.concatenate(
        [
            jnp.concatenate([unpack_full(first, at, tiles), unpack_full(rest, n, tiles)], axis=1),
            jnp.concatenate([unpack_full(rest, 0, tiles), unpack_full(rest, 2 * n, tiles)], axis=1),
        ],
        axis=0,
    )


def times_inverse(cross, high, low, inner):
    e = cross.shape[1] // 2
    return dot3(split(cross[:, :e]), (high[:e], low[:e])) + dot3(
        split(cross[:, e:]), (high[inner], low[inner])
    )


def rows_kernel(
    place, leaf, high, low, a0, c01, c02, swapped, c21, c22, top, bottom, block, col, own, sem
):
    e = leaf.shape[1] // 4
    n_sym = len(upper(e // T)) * T
    ext, _ = sides(place)
    copies = []
    for r in range(2):
        for c in range(2):
            target = own.at[pl.ds(r * e, e), pl.ds(c * e, e)]
            source = leaf_block(leaf, ext[r], ext[c], 0, 0, e)
            copies.append(pltpu.make_async_copy(source, target, sem.at[2 * r + c]))
            copies[-1].start()
    same = place[0] == place[1]
    mine = cross_block(a0, n_sym, c01, c02)

    @pl.when(same)
    def _():
        col[...] = mine

    @pl.when(jnp.logical_not(same))
    def _():
        col[...] = cross_block(swapped, 0, c21, c22)

    left = split(times_inverse(mine, high[...], low[...], slice(e, 2 * e)))
    top[...], bottom[...] = left
    left = [x[:, : 2 * e] for x in left]
    block[...] = -dot3(left, split(col[...]), NT)
    for copy in copies:
        copy.wait()

    @pl.when(same)
    def _():
        block[...] = block[...] + own[...]


def own_rows(place, leaf, high, low, a0, c01, c02, swapped, c21, c22):
    e = leaf.shape[1] // 4
    return call(
        rows_kernel,
        "own_rows",
        [((2 * e, 3 * e), BF16)] * 2 + [((2 * e, 2 * e), F32)],
        [(SMEM, place), (HBM, leaf)]
        + [(VMEM, x) for x in (high, low, a0, c01, c02, swapped, c21, c22)],
        [
            pltpu.VMEM((2 * e, 2 * e), F32),
            pltpu.VMEM((2 * e, 2 * e), F32),
            pltpu.SemaphoreType.DMA((4,)),
        ],
    )


def spot(place, e, side, which):
    x = place[0] if which == 0 else 1 - place[0]
    return pl.ds(pl.multiple_of((2 * side + x) * e, T), e)


def write(out, place, value, a, b):
    e = out.shape[1] // 4
    for r in range(2):
        for c in range(2):
            out[0, spot(place, e, r, a), spot(place, e, c, b)] = value[
                r * e : (r + 1) * e, c * e : (c + 1) * e
            ]


def pick(ref, rows, b):
    e = ref.shape[1] // 3
    return jnp.concatenate([ref[rows, :e], ref[rows, (1 + b) * e : (2 + b) * e]], axis=1)


def products_kernel(
    place, high, low, top, bottom, block, a0, c01, c02, a1, c11, c12, a3, c31, c32, out, part, scratch
):
    e = out.shape[1] // 4
    n_sym = len(upper(e // T)) * T
    same = place[0] == place[1]
    write(out, place, block[...], 0, 0)
    everything = slice(0, 2 * e)

    @pl.when(same)
    def _():
        across = cross_block(a1, n_sym, c11, c12)
        right = split(across)
        left = [pick(x, everything, 1) for x in (top, bottom)]
        write(out, place, -dot3(left, right, NT), 0, 1)
        scratch[...] = times_inverse(across, high[...], low[...], slice(2 * e, 3 * e))
        left = split(pick(scratch, everything, 0))
        write(out, place, -dot3(left, split(cross_block(a0, n_sym, c01, c02)), NT), 1, 0)
        left = split(pick(scratch, everything, 1))
        part[...] = -dot3(left, right, NT)

    @pl.when(jnp.logical_not(same))
    def _():
        right = split(cross_block(a3, n_sym, c31, c32))
        left = [pick(x, everything, 1) for x in (top, bottom)]
        write(out, place, -dot3(left, right, NT), 0, 1)


def products(place, high, low, top, bottom, block, mine, across, corner):
    e = block.shape[0] // 2
    return call(
        products_kernel,
        "products",
        [((1, 4 * e, 4 * e), F32), ((2 * e, 2 * e), F32)],
        [(SMEM, place)]
        + [(VMEM, x) for x in (high, low, top, bottom, block, *mine, *across, *corner)],
        [pltpu.VMEM((2 * e, 3 * e), F32)],
    )


def finish_kernel(
    place, before, high, low, part, passed, last, a1, c11, swapped, c21, c22, a3, c31, out, held, scratch, sem
):
    e = out.shape[1] // 4
    tiles = e // T
    n_sym = len(upper(tiles)) * T

    def targets(b):
        return [
            (
                held.at[pl.ds(r * e, e), pl.ds((2 * b + c) * e, e)],
                out.at[0, spot(place, e, r, 1), spot(place, e, c, b)],
            )
            for r in range(2)
            for c in range(2)
        ]

    @pl.when(place[0] == place[1])
    def _():
        half = last.shape[0]
        for at, (i, j) in enumerate(upper(2 * tiles)):
            ref, at = (last, at * T) if at * T < half else (passed, at * T - half)
            piece = ref[at : at + T, :]
            r, c = slice(i * T, (i + 1) * T), slice(j * T, (j + 1) * T)
            shift = 2 * e
            held[r, j * T + shift : (j + 1) * T + shift] = part[r, c] + piece
            if i != j:
                held[c, i * T + shift : (i + 1) * T + shift] = part[c, r] + piece.T
        run_copies(targets(1), sem)

    @pl.when(place[0] != place[1])
    def _():
        across = cross_block(a1, n_sym, c11, last)
        scratch[...] = times_inverse(across, high[...], low[...], slice(2 * e, 3 * e))
        everything = slice(0, 2 * e)
        copies = []
        for b in range(2):
            col = cross_block(swapped, 0, c21, c22) if b == 0 else cross_block(a3, n_sym, c31, passed)
            left = split(pick(scratch, everything, b))
            held[:, 2 * e * b : 2 * e * (b + 1)] = -dot3(left, split(col), NT)
            for i, (source, target) in enumerate(targets(b)):
                copies.append(pltpu.make_async_copy(source, target, sem.at[4 * b + i]))
                copies[-1].start()
        for copy in copies:
            copy.wait()


def finish(place, before, high, low, part, passed, last, a1, c11, swapped, c21, c22, a3, c31):
    e = before.shape[1] // 4
    return call(
        finish_kernel,
        "finish",
        [(before.shape, F32)],
        [(SMEM, place), (HBM, before)]
        + [
            (VMEM, x)
            for x in (high, low, part, passed, last, a1, c11, swapped, c21, c22, a3, c31)
        ],
        [
            pltpu.VMEM((2 * e, 4 * e), F32),
            pltpu.VMEM((2 * e, 3 * e), F32),
            pltpu.SemaphoreType.DMA((8,)),
        ],
        out_specs=[HBM],
        input_output_aliases={1: 0},
    )[0]


def tie(*values):
    return lax.optimization_barrier(values)


def solution(mesh):
    nx, ny = mesh.shape["gx"], mesh.shape["gy"]
    devices = [(x, y) for x in range(nx) for y in range(ny)]

    def is_same(x, y):
        return x // (nx // 2) == y // (ny // 2)

    def send(value, along_y, only=None):
        pairs = []
        for x, y in devices:
            if only is None or is_same(x, y) == only:
                to = (x, (y + ny // 2) % ny) if along_y else ((x + nx // 2) % nx, y)
                pairs.append((x * ny + y, to[0] * ny + to[1]))
        return lax.ppermute(value, ("gx", "gy"), pairs)

    def body(leaf):
        e = leaf.shape[1] // 4
        v = lax.axis_index("gx") // (nx // 2)
        u = lax.axis_index("gy") // (ny // 2)
        place = jnp.stack([v, u]).astype(jnp.int32)
        same = u == v
        a, hs = cut_first(place, leaf)
        a_x = send(a, False)
        hs_y = send(hs, True)
        outer0, swap, b, c = cut_second(place, leaf)
        swapped = send(swap, True)
        b, c1, c2 = gauge(hs, hs_y, b, c, swap.shape[0])
        b_x = send(b, False)
        b_y = send(b, True)
        a_x, b_y = tie(a_x, b_y)
        a_d = send(a_x, True)
        b_d = send(b_x, True)
        c1, b_x = tie(c1, b_x)
        c1_x = send(c1, False)
        c1, c2, b_d = tie(c1, c2, b_d)
        c1_y = send(c1, True, only=True)
        c2_y = send(c2, True, only=True)
        side = factor_start((a, a_x, hs_y, a_d), (b, b_x, b_y, b_d))
        third, c1_x, side = tie(jnp.where(same, swapped, c2), c1_x, side)
        third = send(third, False)
        c1_d = send(c1_x, True, only=True)
        high, low = factor_end(place, side, (b, b_x, b_y, b_d))
        last, high = tie(jnp.where(same, c2, outer0), high)
        last = send(last, False)
        passed = send(third, True)
        top, bottom, block = own_rows(place, leaf, high, low, a, c1, c2, swapped, c1_y, c2_y)
        out, part = products(
            place, high, low, top, bottom, block, (a, c1, c2), (a_x, c1_x, third), (a_d, c1_d, passed)
        )
        return finish(
            place, out, high, low, part, passed, last, a_x, c1_x, swapped, c1_y, c2_y, a_d, c1_d
        )

    return jax.shard_map(
        body,
        mesh=mesh,
        in_specs=(P(None, "gy", "gx"),),
        out_specs=P(None, "gy", "gx"),
        check_vma=False,
    )
```

```python
import math

import jax
import jax.numpy as jnp
from jax import lax
from jax.experimental import pallas as pl
from jax.experimental.pallas import tpu as pltpu
from jax.sharding import PartitionSpec as P

F32 = jnp.float32
BF16 = jnp.bfloat16
T = 128
R = 16
FIRST = 2
COST = 10**10
HBM = pl.BlockSpec(memory_space=pl.ANY)
VMEM = pl.BlockSpec(memory_space=pltpu.VMEM)
SMEM = pl.BlockSpec(memory_space=pltpu.SMEM)
PARAMS = pltpu.CompilerParams(vmem_limit_bytes=32 * 2**20)


def dot(a, b, dims=((1,), (0,))):
    return lax.dot_general(
        a, b, (dims, ((), ())), precision=lax.Precision.HIGHEST, preferred_element_type=F32
    )


def dot16(a, b, dims=((1,), (0,))):
    return lax.dot_general(a, b, (dims, ((), ())), preferred_element_type=F32)


def split(a):
    high = a.astype(BF16)
    return high, (a - high.astype(F32)).astype(BF16)


def dot3(a, b, dims=((1,), (0,))):
    return dot16(a[0], b[0], dims) + (dot16(a[0], b[1], dims) + dot16(a[1], b[0], dims))


NT = ((1,), (1,))
TN = ((0,), (0,))


def upper(n):
    return [(i, j) for i in range(n) for j in range(i, n)]


def across_lanes(x, k):
    return jnp.broadcast_to(x[:, k : k + 1], x.shape)


def across_rows(x, k):
    return jnp.broadcast_to(x[k : k + 1, :], x.shape)


def panel(rows, c0, lower):
    sub = lax.broadcasted_iota(jnp.int32, rows.shape, 0)
    lane = lax.broadcasted_iota(jnp.int32, rows.shape, 1)
    cols = [across_lanes(rows, c0 + k) for k in range(R)]
    out = jnp.where((lane >= c0) & (lane < c0 + R), (lane - c0 == sub).astype(F32), rows)
    half = out
    scale = jnp.ones_like(rows)
    for k in range(R):
        pivot = across_rows(cols[k], k)
        inv = 1.0 / pivot
        here = sub == k
        mult = cols[k]

        def step(x):
            row = across_rows(x, k) * inv
            return jnp.where(here, row, x - mult * row)

        if lower:
            scale = jnp.where(here, pivot, scale)
            half = half - jnp.where(sub > k, mult, 0.0) * (across_rows(half, k) * inv)
        out = step(out)
        for j in range(k + 1, R):
            cols[j] = step(cols[j])
    return out, half * lax.rsqrt(scale) if lower else None


def put_rows(matrix, rows, r0):
    parts = [matrix[:r0]] if r0 else []
    parts.append(rows)
    if r0 + rows.shape[0] < matrix.shape[0]:
        parts.append(matrix[r0 + rows.shape[0] :])
    return jnp.concatenate(parts, axis=0)


def invert_tile(m, lower=False):
    lane = lax.broadcasted_iota(jnp.int32, (T, T), 1)
    sub = lax.broadcasted_iota(jnp.int32, (T, T), 0)
    rows = m[:R]
    for c0 in range(0, T, R):
        swept, half = panel(rows, c0, lower)
        if c0 + R < T:
            old = m[c0 + R : c0 + 2 * R]
            inside = (lane[:R] >= c0) & (lane[:R] < c0 + R)
            rows = jnp.where(inside, 0.0, old)
            for k in range(R):
                rows = rows - across_lanes(old, c0 + k) * across_rows(swept, k)
        wide = put_rows(jnp.zeros((T, T), F32), swept, c0)
        rest = jnp.where((lane >= c0) & (lane < c0 + R), 0.0, m) - dot(m, wide)
        if lower:
            rest = jnp.where(sub < c0, m, rest)
        m = put_rows(rest, half if lower else swept, c0)
    return jnp.where(lane > sub, 0.0, m) if lower else m


def sweep(ref, start, stop):
    n = ref.shape[0]
    for p in range(start, stop, T):
        pivot = invert_tile(ref[p : p + T, p : p + T])
        rows = dot(pivot, ref[p : p + T, :])
        parts = ([rows[:, :p]] if p else []) + [pivot]
        if p + T < n:
            parts.append(rows[:, p + T :])
        rows = jnp.concatenate(parts, axis=1)
        for q in range(0, n, T):
            if q != p:
                change = dot(ref[q : q + T, p : p + T], rows)
                ref[q : q + T, p : p + T] = jnp.zeros((T, T), F32)
                ref[q : q + T, :] = ref[q : q + T, :] - change
        ref[p : p + T, :] = rows


def inverse_factor(ref):
    n = ref.shape[0]
    for p in range(0, n, T):
        pivot = invert_tile(ref[p : p + T, p : p + T], lower=True)
        scaled = dot(pivot, ref[p : p + T, :])
        for q in range(p + T, n, T):
            weight = scaled[:, q : q + T]
            ref[q : q + T, :] = ref[q : q + T, :] - dot(weight, scaled, TN)
            ref[q : q + T, p : p + T] = -dot(weight, pivot, TN)
        for q in range(0, n, T):
            if q < p:
                ref[p : p + T, q : q + T] = scaled[:, q : q + T]
            else:
                ref[p : p + T, q : q + T] = pivot if q == p else jnp.zeros((T, T), F32)


def leaf_block(leaf, side_r, side_c, r, c, size):
    e = leaf.shape[1] // 4
    return leaf.at[
        0,
        pl.ds(pl.multiple_of(side_r * e + r * size, T), size),
        pl.ds(pl.multiple_of(side_c * e + c * size, T), size),
    ]


def run_copies(pairs, sem):
    copies = [pltpu.make_async_copy(a, b, sem.at[i]) for i, (a, b) in enumerate(pairs)]
    for copy in copies:
        copy.start()
    for copy in copies:
        copy.wait()


def sides(place):
    v, u = place[0], place[1]
    return [v, 2 + u], [1 - v, 3 - u]


def unpack(ref, at, tiles):
    held = {}
    for r, c in upper(tiles):
        held[r, c] = ref[at : at + T, :]
        if c > r:
            held[c, r] = held[r, c].T
        at += T
    return jnp.concatenate(
        [jnp.concatenate([held[r, c] for c in range(tiles)], axis=1) for r in range(tiles)], axis=0
    )


def call(kernel, name, outs, ins, scratch, **more):
    return pl.pallas_call(
        kernel,
        out_shape=[jax.ShapeDtypeStruct(shape, dtype) for shape, dtype in outs],
        in_specs=[spec for spec, _ in ins],
        out_specs=more.pop("out_specs", [VMEM] * len(outs)),
        scratch_shapes=scratch,
        compiler_params=PARAMS,
        cost_estimate=pl.CostEstimate(flops=COST, bytes_accessed=COST, transcendentals=0),
        name=name,
        **more,
    )(*[value for _, value in ins])


def block_tiles(leaf, side_r, side_c, at):
    tiles = leaf.shape[1] // 4 // T
    return leaf_block(leaf, side_r, side_c, at // tiles, at % tiles, T)


def cut_first_kernel(place, leaf, a, hh, sem):
    tiles = leaf.shape[1] // 4 // T
    ext, inn = sides(place)
    n_sym = len(upper(tiles))
    pairs = []
    for at, (r, c) in enumerate(upper(tiles)):
        pairs.append((leaf_block(leaf, inn[0], inn[0], r, c, T), a.at[pl.ds(at * T, T)]))
        pairs.append((leaf_block(leaf, inn[1], inn[1], r, c, T), hh.at[pl.ds(at * T, T)]))
    for at in range(FIRST):
        pairs.append(
            (block_tiles(leaf, ext[0], inn[0], at), a.at[pl.ds((n_sym + at) * T, T)])
        )
    run_copies(pairs, sem)


def cut_first(place, leaf):
    n_sym = len(upper(leaf.shape[1] // 4 // T))
    return call(
        cut_first_kernel,
        "cut_first",
        [(((n_sym + FIRST) * T, T), F32), ((n_sym * T, T), F32)],
        [(SMEM, place), (HBM, leaf)],
        [pltpu.SemaphoreType.DMA((2 * n_sym + FIRST,))],
    )


def cut_second_kernel(place, leaf, swap, outer0, b, c, sem):
    e = leaf.shape[1] // 4
    tiles = e // T
    ext, inn = sides(place)
    n_sym = len(upper(tiles))
    pairs = [
        (leaf_block(leaf, inn[0], inn[1], 0, 0, e), b),
        (leaf_block(leaf, ext[0], inn[0], 0, 0, e), c.at[pl.ds(0, e)]),
        (leaf_block(leaf, ext[1], inn[0], 0, 0, e), c.at[pl.ds(e, e)]),
        (leaf_block(leaf, ext[0], inn[1], 0, 0, e), c.at[pl.ds(2 * e, e)]),
        (leaf_block(leaf, ext[1], inn[1], 0, 0, e), c.at[pl.ds(3 * e, e)]),
    ]
    for at, (r, k) in enumerate(upper(tiles)):
        pairs.append((leaf_block(leaf, inn[0], inn[0], r, k, T), swap.at[pl.ds(at * T, T)]))
    half = outer0.shape[0] // T
    second = []
    for at, (r, k) in enumerate(upper(2 * tiles)):
        source = leaf_block(leaf, ext[r // tiles], ext[k // tiles], r % tiles, k % tiles, T)
        if at < half:
            pairs.append((source, outer0.at[pl.ds(at * T, T)]))
        else:
            second.append((source, swap.at[pl.ds((n_sym + at - half) * T, T)]))
    run_copies(pairs, sem)
    same = place[0] == place[1]

    @pl.when(same)
    def _():
        cross = [
            (block_tiles(leaf, ext[0], inn[0], at), swap.at[pl.ds((n_sym + at) * T, T)])
            for at in range(FIRST)
        ]
        run_copies(cross, sem)

    @pl.when(jnp.logical_not(same))
    def _():
        run_copies(second, sem)


def cut_second(place, leaf):
    e = leaf.shape[1] // 4
    n_sym = len(upper(e // T))
    half = len(upper(2 * (e // T))) // 2
    return call(
        cut_second_kernel,
        "cut_second",
        [(((n_sym + half) * T, T), F32), ((half * T, T), F32), ((e, e), F32), ((4 * e, e), F32)],
        [(SMEM, place), (HBM, leaf)],
        [pltpu.SemaphoreType.DMA((n_sym + half + 5,))],
    )


def gauge_kernel(mine, along, b, c, b_out, c1, c2, held):
    e = held.shape[0]
    tiles = e // T
    held[...] = unpack(mine, 0, tiles) + unpack(along, 0, tiles)
    inverse_factor(held)
    b_out[...] = dot(b[...], held[...], NT)
    scaled = dot3(split(c[2 * e :, :]), split(held[...]), NT)
    for at in range(FIRST, 4 * tiles * tiles):
        r, k = at // tiles * T, at % tiles * T
        tile = c[r : r + T, k : k + T] if r < 2 * e else scaled[r - 2 * e : r - 2 * e + T, k : k + T]
        spot = (at - FIRST) * T
        ref, spot = (c1, spot) if spot < c1.shape[0] else (c2, spot - c1.shape[0])
        ref[spot : spot + T, :] = tile


def gauge(mine, along, b, c, last):
    e = b.shape[0]
    return call(
        gauge_kernel,
        "gauge_side",
        [((e, e), F32), ((4 * e * e // T - FIRST * T - last, T), F32), ((last, T), F32)],
        [(VMEM, x) for x in (mine, along, b, c)],
        [pltpu.VMEM((e, e), F32)],
    )


def couple(b):
    mine, across, along, corner = (ref[...] for ref in b)
    return jnp.concatenate(
        [jnp.concatenate([mine, across], axis=1), jnp.concatenate([along, corner], axis=1)], axis=0
    )


def factor_start_kernel(a0, a1, a2, a3, b0, b1, b2, b3, side):
    e = b0.shape[0]
    tiles = e // T
    coup = couple((b0, b1, b2, b3))
    side[...] = -dot(coup, coup, NT)
    side[:e, :e] = side[:e, :e] + (unpack(a0, 0, tiles) + unpack(a1, 0, tiles))
    side[e:, e:] = side[e:, e:] + (unpack(a2, 0, tiles) + unpack(a3, 0, tiles))
    sweep(side, 0, e)


def factor_start(a, b):
    e = b[0].shape[0]
    return call(
        factor_start_kernel,
        "factor_start",
        [((2 * e, 2 * e), F32)],
        [(VMEM, x) for x in (*a, *b)],
        [],
    )[0]


def factor_end_kernel(place, side_in, b0, b1, b2, b3, high, low, side, full):
    e = b0.shape[0]
    side[...] = side_in[...]
    sweep(side, e, 2 * e)
    coup = split(couple((b0, b1, b2, b3)))
    away = dot3(split(side[...]), coup)
    shape = full.shape
    unit = lax.broadcasted_iota(jnp.int32, shape, 0) == lax.broadcasted_iota(jnp.int32, shape, 1)
    full[...] = dot3(coup, split(away), TN) + unit.astype(F32)

    def emit(value, rows, columns):
        high[rows, columns], low[rows, columns] = split(value)

    first, rest = slice(0, e), slice(e, 3 * e)
    emit(full[...], rest, rest)
    emit(-away[:e, :], first, rest)
    same = place[0] == place[1]

    @pl.when(same)
    def _():
        emit(side[:e, :e], first, first)
        emit(-away[:e, :].T, rest, first)

    @pl.when(jnp.logical_not(same))
    def _():
        emit(side[:e, e:], first, first)
        emit(-away[e:, :].T, rest, first)


def factor_end(place, side, b):
    e = b[0].shape[0]
    return call(
        factor_end_kernel,
        "factor_end",
        [((3 * e, 3 * e), BF16)] * 2,
        [(SMEM, place), (VMEM, side)] + [(VMEM, x) for x in b],
        [pltpu.VMEM((2 * e, 2 * e), F32), pltpu.VMEM((2 * e, 2 * e), F32)],
    )


def cross_block(first, c1, c2):
    n1, n2 = c1.shape[0] // T, c2.shape[0] // T
    tiles = math.isqrt((FIRST + n1 + n2) // 4)
    n_sym = len(upper(tiles))
    held = [first[(n_sym + at) * T : (n_sym + at + 1) * T, :] for at in range(FIRST)]
    held += [ref[at * T : (at + 1) * T, :] for ref, n in ((c1, n1), (c2, n2)) for at in range(n)]
    rows = []
    for r in range(2 * tiles):
        side = r // tiles
        row = [held[((side + 2 * c) * tiles + r % tiles) * tiles + k] for c in range(2) for k in range(tiles)]
        rows.append(jnp.concatenate(row, axis=1))
    return jnp.concatenate(rows, axis=0)


def times_inverse(cross, high, low, inner):
    e = cross.shape[1] // 2
    return dot3(split(cross[:, :e]), (high[:e], low[:e])) + dot3(
        split(cross[:, e:]), (high[inner], low[inner])
    )


def rows_kernel(
    place, leaf, high, low, a0, c01, c02, swapped, c21, c22, top, bottom, block, col, own, sem
):
    e = leaf.shape[1] // 4
    ext, _ = sides(place)
    copies = []
    for r in range(2):
        for c in range(2):
            target = own.at[pl.ds(r * e, e), pl.ds(c * e, e)]
            source = leaf_block(leaf, ext[r], ext[c], 0, 0, e)
            copies.append(pltpu.make_async_copy(source, target, sem.at[2 * r + c]))
            copies[-1].start()
    same = place[0] == place[1]
    mine = cross_block(a0, c01, c02)

    @pl.when(same)
    def _():
        col[...] = mine

    @pl.when(jnp.logical_not(same))
    def _():
        col[...] = cross_block(swapped, c21, c22)

    left = split(times_inverse(mine, high[...], low[...], slice(e, 2 * e)))
    top[...], bottom[...] = left
    left = [x[:, : 2 * e] for x in left]
    block[...] = -dot3(left, split(col[...]), NT)
    for copy in copies:
        copy.wait()

    @pl.when(same)
    def _():
        block[...] = block[...] + own[...]


def own_rows(place, leaf, high, low, a0, c01, c02, swapped, c21, c22):
    e = leaf.shape[1] // 4
    return call(
        rows_kernel,
        "own_rows",
        [((2 * e, 3 * e), BF16)] * 2 + [((2 * e, 2 * e), F32)],
        [(SMEM, place), (HBM, leaf)]
        + [(VMEM, x) for x in (high, low, a0, c01, c02, swapped, c21, c22)],
        [
            pltpu.VMEM((2 * e, 2 * e), F32),
            pltpu.VMEM((2 * e, 2 * e), F32),
            pltpu.SemaphoreType.DMA((4,)),
        ],
    )


def spot(place, e, side, which):
    x = place[0] if which == 0 else 1 - place[0]
    return pl.ds(pl.multiple_of((2 * side + x) * e, T), e)


def write(out, place, value, a, b):
    e = out.shape[1] // 4
    for r in range(2):
        for c in range(2):
            out[0, spot(place, e, r, a), spot(place, e, c, b)] = value[
                r * e : (r + 1) * e, c * e : (c + 1) * e
            ]


def pick(ref, rows, b):
    e = ref.shape[1] // 3
    return jnp.concatenate([ref[rows, :e], ref[rows, (1 + b) * e : (2 + b) * e]], axis=1)


def products_kernel(
    place, high, low, top, bottom, block, a0, c01, c02, a1, c11, c12, a3, c31, c32, out, part, scratch
):
    e = out.shape[1] // 4
    same = place[0] == place[1]
    write(out, place, block[...], 0, 0)
    everything = slice(0, 2 * e)

    @pl.when(same)
    def _():
        across = cross_block(a1, c11, c12)
        right = split(across)
        left = [pick(x, everything, 1) for x in (top, bottom)]
        write(out, place, -dot3(left, right, NT), 0, 1)
        scratch[...] = times_inverse(across, high[...], low[...], slice(2 * e, 3 * e))
        left = split(pick(scratch, everything, 0))
        write(out, place, -dot3(left, split(cross_block(a0, c01, c02)), NT), 1, 0)
        left = split(pick(scratch, everything, 1))
        part[...] = -dot3(left, right, NT)

    @pl.when(jnp.logical_not(same))
    def _():
        right = split(cross_block(a3, c31, c32))
        left = [pick(x, everything, 1) for x in (top, bottom)]
        write(out, place, -dot3(left, right, NT), 0, 1)


def products(place, high, low, top, bottom, block, mine, across, corner):
    e = block.shape[0] // 2
    return call(
        products_kernel,
        "products",
        [((1, 4 * e, 4 * e), F32), ((2 * e, 2 * e), F32)],
        [(SMEM, place)]
        + [(VMEM, x) for x in (high, low, top, bottom, block, *mine, *across, *corner)],
        [pltpu.VMEM((2 * e, 3 * e), F32)],
    )


def finish_kernel(
    place, before, high, low, part, passed, last, a1, c11, swapped, c21, c22, a3, c31, out, held, scratch, sem
):
    e = out.shape[1] // 4
    tiles = e // T

    def targets(b):
        return [
            (
                held.at[pl.ds(r * e, e), pl.ds((2 * b + c) * e, e)],
                out.at[0, spot(place, e, r, 1), spot(place, e, c, b)],
            )
            for r in range(2)
            for c in range(2)
        ]

    @pl.when(place[0] == place[1])
    def _():
        half = last.shape[0]
        for at, (i, j) in enumerate(upper(2 * tiles)):
            ref, at = (last, at * T) if at * T < half else (passed, at * T - half)
            piece = ref[at : at + T, :]
            r, c = slice(i * T, (i + 1) * T), slice(j * T, (j + 1) * T)
            shift = 2 * e
            held[r, j * T + shift : (j + 1) * T + shift] = part[r, c] + piece
            if i != j:
                held[c, i * T + shift : (i + 1) * T + shift] = part[c, r] + piece.T
        run_copies(targets(1), sem)

    @pl.when(place[0] != place[1])
    def _():
        across = cross_block(a1, c11, last)
        scratch[...] = times_inverse(across, high[...], low[...], slice(2 * e, 3 * e))
        everything = slice(0, 2 * e)
        copies = []
        for b in range(2):
            col = cross_block(swapped, c21, c22) if b == 0 else cross_block(a3, c31, passed)
            left = split(pick(scratch, everything, b))
            held[:, 2 * e * b : 2 * e * (b + 1)] = -dot3(left, split(col), NT)
            for i, (source, target) in enumerate(targets(b)):
                copies.append(pltpu.make_async_copy(source, target, sem.at[4 * b + i]))
                copies[-1].start()
        for copy in copies:
            copy.wait()


def finish(place, before, high, low, part, passed, last, a1, c11, swapped, c21, c22, a3, c31):
    e = before.shape[1] // 4
    return call(
        finish_kernel,
        "finish",
        [(before.shape, F32)],
        [(SMEM, place), (HBM, before)]
        + [
            (VMEM, x)
            for x in (high, low, part, passed, last, a1, c11, swapped, c21, c22, a3, c31)
        ],
        [
            pltpu.VMEM((2 * e, 4 * e), F32),
            pltpu.VMEM((2 * e, 3 * e), F32),
            pltpu.SemaphoreType.DMA((8,)),
        ],
        out_specs=[HBM],
        input_output_aliases={1: 0},
    )[0]


def tie(*values):
    return lax.optimization_barrier(values)


def solution(mesh):
    nx, ny = mesh.shape["gx"], mesh.shape["gy"]
    devices = [(x, y) for x in range(nx) for y in range(ny)]

    def is_same(x, y):
        return x // (nx // 2) == y // (ny // 2)

    def send(value, along_y, only=None):
        pairs = []
        for x, y in devices:
            if only is None or is_same(x, y) == only:
                to = (x, (y + ny // 2) % ny) if along_y else ((x + nx // 2) % nx, y)
                pairs.append((x * ny + y, to[0] * ny + to[1]))
        return lax.ppermute(value, ("gx", "gy"), pairs)

    def body(leaf):
        e = leaf.shape[1] // 4
        v = lax.axis_index("gx") // (nx // 2)
        u = lax.axis_index("gy") // (ny // 2)
        place = jnp.stack([v, u]).astype(jnp.int32)
        same = u == v
        a, hh = cut_first(place, leaf)
        a_x = send(a, False)
        hh_y = send(hh, True)
        swap, outer0, b, c = cut_second(place, leaf)
        swapped = send(swap, True)
        b, c1, c2 = gauge(hh, hh_y, b, c, outer0.shape[0])
        b, a_x, swapped = tie(b, a_x, swapped)
        b_x = send(b, False)
        b_y = send(b, True)
        a_d = send(a_x, True)
        a_d, b_x, b_y = tie(a_d, b_x, b_y)
        b_d = send(b_x, True)
        c1, b_x = tie(c1, b_x)
        c1_x = send(c1, False)
        c1, c2, b_d = tie(c1, c2, b_d)
        c1_y = send(c1, True, only=True)
        c2_y = send(c2, True, only=True)
        side = factor_start((a, a_x, swapped, a_d), (b, b_x, b_y, b_d))
        third, side = tie(jnp.where(same, swapped[-outer0.shape[0] :], c2), side)
        third = send(third, False)
        c1_d = send(c1_x, True, only=True)
        high, low = factor_end(place, side, (b, b_x, b_y, b_d))
        last, high = tie(jnp.where(same, c2, outer0), high)
        last = send(last, False)
        passed = send(third, True)
        top, bottom, block = own_rows(place, leaf, high, low, a, c1, c2, swapped, c1_y, c2_y)
        out, part = products(
            place, high, low, top, bottom, block, (a, c1, c2), (a_x, c1_x, third), (a_d, c1_d, passed)
        )
        return finish(
            place, out, high, low, part, passed, last, a_x, c1_x, swapped, c1_y, c2_y, a_d, c1_d
        )

    return jax.shard_map(
        body,
        mesh=mesh,
        in_specs=(P(None, "gy", "gx"),),
        out_specs=P(None, "gy", "gx"),
        check_vma=False,
    )
```

```python
import math

import jax
import jax.numpy as jnp
from jax import lax
from jax.experimental import pallas as pl
from jax.experimental.pallas import tpu as pltpu
from jax.sharding import PartitionSpec as P

F32 = jnp.float32
BF16 = jnp.bfloat16
T = 128
R = 16
FIRST = 1
HBM = pl.BlockSpec(memory_space=pl.ANY)
FAR = pl.BlockSpec(memory_space=pltpu.HBM)
VMEM = pl.BlockSpec(memory_space=pltpu.VMEM)
SMEM = pl.BlockSpec(memory_space=pltpu.SMEM)
PARAMS = pltpu.CompilerParams(vmem_limit_bytes=32 * 2**20)


def dot(a, b, dims=((1,), (0,))):
    return lax.dot_general(
        a, b, (dims, ((), ())), precision=lax.Precision.HIGHEST, preferred_element_type=F32
    )


def dot16(a, b, dims=((1,), (0,))):
    return lax.dot_general(a, b, (dims, ((), ())), preferred_element_type=F32)


def split(a):
    high = a.astype(BF16)
    return high, (a - high.astype(F32)).astype(BF16)


def dot3(a, b, dims=((1,), (0,))):
    return dot16(a[0], b[0], dims) + (dot16(a[0], b[1], dims) + dot16(a[1], b[0], dims))


NT = ((1,), (1,))
TN = ((0,), (0,))


def upper(n):
    return [(i, j) for i in range(n) for j in range(i, n)]


def across_lanes(x, k):
    return jnp.broadcast_to(x[:, k : k + 1], x.shape)


def across_rows(x, k):
    return jnp.broadcast_to(x[k : k + 1, :], x.shape)


def panel(rows, c0, lower):
    sub = lax.broadcasted_iota(jnp.int32, rows.shape, 0)
    lane = lax.broadcasted_iota(jnp.int32, rows.shape, 1)
    cols = [across_lanes(rows, c0 + k) for k in range(R)]
    out = jnp.where((lane >= c0) & (lane < c0 + R), (lane - c0 == sub).astype(F32), rows)
    half = out
    scale = jnp.ones_like(rows)
    for k in range(R):
        pivot = across_rows(cols[k], k)
        inv = 1.0 / pivot
        here = sub == k
        mult = cols[k]

        def step(x):
            row = across_rows(x, k) * inv
            return jnp.where(here, row, x - mult * row)

        if lower:
            scale = jnp.where(here, pivot, scale)
            half = half - jnp.where(sub > k, mult, 0.0) * (across_rows(half, k) * inv)
        out = step(out)
        for j in range(k + 1, R):
            cols[j] = step(cols[j])
    return out, half * lax.rsqrt(scale) if lower else None


def put_rows(matrix, rows, r0):
    parts = [matrix[:r0]] if r0 else []
    parts.append(rows)
    if r0 + rows.shape[0] < matrix.shape[0]:
        parts.append(matrix[r0 + rows.shape[0] :])
    return jnp.concatenate(parts, axis=0)


def invert_tile(m, lower=False):
    lane = lax.broadcasted_iota(jnp.int32, (T, T), 1)
    sub = lax.broadcasted_iota(jnp.int32, (T, T), 0)
    rows = m[:R]
    for c0 in range(0, T, R):
        swept, half = panel(rows, c0, lower)
        if c0 + R < T:
            old = m[c0 + R : c0 + 2 * R]
            inside = (lane[:R] >= c0) & (lane[:R] < c0 + R)
            rows = jnp.where(inside, 0.0, old)
            for k in range(R):
                rows = rows - across_lanes(old, c0 + k) * across_rows(swept, k)
        wide = put_rows(jnp.zeros((T, T), F32), swept, c0)
        rest = jnp.where((lane >= c0) & (lane < c0 + R), 0.0, m) - dot(m, wide)
        if lower:
            rest = jnp.where(sub < c0, m, rest)
        m = put_rows(rest, half if lower else swept, c0)
    return jnp.where(lane > sub, 0.0, m) if lower else m


def sweep(ref, start, stop):
    n = ref.shape[0]
    for p in range(start, stop, T):
        pivot = invert_tile(ref[p : p + T, p : p + T])
        rows = dot(pivot, ref[p : p + T, :])
        parts = ([rows[:, :p]] if p else []) + [pivot]
        if p + T < n:
            parts.append(rows[:, p + T :])
        rows = jnp.concatenate(parts, axis=1)
        for q in range(0, n, T):
            if q != p:
                change = dot(ref[q : q + T, p : p + T], rows)
                ref[q : q + T, p : p + T] = jnp.zeros((T, T), F32)
                ref[q : q + T, :] = ref[q : q + T, :] - change
        ref[p : p + T, :] = rows


def inverse_factor(ref):
    n = ref.shape[0]
    for p in range(0, n, T):
        pivot = invert_tile(ref[p : p + T, p : p + T], lower=True)
        scaled = dot(pivot, ref[p : p + T, :])
        for q in range(p + T, n, T):
            weight = scaled[:, q : q + T]
            ref[q : q + T, :] = ref[q : q + T, :] - dot(weight, scaled, TN)
            ref[q : q + T, p : p + T] = -dot(weight, pivot, TN)
        for q in range(0, n, T):
            if q < p:
                ref[p : p + T, q : q + T] = scaled[:, q : q + T]
            else:
                ref[p : p + T, q : q + T] = pivot if q == p else jnp.zeros((T, T), F32)


def leaf_block(leaf, side_r, side_c, r, c, size):
    e = leaf.shape[1] // 4
    return leaf.at[
        0,
        pl.ds(pl.multiple_of(side_r * e + r * size, T), size),
        pl.ds(pl.multiple_of(side_c * e + c * size, T), size),
    ]


def run_copies(pairs, sem):
    copies = [pltpu.make_async_copy(a, b, sem.at[i]) for i, (a, b) in enumerate(pairs)]
    for copy in copies:
        copy.start()
    for copy in copies:
        copy.wait()


def sides(place):
    v, u = place[0], place[1]
    return [v, 2 + u], [1 - v, 3 - u]


def unpack(ref, at, tiles):
    held = {}
    for r, c in upper(tiles):
        held[r, c] = ref[at : at + T, :]
        if c > r:
            held[c, r] = held[r, c].T
        at += T
    return jnp.concatenate(
        [jnp.concatenate([held[r, c] for c in range(tiles)], axis=1) for r in range(tiles)], axis=0
    )


def call(kernel, name, cost, outs, ins, scratch, **more):
    return pl.pallas_call(
        kernel,
        out_shape=[jax.ShapeDtypeStruct(shape, dtype) for shape, dtype in outs],
        in_specs=[spec for spec, _ in ins],
        out_specs=more.pop("out_specs", [VMEM] * len(outs)),
        scratch_shapes=scratch,
        compiler_params=PARAMS,
        cost_estimate=pl.CostEstimate(flops=cost, bytes_accessed=cost, transcendentals=0),
        name=name,
        **more,
    )(*[value for _, value in ins])


def block_tiles(leaf, side_r, side_c, at):
    tiles = leaf.shape[1] // 4 // T
    return leaf_block(leaf, side_r, side_c, at // tiles, at % tiles, T)


def cut_first_kernel(place, leaf, a, sem):
    tiles = leaf.shape[1] // 4 // T
    ext, inn = sides(place)
    n_sym = len(upper(tiles))
    pairs = []
    for at, (r, c) in enumerate(upper(tiles)):
        pairs.append((leaf_block(leaf, inn[0], inn[0], r, c, T), a.at[pl.ds(at * T, T)]))
    for at in range(FIRST):
        pairs.append(
            (block_tiles(leaf, ext[0], inn[0], at), a.at[pl.ds((n_sym + at) * T, T)])
        )
    run_copies(pairs, sem)


def cut_first(place, leaf):
    n_sym = len(upper(leaf.shape[1] // 4 // T))
    return call(
        cut_first_kernel,
        "cut_first",
        1000 * 10**6,
        [(((n_sym + FIRST) * T, T), F32)],
        [(SMEM, place), (FAR, leaf)],
        [pltpu.SemaphoreType.DMA((n_sym + FIRST,))],
    )[0]


def cut_side_kernel(place, leaf, hh, sem):
    tiles = leaf.shape[1] // 4 // T
    _, inn = sides(place)
    pairs = []
    for at, (r, c) in enumerate(upper(tiles)):
        pairs.append((leaf_block(leaf, inn[1], inn[1], r, c, T), hh.at[pl.ds(at * T, T)]))
    run_copies(pairs, sem)


def cut_side(place, leaf):
    n_sym = len(upper(leaf.shape[1] // 4 // T))
    return call(
        cut_side_kernel,
        "cut_side",
        1000 * 10**6,
        [((n_sym * T, T), F32)],
        [(SMEM, place), (FAR, leaf)],
        [pltpu.SemaphoreType.DMA((n_sym,))],
    )[0]


def cut_second_kernel(place, leaf, swap, outer0, b, c, sem):
    e = leaf.shape[1] // 4
    tiles = e // T
    ext, inn = sides(place)
    n_sym = len(upper(tiles))
    pairs = [
        (leaf_block(leaf, inn[0], inn[1], 0, 0, e), b),
        (leaf_block(leaf, ext[0], inn[0], 0, 0, e), c.at[pl.ds(0, e)]),
        (leaf_block(leaf, ext[1], inn[0], 0, 0, e), c.at[pl.ds(e, e)]),
        (leaf_block(leaf, ext[0], inn[1], 0, 0, e), c.at[pl.ds(2 * e, e)]),
        (leaf_block(leaf, ext[1], inn[1], 0, 0, e), c.at[pl.ds(3 * e, e)]),
    ]
    for at, (r, k) in enumerate(upper(tiles)):
        pairs.append((leaf_block(leaf, inn[0], inn[0], r, k, T), swap.at[pl.ds(at * T, T)]))
    half = outer0.shape[0] // T
    second = []
    for at, (r, k) in enumerate(upper(2 * tiles)):
        source = leaf_block(leaf, ext[r // tiles], ext[k // tiles], r % tiles, k % tiles, T)
        if at < half:
            pairs.append((source, outer0.at[pl.ds(at * T, T)]))
        else:
            second.append((source, swap.at[pl.ds((n_sym + at - half) * T, T)]))
    run_copies(pairs, sem)
    same = place[0] == place[1]

    @pl.when(same)
    def _():
        cross = [
            (block_tiles(leaf, ext[0], inn[0], at), swap.at[pl.ds((n_sym + at) * T, T)])
            for at in range(FIRST)
        ]
        run_copies(cross, sem)

    @pl.when(jnp.logical_not(same))
    def _():
        run_copies(second, sem)


def cut_second(place, leaf):
    e = leaf.shape[1] // 4
    n_sym = len(upper(e // T))
    half = len(upper(2 * (e // T))) // 2
    return call(
        cut_second_kernel,
        "cut_second",
        1000 * 10**6,
        [(((n_sym + half) * T, T), F32), ((half * T, T), F32), ((e, e), F32), ((4 * e, e), F32)],
        [(SMEM, place), (HBM, leaf)],
        [pltpu.SemaphoreType.DMA((n_sym + half + 5,))],
    )


def gauge_kernel(mine, along, b, b_out, factor):
    e = factor.shape[0]
    tiles = e // T
    factor[...] = unpack(mine, 0, tiles) + unpack(along, 0, tiles)
    inverse_factor(factor)
    b_out[...] = dot(b[...], factor[...], NT)


def gauge(mine, along, b):
    e = b.shape[0]
    return call(
        gauge_kernel,
        "gauge_side",
        8000 * 10**6,
        [((e, e), F32), ((e, e), F32)],
        [(VMEM, x) for x in (mine, along, b)],
        [],
    )


def scale_kernel(factor, c, c1, c2):
    e = factor.shape[0]
    tiles = e // T
    scaled = dot3(split(c[2 * e :, :]), split(factor[...]), NT)
    for at in range(FIRST, 4 * tiles * tiles):
        r, k = at // tiles * T, at % tiles * T
        tile = c[r : r + T, k : k + T] if r < 2 * e else scaled[r - 2 * e : r - 2 * e + T, k : k + T]
        spot = (at - FIRST) * T
        ref, spot = (c1, spot) if spot < c1.shape[0] else (c2, spot - c1.shape[0])
        ref[spot : spot + T, :] = tile


def scale_cross(factor, c, last):
    e = factor.shape[0]
    return call(
        scale_kernel,
        "scale_cross",
        2000 * 10**6,
        [((4 * e * e // T - FIRST * T - last, T), F32), ((last, T), F32)],
        [(VMEM, x) for x in (factor, c)],
        [],
    )


def couple(b):
    mine, across, along, corner = (ref[...] for ref in b)
    return jnp.concatenate(
        [jnp.concatenate([mine, across], axis=1), jnp.concatenate([along, corner], axis=1)], axis=0
    )


def factor_start_kernel(a0, a1, a2, a3, b0, b1, b2, b3, side):
    e = b0.shape[0]
    tiles = e // T
    coup = couple((b0, b1, b2, b3))
    side[...] = -dot(coup, coup, NT)
    side[:e, :e] = side[:e, :e] + (unpack(a0, 0, tiles) + unpack(a1, 0, tiles))
    side[e:, e:] = side[e:, e:] + (unpack(a2, 0, tiles) + unpack(a3, 0, tiles))
    sweep(side, 0, e)


def factor_start(a, b):
    e = b[0].shape[0]
    return call(
        factor_start_kernel,
        "factor_start",
        10000 * 10**6,
        [((2 * e, 2 * e), F32)],
        [(VMEM, x) for x in (*a, *b)],
        [],
    )[0]


def factor_end_kernel(place, side_in, b0, b1, b2, b3, high, low, side, full):
    e = b0.shape[0]
    side[...] = side_in[...]
    sweep(side, e, 2 * e)
    coup = split(couple((b0, b1, b2, b3)))
    away = dot3(split(side[...]), coup)
    shape = full.shape
    unit = lax.broadcasted_iota(jnp.int32, shape, 0) == lax.broadcasted_iota(jnp.int32, shape, 1)
    full[...] = dot3(coup, split(away), TN) + unit.astype(F32)

    def emit(value, rows, columns):
        high[rows, columns], low[rows, columns] = split(value)

    first, rest = slice(0, e), slice(e, 3 * e)
    emit(full[...], rest, rest)
    emit(-away[:e, :], first, rest)
    same = place[0] == place[1]

    @pl.when(same)
    def _():
        emit(side[:e, :e], first, first)
        emit(-away[:e, :].T, rest, first)

    @pl.when(jnp.logical_not(same))
    def _():
        emit(side[:e, e:], first, first)
        emit(-away[e:, :].T, rest, first)


def factor_end(place, side, b):
    e = b[0].shape[0]
    return call(
        factor_end_kernel,
        "factor_end",
        10000 * 10**6,
        [((3 * e, 3 * e), BF16)] * 2,
        [(SMEM, place), (VMEM, side)] + [(VMEM, x) for x in b],
        [pltpu.VMEM((2 * e, 2 * e), F32), pltpu.VMEM((2 * e, 2 * e), F32)],
    )


def cross_block(first, c1, c2):
    n1, n2 = c1.shape[0] // T, c2.shape[0] // T
    tiles = math.isqrt((FIRST + n1 + n2) // 4)
    n_sym = len(upper(tiles))
    held = [first[(n_sym + at) * T : (n_sym + at + 1) * T, :] for at in range(FIRST)]
    held += [ref[at * T : (at + 1) * T, :] for ref, n in ((c1, n1), (c2, n2)) for at in range(n)]
    rows = []
    for r in range(2 * tiles):
        side = r // tiles
        row = [held[((side + 2 * c) * tiles + r % tiles) * tiles + k] for c in range(2) for k in range(tiles)]
        rows.append(jnp.concatenate(row, axis=1))
    return jnp.concatenate(rows, axis=0)


def times_inverse(cross, high, low, inner):
    e = cross.shape[1] // 2
    return dot3(split(cross[:, :e]), (high[:e], low[:e])) + dot3(
        split(cross[:, e:]), (high[inner], low[inner])
    )


def rows_kernel(
    place, leaf, high, low, a0, c01, c02, swapped, c21, c22, top, bottom, block, col, own, sem
):
    e = leaf.shape[1] // 4
    ext, _ = sides(place)
    copies = []
    for r in range(2):
        for c in range(2):
            target = own.at[pl.ds(r * e, e), pl.ds(c * e, e)]
            source = leaf_block(leaf, ext[r], ext[c], 0, 0, e)
            copies.append(pltpu.make_async_copy(source, target, sem.at[2 * r + c]))
            copies[-1].start()
    same = place[0] == place[1]
    mine = cross_block(a0, c01, c02)

    @pl.when(same)
    def _():
        col[...] = mine

    @pl.when(jnp.logical_not(same))
    def _():
        col[...] = cross_block(swapped, c21, c22)

    left = split(times_inverse(mine, high[...], low[...], slice(e, 2 * e)))
    top[...], bottom[...] = left
    left = [x[:, : 2 * e] for x in left]
    block[...] = -dot3(left, split(col[...]), NT)
    for copy in copies:
        copy.wait()

    @pl.when(same)
    def _():
        block[...] = block[...] + own[...]


def own_rows(place, leaf, high, low, a0, c01, c02, swapped, c21, c22):
    e = leaf.shape[1] // 4
    return call(
        rows_kernel,
        "own_rows",
        500 * 10**6,
        [((2 * e, 3 * e), BF16)] * 2 + [((2 * e, 2 * e), F32)],
        [(SMEM, place), (HBM, leaf)]
        + [(VMEM, x) for x in (high, low, a0, c01, c02, swapped, c21, c22)],
        [
            pltpu.VMEM((2 * e, 2 * e), F32),
            pltpu.VMEM((2 * e, 2 * e), F32),
            pltpu.SemaphoreType.DMA((4,)),
        ],
    )


def spot(place, e, side, which):
    x = place[0] if which == 0 else 1 - place[0]
    return pl.ds(pl.multiple_of((2 * side + x) * e, T), e)


def write(out, place, value, a, b):
    e = out.shape[1] // 4
    for r in range(2):
        for c in range(2):
            out[0, spot(place, e, r, a), spot(place, e, c, b)] = value[
                r * e : (r + 1) * e, c * e : (c + 1) * e
            ]


def pick(ref, rows, b):
    e = ref.shape[1] // 3
    return jnp.concatenate([ref[rows, :e], ref[rows, (1 + b) * e : (2 + b) * e]], axis=1)


def products_kernel(
    place, high, low, top, bottom, block, a0, c01, c02, a1, c11, c12, a3, c31, c32, out, part, scratch
):
    e = out.shape[1] // 4
    same = place[0] == place[1]
    write(out, place, block[...], 0, 0)
    everything = slice(0, 2 * e)

    @pl.when(same)
    def _():
        across = cross_block(a1, c11, c12)
        right = split(across)
        left = [pick(x, everything, 1) for x in (top, bottom)]
        write(out, place, -dot3(left, right, NT), 0, 1)
        scratch[...] = times_inverse(across, high[...], low[...], slice(2 * e, 3 * e))
        left = split(pick(scratch, everything, 0))
        write(out, place, -dot3(left, split(cross_block(a0, c01, c02)), NT), 1, 0)
        left = split(pick(scratch, everything, 1))
        part[:, : 2 * e] = -dot3(left, right, NT)

    @pl.when(jnp.logical_not(same))
    def _():
        right = split(cross_block(a3, c31, c32))
        left = [pick(x, everything, 1) for x in (top, bottom)]
        write(out, place, -dot3(left, right, NT), 0, 1)
        across = cross_block(a1, c11, jnp.zeros_like(c12))
        part[...] = times_inverse(across, high[...], low[...], slice(2 * e, 3 * e))


def products(place, high, low, top, bottom, block, mine, across, corner):
    e = block.shape[0] // 2
    return call(
        products_kernel,
        "products",
        500 * 10**6,
        [((1, 4 * e, 4 * e), F32), ((2 * e, 3 * e), F32)],
        [(SMEM, place)]
        + [(VMEM, x) for x in (high, low, top, bottom, block, *mine, *across, *corner)],
        [pltpu.VMEM((2 * e, 3 * e), F32)],
    )


def finish_kernel(
    place, before, high, low, part, passed, last, c11, swapped, c21, c22, a3, c31, out, held, scratch, sem
):
    e = out.shape[1] // 4
    tiles = e // T
    n_sym = len(upper(tiles))

    def targets(b):
        return [
            (
                held.at[pl.ds(r * e, e), pl.ds((2 * b + c) * e, e)],
                out.at[0, spot(place, e, r, 1), spot(place, e, c, b)],
            )
            for r in range(2)
            for c in range(2)
        ]

    @pl.when(place[0] == place[1])
    def _():
        half = last.shape[0]
        for at, (i, j) in enumerate(upper(2 * tiles)):
            ref, at = (last, at * T) if at * T < half else (passed, at * T - half)
            piece = ref[at : at + T, :]
            r, c = slice(i * T, (i + 1) * T), slice(j * T, (j + 1) * T)
            shift = 2 * e
            held[r, j * T + shift : (j + 1) * T + shift] = part[r, c] + piece
            if i != j:
                held[c, i * T + shift : (i + 1) * T + shift] = part[c, r] + piece.T
        run_copies(targets(1), sem)

    @pl.when(place[0] != place[1])
    def _():
        nothing = jnp.zeros(((n_sym + FIRST) * T, T), F32)
        late = cross_block(nothing, jnp.zeros_like(c11), last)[:, e:]
        inner = slice(2 * e, 3 * e)
        start = (2 * tiles * tiles - last.shape[0] // T) // tiles * T
        scratch[:start, :] = part[:start, :]
        scratch[start:, :] = part[start:, :] + dot3(split(late[start:]), (high[inner], low[inner]))
        everything = slice(0, 2 * e)
        copies = []
        for b in range(2):
            col = cross_block(swapped, c21, c22) if b == 0 else cross_block(a3, c31, passed)
            left = split(pick(scratch, everything, b))
            held[:, 2 * e * b : 2 * e * (b + 1)] = -dot3(left, split(col), NT)
            for i, (source, target) in enumerate(targets(b)):
                copies.append(pltpu.make_async_copy(source, target, sem.at[4 * b + i]))
                copies[-1].start()
        for copy in copies:
            copy.wait()


def finish(place, before, high, low, part, passed, last, c11, swapped, c21, c22, a3, c31):
    e = before.shape[1] // 4
    return call(
        finish_kernel,
        "finish",
        500 * 10**6,
        [(before.shape, F32)],
        [(SMEM, place), (HBM, before)]
        + [
            (VMEM, x)
            for x in (high, low, part, passed, last, c11, swapped, c21, c22, a3, c31)
        ],
        [
            pltpu.VMEM((2 * e, 4 * e), F32),
            pltpu.VMEM((2 * e, 3 * e), F32),
            pltpu.SemaphoreType.DMA((8,)),
        ],
        out_specs=[HBM],
        input_output_aliases={1: 0},
    )[0]


def tie(*values):
    return lax.optimization_barrier(values)


def solution(mesh):
    nx, ny = mesh.shape["gx"], mesh.shape["gy"]
    devices = [(x, y) for x in range(nx) for y in range(ny)]

    def is_same(x, y):
        return x // (nx // 2) == y // (ny // 2)

    def send(value, along_y, only=None):
        pairs = []
        for x, y in devices:
            if only is None or is_same(x, y) == only:
                to = (x, (y + ny // 2) % ny) if along_y else ((x + nx // 2) % nx, y)
                pairs.append((x * ny + y, to[0] * ny + to[1]))
        return lax.ppermute(value, ("gx", "gy"), pairs)

    def body(leaf):
        e = leaf.shape[1] // 4
        v = lax.axis_index("gx") // (nx // 2)
        u = lax.axis_index("gy") // (ny // 2)
        place = jnp.stack([v, u]).astype(jnp.int32)
        same = u == v
        a = cut_first(place, leaf)
        a_x = send(a, False)
        here, a = tie(place, a)
        hh = cut_side(here, leaf)
        hh_y = send(hh, True)
        swap, outer0, b, c = cut_second(place, leaf)
        swapped = send(swap, True)
        b, factor = gauge(hh, hh_y, b)
        b_x = send(b, False)
        c1, c2 = scale_cross(factor, c, outer0.shape[0])
        b, a_x, c1, swapped = tie(b, a_x, c1, swapped)
        b_y = send(b, True)
        a_d = send(a_x, True)
        a_d, b_x, b_y = tie(a_d, b_x, b_y)
        b_d = send(b_x, True)
        c1, b_x = tie(c1, b_x)
        c1_x = send(c1, False)
        c1, c2, b_d = tie(c1, c2, b_d)
        c1_y = send(c1, True, only=True)
        c2_y = send(c2, True, only=True)
        side = factor_start((a, a_x, swapped, a_d), (b, b_x, b_y, b_d))
        third, side = tie(jnp.where(same, swapped[-outer0.shape[0] :], c2), side)
        third = send(third, False)
        high, low = factor_end(place, side, (b, b_x, b_y, b_d))
        c1_x, high = tie(c1_x, high)
        c1_d = send(c1_x, True, only=True)
        top, bottom, block = own_rows(place, leaf, high, low, a, c1, c2, swapped, c1_y, c2_y)
        last, third, block = tie(jnp.where(same, c2, outer0), third, block)
        last = send(last, False)
        passed = send(third, True)
        out, part = products(
            place, high, low, top, bottom, block, (a, c1, c2), (a_x, c1_x, third), (a_d, c1_d, passed)
        )
        return finish(
            place, out, high, low, part, passed, last, c1_x, swapped, c1_y, c2_y, a_d, c1_d
        )

    return jax.shard_map(
        body,
        mesh=mesh,
        in_specs=(P(None, "gy", "gx"),),
        out_specs=P(None, "gy", "gx"),
        check_vma=False,
    )
```

```python
import math

import jax
import jax.numpy as jnp
from jax import lax
from jax.experimental import pallas as pl
from jax.experimental.pallas import tpu as pltpu
from jax.sharding import PartitionSpec as P

F32 = jnp.float32
BF16 = jnp.bfloat16
T = 128
R = 16
FIRST = 1
SECOND = 8
HBM = pl.BlockSpec(memory_space=pl.ANY)
FAR = pl.BlockSpec(memory_space=pltpu.HBM)
VMEM = pl.BlockSpec(memory_space=pltpu.VMEM)
SMEM = pl.BlockSpec(memory_space=pltpu.SMEM)
PARAMS = pltpu.CompilerParams(vmem_limit_bytes=32 * 2**20)


def dot(a, b, dims=((1,), (0,))):
    return lax.dot_general(
        a, b, (dims, ((), ())), precision=lax.Precision.HIGHEST, preferred_element_type=F32
    )


def dot16(a, b, dims=((1,), (0,))):
    return lax.dot_general(a, b, (dims, ((), ())), preferred_element_type=F32)


def split(a):
    high = a.astype(BF16)
    return high, (a - high.astype(F32)).astype(BF16)


def dot3(a, b, dims=((1,), (0,))):
    return dot16(a[0], b[0], dims) + (dot16(a[0], b[1], dims) + dot16(a[1], b[0], dims))


NT = ((1,), (1,))
TN = ((0,), (0,))


def upper(n):
    return [(i, j) for i in range(n) for j in range(i, n)]


def across_lanes(x, k):
    return jnp.broadcast_to(x[:, k : k + 1], x.shape)


def across_rows(x, k):
    return jnp.broadcast_to(x[k : k + 1, :], x.shape)


def panel(rows, c0, lower):
    sub = lax.broadcasted_iota(jnp.int32, rows.shape, 0)
    lane = lax.broadcasted_iota(jnp.int32, rows.shape, 1)
    cols = [across_lanes(rows, c0 + k) for k in range(R)]
    out = jnp.where((lane >= c0) & (lane < c0 + R), (lane - c0 == sub).astype(F32), rows)
    half = out
    scale = jnp.ones_like(rows)
    for k in range(R):
        pivot = across_rows(cols[k], k)
        inv = 1.0 / pivot
        here = sub == k
        mult = cols[k]

        def step(x):
            row = across_rows(x, k) * inv
            return jnp.where(here, row, x - mult * row)

        if lower:
            scale = jnp.where(here, pivot, scale)
            half = half - jnp.where(sub > k, mult, 0.0) * (across_rows(half, k) * inv)
        out = step(out)
        for j in range(k + 1, R):
            cols[j] = step(cols[j])
    return out, half * lax.rsqrt(scale) if lower else None


def put_rows(matrix, rows, r0):
    parts = [matrix[:r0]] if r0 else []
    parts.append(rows)
    if r0 + rows.shape[0] < matrix.shape[0]:
        parts.append(matrix[r0 + rows.shape[0] :])
    return jnp.concatenate(parts, axis=0)


def invert_tile(m, lower=False):
    lane = lax.broadcasted_iota(jnp.int32, (T, T), 1)
    sub = lax.broadcasted_iota(jnp.int32, (T, T), 0)
    rows = m[:R]
    for c0 in range(0, T, R):
        swept, half = panel(rows, c0, lower)
        if c0 + R < T:
            old = m[c0 + R : c0 + 2 * R]
            inside = (lane[:R] >= c0) & (lane[:R] < c0 + R)
            rows = jnp.where(inside, 0.0, old)
            for k in range(R):
                rows = rows - across_lanes(old, c0 + k) * across_rows(swept, k)
        wide = put_rows(jnp.zeros((T, T), F32), swept, c0)
        rest = jnp.where((lane >= c0) & (lane < c0 + R), 0.0, m) - dot(m, wide)
        if lower:
            rest = jnp.where(sub < c0, m, rest)
        m = put_rows(rest, half if lower else swept, c0)
    return jnp.where(lane > sub, 0.0, m) if lower else m


def sweep(ref, start, stop):
    n = ref.shape[0]
    for p in range(start, stop, T):
        pivot = invert_tile(ref[p : p + T, p : p + T])
        rows = dot(pivot, ref[p : p + T, :])
        parts = ([rows[:, :p]] if p else []) + [pivot]
        if p + T < n:
            parts.append(rows[:, p + T :])
        rows = jnp.concatenate(parts, axis=1)
        for q in range(0, n, T):
            if q != p:
                change = dot(ref[q : q + T, p : p + T], rows)
                ref[q : q + T, p : p + T] = jnp.zeros((T, T), F32)
                ref[q : q + T, :] = ref[q : q + T, :] - change
        ref[p : p + T, :] = rows


def inverse_factor(ref):
    n = ref.shape[0]
    for p in range(0, n, T):
        pivot = invert_tile(ref[p : p + T, p : p + T], lower=True)
        scaled = dot(pivot, ref[p : p + T, :])
        for q in range(p + T, n, T):
            weight = scaled[:, q : q + T]
            ref[q : q + T, :] = ref[q : q + T, :] - dot(weight, scaled, TN)
            ref[q : q + T, p : p + T] = -dot(weight, pivot, TN)
        for q in range(0, n, T):
            if q < p:
                ref[p : p + T, q : q + T] = scaled[:, q : q + T]
            else:
                ref[p : p + T, q : q + T] = pivot if q == p else jnp.zeros((T, T), F32)


def leaf_block(leaf, side_r, side_c, r, c, size):
    e = leaf.shape[1] // 4
    return leaf.at[
        0,
        pl.ds(pl.multiple_of(side_r * e + r * size, T), size),
        pl.ds(pl.multiple_of(side_c * e + c * size, T), size),
    ]


def run_copies(pairs, sem):
    copies = [pltpu.make_async_copy(a, b, sem.at[i]) for i, (a, b) in enumerate(pairs)]
    for copy in copies:
        copy.start()
    for copy in copies:
        copy.wait()


def sides(place):
    v, u = place[0], place[1]
    return [v, 2 + u], [1 - v, 3 - u]


def unpack(ref, at, tiles):
    held = {}
    for r, c in upper(tiles):
        held[r, c] = ref[at : at + T, :]
        if c > r:
            held[c, r] = held[r, c].T
        at += T
    return jnp.concatenate(
        [jnp.concatenate([held[r, c] for c in range(tiles)], axis=1) for r in range(tiles)], axis=0
    )


def call(kernel, name, cost, outs, ins, scratch, **more):
    return pl.pallas_call(
        kernel,
        out_shape=[jax.ShapeDtypeStruct(shape, dtype) for shape, dtype in outs],
        in_specs=[spec for spec, _ in ins],
        out_specs=more.pop("out_specs", [VMEM] * len(outs)),
        scratch_shapes=scratch,
        compiler_params=PARAMS,
        cost_estimate=pl.CostEstimate(flops=cost, bytes_accessed=cost, transcendentals=0),
        name=name,
        **more,
    )(*[value for _, value in ins])


def block_tiles(leaf, side_r, side_c, at):
    tiles = leaf.shape[1] // 4 // T
    return leaf_block(leaf, side_r, side_c, at // tiles, at % tiles, T)


def cross_tile(leaf, ext, inn, at):
    n = (leaf.shape[1] // 4 // T) ** 2
    return block_tiles(leaf, ext[at // n % 2], inn[at // n // 2], at % n)


def cut_first_kernel(place, leaf, a, sem):
    tiles = leaf.shape[1] // 4 // T
    ext, inn = sides(place)
    n_sym = len(upper(tiles))
    pairs = []
    for at, (r, c) in enumerate(upper(tiles)):
        pairs.append((leaf_block(leaf, inn[0], inn[0], r, c, T), a.at[pl.ds(at * T, T)]))
    for at in range(FIRST):
        pairs.append(
            (cross_tile(leaf, ext, inn, at), a.at[pl.ds((n_sym + at) * T, T)])
        )
    run_copies(pairs, sem)


def cut_first(place, leaf):
    n_sym = len(upper(leaf.shape[1] // 4 // T))
    return call(
        cut_first_kernel,
        "cut_first",
        1000 * 10**6,
        [(((n_sym + FIRST) * T, T), F32)],
        [(SMEM, place), (FAR, leaf)],
        [pltpu.SemaphoreType.DMA((n_sym + FIRST,))],
    )[0]


def cut_side_kernel(place, leaf, hh, sem):
    tiles = leaf.shape[1] // 4 // T
    _, inn = sides(place)
    pairs = []
    for at, (r, c) in enumerate(upper(tiles)):
        pairs.append((leaf_block(leaf, inn[1], inn[1], r, c, T), hh.at[pl.ds(at * T, T)]))
    run_copies(pairs, sem)


def cut_side(place, leaf):
    n_sym = len(upper(leaf.shape[1] // 4 // T))
    return call(
        cut_side_kernel,
        "cut_side",
        1000 * 10**6,
        [((n_sym * T, T), F32)],
        [(SMEM, place), (FAR, leaf)],
        [pltpu.SemaphoreType.DMA((n_sym,))],
    )[0]


def cut_second_kernel(place, leaf, swap, outer0, b, c, sem):
    e = leaf.shape[1] // 4
    tiles = e // T
    ext, inn = sides(place)
    n_sym = len(upper(tiles))
    pairs = [
        (leaf_block(leaf, inn[0], inn[1], 0, 0, e), b),
        (leaf_block(leaf, ext[0], inn[0], 0, 0, e), c.at[pl.ds(0, e)]),
        (leaf_block(leaf, ext[1], inn[0], 0, 0, e), c.at[pl.ds(e, e)]),
        (leaf_block(leaf, ext[0], inn[1], 0, 0, e), c.at[pl.ds(2 * e, e)]),
        (leaf_block(leaf, ext[1], inn[1], 0, 0, e), c.at[pl.ds(3 * e, e)]),
    ]
    for at, (r, k) in enumerate(upper(tiles)):
        pairs.append((leaf_block(leaf, inn[0], inn[0], r, k, T), swap.at[pl.ds(at * T, T)]))
    half = outer0.shape[0] // T
    second = []
    for at, (r, k) in enumerate(upper(2 * tiles)):
        source = leaf_block(leaf, ext[r // tiles], ext[k // tiles], r % tiles, k % tiles, T)
        if at < half:
            pairs.append((source, outer0.at[pl.ds(at * T, T)]))
        else:
            second.append((source, swap.at[pl.ds((n_sym + at - half) * T, T)]))
    run_copies(pairs, sem)
    same = place[0] == place[1]

    @pl.when(same)
    def _():
        cross = [
            (cross_tile(leaf, ext, inn, at), swap.at[pl.ds((n_sym + at) * T, T)])
            for at in range(half)
        ]
        run_copies(cross, sem)

    @pl.when(jnp.logical_not(same))
    def _():
        run_copies(second, sem)


def cut_second(place, leaf):
    e = leaf.shape[1] // 4
    n_sym = len(upper(e // T))
    half = len(upper(2 * (e // T))) // 2
    return call(
        cut_second_kernel,
        "cut_second",
        1000 * 10**6,
        [(((n_sym + half) * T, T), F32), ((half * T, T), F32), ((e, e), F32), ((4 * e, e), F32)],
        [(SMEM, place), (HBM, leaf)],
        [pltpu.SemaphoreType.DMA((n_sym + half + 5,))],
    )


def gauge_kernel(mine, along, b, b_out, factor):
    e = factor.shape[0]
    tiles = e // T
    factor[...] = unpack(mine, 0, tiles) + unpack(along, 0, tiles)
    inverse_factor(factor)
    b_out[...] = dot(b[...], factor[...], NT)


def gauge(mine, along, b):
    e = b.shape[0]
    return call(
        gauge_kernel,
        "gauge_side",
        8000 * 10**6,
        [((e, e), F32), ((e, e), F32)],
        [(VMEM, x) for x in (mine, along, b)],
        [],
    )


def scale_kernel(factor, c, c1, c2, rest):
    e = factor.shape[0]
    tiles = e // T
    scaled = dot3(split(c[2 * e :, :]), split(factor[...]), NT)
    total = 4 * tiles * tiles
    for at in range(FIRST, total):
        r, k = at // tiles * T, at % tiles * T
        tile = c[r : r + T, k : k + T] if r < 2 * e else scaled[r - 2 * e : r - 2 * e + T, k : k + T]
        if at < FIRST + SECOND:
            c1[(at - FIRST) * T : (at - FIRST + 1) * T, :] = tile
        else:
            c2[(at - FIRST - SECOND) * T : (at - FIRST - SECOND + 1) * T, :] = tile
        spot = at * T - (total * T - rest.shape[0])
        if spot >= 0:
            rest[spot : spot + T, :] = tile


def scale_cross(factor, c, swapped):
    e = factor.shape[0]
    total = 4 * e * e // T
    return call(
        scale_kernel,
        "scale_cross",
        2000 * 10**6,
        [((n, T), F32) for n in (SECOND * T, total - (FIRST + SECOND) * T, total - swapped * T)],
        [(VMEM, x) for x in (factor, c)],
        [],
    )


def couple(b):
    mine, across, along, corner = (ref[...] for ref in b)
    return jnp.concatenate(
        [jnp.concatenate([mine, across], axis=1), jnp.concatenate([along, corner], axis=1)], axis=0
    )


def factor_start_kernel(a0, a1, a2, a3, b0, b1, b2, b3, side):
    e = b0.shape[0]
    tiles = e // T
    coup = couple((b0, b1, b2, b3))
    side[...] = -dot(coup, coup, NT)
    side[:e, :e] = side[:e, :e] + (unpack(a0, 0, tiles) + unpack(a1, 0, tiles))
    side[e:, e:] = side[e:, e:] + (unpack(a2, 0, tiles) + unpack(a3, 0, tiles))
    sweep(side, 0, e)


def factor_start(a, b):
    e = b[0].shape[0]
    return call(
        factor_start_kernel,
        "factor_start",
        1000 * 10**6,
        [((2 * e, 2 * e), F32)],
        [(VMEM, x) for x in (*a, *b)],
        [],
    )[0]


def factor_end_kernel(place, side_in, b0, b1, b2, b3, high, low, side, full):
    e = b0.shape[0]
    side[...] = side_in[...]
    sweep(side, e, 2 * e)
    coup = split(couple((b0, b1, b2, b3)))
    away = dot3(split(side[...]), coup)
    shape = full.shape
    unit = lax.broadcasted_iota(jnp.int32, shape, 0) == lax.broadcasted_iota(jnp.int32, shape, 1)
    full[...] = dot3(coup, split(away), TN) + unit.astype(F32)

    def emit(value, rows, columns):
        high[rows, columns], low[rows, columns] = split(value)

    first, rest = slice(0, e), slice(e, 3 * e)
    emit(full[...], rest, rest)
    emit(-away[:e, :], first, rest)
    same = place[0] == place[1]

    @pl.when(same)
    def _():
        emit(side[:e, :e], first, first)
        emit(-away[:e, :].T, rest, first)

    @pl.when(jnp.logical_not(same))
    def _():
        emit(side[:e, e:], first, first)
        emit(-away[e:, :].T, rest, first)


def factor_end(place, side, b):
    e = b[0].shape[0]
    return call(
        factor_end_kernel,
        "factor_end",
        10000 * 10**6,
        [((3 * e, 3 * e), BF16)] * 2,
        [(SMEM, place), (VMEM, side)] + [(VMEM, x) for x in b],
        [pltpu.VMEM((2 * e, 2 * e), F32), pltpu.VMEM((2 * e, 2 * e), F32)],
    )


def cross_block(*pieces):
    held = []
    for ref, skip in pieces:
        for at in range(skip * T, ref.shape[0], T):
            held.append(ref[at : at + T, :])
    tiles = math.isqrt(len(held) // 4)
    rows = []
    for r in range(2 * tiles):
        side = r // tiles
        row = [held[((side + 2 * c) * tiles + r % tiles) * tiles + k] for c in range(2) for k in range(tiles)]
        rows.append(jnp.concatenate(row, axis=1))
    return jnp.concatenate(rows, axis=0)


def symmetric_tiles(e):
    return len(upper(e // T))


def zeros(tiles):
    return jnp.zeros((tiles * T, T), F32), 0


def times_inverse(cross, high, low, inner):
    e = cross.shape[1] // 2
    return dot3(split(cross[:, :e]), (high[:e], low[:e])) + dot3(
        split(cross[:, e:]), (high[inner], low[inner])
    )


def rows_kernel(
    place, leaf, high, low, a0, c01, c02, a1, c11, swapped, rest, top, bottom, block, part, col, own, sem
):
    e = leaf.shape[1] // 4
    n_sym = symmetric_tiles(e)
    ext, _ = sides(place)
    copies = []
    for r in range(2):
        for c in range(2):
            target = own.at[pl.ds(r * e, e), pl.ds(c * e, e)]
            source = leaf_block(leaf, ext[r], ext[c], 0, 0, e)
            copies.append(pltpu.make_async_copy(source, target, sem.at[2 * r + c]))
            copies[-1].start()
    same = place[0] == place[1]
    mine = cross_block((a0, n_sym), (c01, 0), (c02, 0))

    @pl.when(same)
    def _():
        col[...] = mine

    @pl.when(jnp.logical_not(same))
    def _():
        col[...] = cross_block((swapped, n_sym), (rest, 0))
        across = cross_block((a1, n_sym), (c11, 0), zeros(c02.shape[0] // T))
        part[...] = times_inverse(across, high[...], low[...], slice(2 * e, 3 * e))

    left = split(times_inverse(mine, high[...], low[...], slice(e, 2 * e)))
    top[...], bottom[...] = left
    left = [x[:, : 2 * e] for x in left]
    block[...] = -dot3(left, split(col[...]), NT)
    for copy in copies:
        copy.wait()

    @pl.when(same)
    def _():
        block[...] = block[...] + own[...]


def own_rows(place, leaf, high, low, a0, c01, c02, a1, c11, swapped, rest):
    e = leaf.shape[1] // 4
    return call(
        rows_kernel,
        "own_rows",
        500 * 10**6,
        [((2 * e, 3 * e), BF16)] * 2 + [((2 * e, 2 * e), F32), ((2 * e, 3 * e), F32)],
        [(SMEM, place), (HBM, leaf)]
        + [(VMEM, x) for x in (high, low, a0, c01, c02, a1, c11, swapped, rest)],
        [
            pltpu.VMEM((2 * e, 2 * e), F32),
            pltpu.VMEM((2 * e, 2 * e), F32),
            pltpu.SemaphoreType.DMA((4,)),
        ],
    )


def spot(place, e, side, which):
    x = place[0] if which == 0 else 1 - place[0]
    return pl.ds(pl.multiple_of((2 * side + x) * e, T), e)


def write(out, place, value, a, b):
    e = out.shape[1] // 4
    for r in range(2):
        for c in range(2):
            out[0, spot(place, e, r, a), spot(place, e, c, b)] = value[
                r * e : (r + 1) * e, c * e : (c + 1) * e
            ]


def pick(ref, rows, b):
    e = ref.shape[1] // 3
    return jnp.concatenate([ref[rows, :e], ref[rows, (1 + b) * e : (2 + b) * e]], axis=1)


def products_kernel(
    place, high, low, top, bottom, block, a0, c01, c02, a1, c11, third, a3, c31, passed, out, part, scratch
):
    e = out.shape[1] // 4
    n_sym = symmetric_tiles(e)
    same = place[0] == place[1]
    write(out, place, block[...], 0, 0)
    everything = slice(0, 2 * e)

    @pl.when(same)
    def _():
        across = cross_block((a1, n_sym), (c11, 0), (third, 0))
        right = split(across)
        left = [pick(x, everything, 1) for x in (top, bottom)]
        write(out, place, -dot3(left, right, NT), 0, 1)
        scratch[...] = times_inverse(across, high[...], low[...], slice(2 * e, 3 * e))
        left = split(pick(scratch, everything, 0))
        mine = cross_block((a0, n_sym), (c01, 0), (c02, 0))
        write(out, place, -dot3(left, split(mine), NT), 1, 0)
        left = split(pick(scratch, everything, 1))
        part[...] = -dot3(left, right, NT)

    @pl.when(jnp.logical_not(same))
    def _():
        right = split(cross_block((a3, n_sym), (c31, 0), (passed, 0)))
        left = [pick(x, everything, 1) for x in (top, bottom)]
        write(out, place, -dot3(left, right, NT), 0, 1)


def products(place, high, low, top, bottom, block, mine, across, corner):
    e = block.shape[0] // 2
    return call(
        products_kernel,
        "products",
        500 * 10**6,
        [((1, 4 * e, 4 * e), F32), ((2 * e, 2 * e), F32)],
        [(SMEM, place)]
        + [(VMEM, x) for x in (high, low, top, bottom, block, *mine, *across, *corner)],
        [pltpu.VMEM((2 * e, 3 * e), F32)],
    )


def finish_kernel(
    place, before, high, low, block, part, third, passed, last, swapped, rest, a3, c31, out, held, scratch, sem
):
    e = out.shape[1] // 4
    tiles = e // T
    n_sym = symmetric_tiles(e)

    def targets(b):
        return [
            (
                held.at[pl.ds(r * e, e), pl.ds((2 * b + c) * e, e)],
                out.at[0, spot(place, e, r, 1), spot(place, e, c, b)],
            )
            for r in range(2)
            for c in range(2)
        ]

    n_last = last.shape[0] // T

    @pl.when(place[0] == place[1])
    def _():
        skip = passed.shape[0] // T - n_last
        for at, (i, j) in enumerate(upper(2 * tiles)):
            ref, at = (last, at) if at < n_last else (passed, at - n_last + skip)
            piece = ref[at * T : (at + 1) * T, :]
            r, c = slice(i * T, (i + 1) * T), slice(j * T, (j + 1) * T)
            shift = 2 * e
            held[r, j * T + shift : (j + 1) * T + shift] = block[r, c] + piece
            if i != j:
                held[c, i * T + shift : (i + 1) * T + shift] = block[c, r] + piece.T
        run_copies(targets(1), sem)

    @pl.when(place[0] != place[1])
    def _():
        first = third[: third.shape[0] - n_last * T, :]
        late = cross_block(zeros(FIRST + SECOND), (first, 0), (last, 0))[:, e:]
        inner = slice(2 * e, 3 * e)
        scratch[...] = part[...] + dot3(split(late), (high[inner], low[inner]))
        everything = slice(0, 2 * e)
        copies = []
        for b in range(2):
            if b == 0:
                col = cross_block((swapped, n_sym), (rest, 0))
            else:
                col = cross_block((a3, n_sym), (c31, 0), (passed, 0))
            left = split(pick(scratch, everything, b))
            held[:, 2 * e * b : 2 * e * (b + 1)] = -dot3(left, split(col), NT)
            for i, (source, target) in enumerate(targets(b)):
                copies.append(pltpu.make_async_copy(source, target, sem.at[4 * b + i]))
                copies[-1].start()
        for copy in copies:
            copy.wait()


def finish(place, before, high, low, block, part, third, passed, last, swapped, rest, a3, c31):
    e = before.shape[1] // 4
    return call(
        finish_kernel,
        "finish",
        500 * 10**6,
        [(before.shape, F32)],
        [(SMEM, place), (HBM, before)]
        + [
            (VMEM, x)
            for x in (high, low, block, part, third, passed, last, swapped, rest, a3, c31)
        ],
        [
            pltpu.VMEM((2 * e, 4 * e), F32),
            pltpu.VMEM((2 * e, 3 * e), F32),
            pltpu.SemaphoreType.DMA((8,)),
        ],
        out_specs=[HBM],
        input_output_aliases={1: 0},
    )[0]


def tie(*values):
    return lax.optimization_barrier(values)


def solution(mesh):
    nx, ny = mesh.shape["gx"], mesh.shape["gy"]
    devices = [(x, y) for x in range(nx) for y in range(ny)]

    def is_same(x, y):
        return x // (nx // 2) == y // (ny // 2)

    def send(value, along_y, only=None):
        pairs = []
        for x, y in devices:
            if only is None or is_same(x, y) == only:
                to = (x, (y + ny // 2) % ny) if along_y else ((x + nx // 2) % nx, y)
                pairs.append((x * ny + y, to[0] * ny + to[1]))
        return lax.ppermute(value, ("gx", "gy"), pairs)

    def body(leaf):
        e = leaf.shape[1] // 4
        v = lax.axis_index("gx") // (nx // 2)
        u = lax.axis_index("gy") // (ny // 2)
        place = jnp.stack([v, u]).astype(jnp.int32)
        same = u == v
        a = cut_first(place, leaf)
        a_x = send(a, False)
        here, a = tie(place, a)
        hh = cut_side(here, leaf)
        hh_y = send(hh, True)
        swap, outer0, b, c = cut_second(place, leaf)
        swapped = send(swap, True)
        b, factor = gauge(hh, hh_y, b)
        b_x = send(b, False)
        n_last = outer0.shape[0] // T
        c1, c2, rest = scale_cross(factor, c, n_last)
        b, a_x, c1, swapped = tie(b, a_x, c1, swapped)
        b_y = send(b, True)
        a_x, b_y = tie(a_x, b_y)
        a_d = send(a_x, True)
        c1, b_x = tie(c1, b_x)
        c1_x = send(c1, False)
        b_x, b_y = tie(b_x, b_y)
        b_d = send(b_x, True)
        rest, b_d = tie(rest, b_d)
        rest = send(rest, True, only=True)
        side = factor_start((a, a_x, swapped, a_d), (b, b_x, b_y, b_d))
        n_mid = c2.shape[0] // T - n_last
        theirs = jnp.concatenate([c2[: n_mid * T], swapped[-n_last * T :]])
        third, side = tie(jnp.where(same, theirs, c2), side)
        third = send(third, False)
        c1_d = send(c1_x, True, only=True)
        high, low = factor_end(place, side, (b, b_x, b_y, b_d))
        top, bottom, block, part = own_rows(
            place, leaf, high, low, a, c1, c2, a_x, c1_x, swapped, rest
        )
        last, third, block = tie(jnp.where(same, c2[n_mid * T :], outer0), third, block)
        last = send(last, False)
        passed = send(third, True)
        out, block = products(
            place, high, low, top, bottom, block, (a, c1, c2), (a_x, c1_x, third), (a_d, c1_d, passed)
        )
        return finish(
            place, out, high, low, block, part, third, passed, last, swapped, rest, a_d, c1_d
        )

    return jax.shard_map(
        body,
        mesh=mesh,
        in_specs=(P(None, "gy", "gx"),),
        out_specs=P(None, "gy", "gx"),
        check_vma=False,
    )
```

```python
import functools
import math

import jax
import jax.numpy as jnp
from jax import lax
from jax.experimental import pallas as pl
from jax.experimental.pallas import tpu as pltpu
from jax.sharding import PartitionSpec as P

F32 = jnp.float32
BF16 = jnp.bfloat16
T = 128
R = 16
FIRST = 1
SECOND = 8
HBM = pl.BlockSpec(memory_space=pl.ANY)
FAR = pl.BlockSpec(memory_space=pltpu.HBM)
VMEM = pl.BlockSpec(memory_space=pltpu.VMEM)
SMEM = pl.BlockSpec(memory_space=pltpu.SMEM)
PARAMS = pltpu.CompilerParams(vmem_limit_bytes=32 * 2**20)


def dot(a, b, dims=((1,), (0,))):
    return lax.dot_general(
        a, b, (dims, ((), ())), precision=lax.Precision.HIGHEST, preferred_element_type=F32
    )


def dot16(a, b, dims=((1,), (0,))):
    return lax.dot_general(a, b, (dims, ((), ())), preferred_element_type=F32)


def split(a):
    high = a.astype(BF16)
    return high, (a - high.astype(F32)).astype(BF16)


def dot3(a, b, dims=((1,), (0,))):
    return dot16(a[0], b[0], dims) + (dot16(a[0], b[1], dims) + dot16(a[1], b[0], dims))


NT = ((1,), (1,))
TN = ((0,), (0,))


def upper(n):
    return [(i, j) for i in range(n) for j in range(i, n)]


def across_lanes(x, k):
    return jnp.broadcast_to(x[:, k : k + 1], x.shape)


def across_rows(x, k):
    return jnp.broadcast_to(x[k : k + 1, :], x.shape)


def panel(rows, c0, lower):
    sub = lax.broadcasted_iota(jnp.int32, rows.shape, 0)
    lane = lax.broadcasted_iota(jnp.int32, rows.shape, 1)
    cols = [across_lanes(rows, c0 + k) for k in range(R)]
    out = jnp.where((lane >= c0) & (lane < c0 + R), (lane - c0 == sub).astype(F32), rows)
    half = out
    scale = jnp.ones_like(rows)
    for k in range(R):
        pivot = across_rows(cols[k], k)
        inv = 1.0 / pivot
        here = sub == k
        mult = cols[k]

        def step(x):
            row = across_rows(x, k) * inv
            return jnp.where(here, row, x - mult * row)

        if lower:
            scale = jnp.where(here, pivot, scale)
            half = half - jnp.where(sub > k, mult, 0.0) * (across_rows(half, k) * inv)
        out = step(out)
        for j in range(k + 1, R):
            cols[j] = step(cols[j])
    return out, half * lax.rsqrt(scale) if lower else None


def put_rows(matrix, rows, r0):
    parts = [matrix[:r0]] if r0 else []
    parts.append(rows)
    if r0 + rows.shape[0] < matrix.shape[0]:
        parts.append(matrix[r0 + rows.shape[0] :])
    return jnp.concatenate(parts, axis=0)


def invert_tile(m, lower=False):
    lane = lax.broadcasted_iota(jnp.int32, (T, T), 1)
    sub = lax.broadcasted_iota(jnp.int32, (T, T), 0)
    rows = m[:R]
    for c0 in range(0, T, R):
        swept, half = panel(rows, c0, lower)
        if c0 + R < T:
            old = m[c0 + R : c0 + 2 * R]
            inside = (lane[:R] >= c0) & (lane[:R] < c0 + R)
            rows = jnp.where(inside, 0.0, old)
            for k in range(R):
                rows = rows - across_lanes(old, c0 + k) * across_rows(swept, k)
        wide = put_rows(jnp.zeros((T, T), F32), swept, c0)
        rest = jnp.where((lane >= c0) & (lane < c0 + R), 0.0, m) - dot(m, wide)
        if lower:
            rest = jnp.where(sub < c0, m, rest)
        m = put_rows(rest, half if lower else swept, c0)
    return jnp.where(lane > sub, 0.0, m) if lower else m


def sweep(ref, start, stop):
    n = ref.shape[0]
    for p in range(start, stop, T):
        pivot = invert_tile(ref[p : p + T, p : p + T])
        rows = dot(pivot, ref[p : p + T, :])
        parts = ([rows[:, :p]] if p else []) + [pivot]
        if p + T < n:
            parts.append(rows[:, p + T :])
        rows = jnp.concatenate(parts, axis=1)
        for q in range(0, n, T):
            if q != p:
                change = dot(ref[q : q + T, p : p + T], rows)
                ref[q : q + T, p : p + T] = jnp.zeros((T, T), F32)
                ref[q : q + T, :] = ref[q : q + T, :] - change
        ref[p : p + T, :] = rows


def inverse_factor(ref):
    n = ref.shape[0]
    for p in range(0, n, T):
        pivot = invert_tile(ref[p : p + T, p : p + T], lower=True)
        scaled = dot(pivot, ref[p : p + T, :])
        for q in range(p + T, n, T):
            weight = scaled[:, q : q + T]
            ref[q : q + T, :] = ref[q : q + T, :] - dot(weight, scaled, TN)
            ref[q : q + T, p : p + T] = -dot(weight, pivot, TN)
        for q in range(0, n, T):
            if q < p:
                ref[p : p + T, q : q + T] = scaled[:, q : q + T]
            else:
                ref[p : p + T, q : q + T] = pivot if q == p else jnp.zeros((T, T), F32)


def leaf_block(leaf, side_r, side_c, r, c, size):
    e = leaf.shape[1] // 4
    return leaf.at[
        0,
        pl.ds(pl.multiple_of(side_r * e + r * size, T), size),
        pl.ds(pl.multiple_of(side_c * e + c * size, T), size),
    ]


def run_copies(pairs, sem):
    copies = [pltpu.make_async_copy(a, b, sem.at[i]) for i, (a, b) in enumerate(pairs)]
    for copy in copies:
        copy.start()
    for copy in copies:
        copy.wait()


def sides(place):
    v, u = place[0], place[1]
    return [v, 2 + u], [1 - v, 3 - u]


def unpack(ref, at, tiles):
    held = {}
    for r, c in upper(tiles):
        held[r, c] = ref[at : at + T, :]
        if c > r:
            held[c, r] = held[r, c].T
        at += T
    return jnp.concatenate(
        [jnp.concatenate([held[r, c] for c in range(tiles)], axis=1) for r in range(tiles)], axis=0
    )


def call(kernel, name, cost, outs, ins, scratch, **more):
    return pl.pallas_call(
        kernel,
        out_shape=[jax.ShapeDtypeStruct(shape, dtype) for shape, dtype in outs],
        in_specs=[spec for spec, _ in ins],
        out_specs=more.pop("out_specs", [VMEM] * len(outs)),
        scratch_shapes=scratch,
        compiler_params=PARAMS,
        cost_estimate=pl.CostEstimate(flops=cost, bytes_accessed=cost, transcendentals=0),
        name=name,
        **more,
    )(*[value for _, value in ins])


def block_tiles(leaf, side_r, side_c, at):
    tiles = leaf.shape[1] // 4 // T
    return leaf_block(leaf, side_r, side_c, at // tiles, at % tiles, T)


def cross_tile(leaf, ext, inn, at):
    n = (leaf.shape[1] // 4 // T) ** 2
    return block_tiles(leaf, ext[at // n % 2], inn[at // n // 2], at % n)


def cut_first_kernel(place, leaf, a, sem):
    tiles = leaf.shape[1] // 4 // T
    ext, inn = sides(place)
    n_sym = len(upper(tiles))
    pairs = []
    for at, (r, c) in enumerate(upper(tiles)):
        pairs.append((leaf_block(leaf, inn[0], inn[0], r, c, T), a.at[pl.ds(at * T, T)]))
    for at in range(FIRST):
        pairs.append(
            (cross_tile(leaf, ext, inn, at), a.at[pl.ds((n_sym + at) * T, T)])
        )
    run_copies(pairs, sem)


def cut_first(place, leaf):
    n_sym = len(upper(leaf.shape[1] // 4 // T))
    return call(
        cut_first_kernel,
        "cut_first",
        1000 * 10**6,
        [(((n_sym + FIRST) * T, T), F32)],
        [(SMEM, place), (FAR, leaf)],
        [pltpu.SemaphoreType.DMA((n_sym + FIRST,))],
    )[0]


def cut_side_kernel(place, leaf, hh, sem):
    tiles = leaf.shape[1] // 4 // T
    _, inn = sides(place)
    pairs = []
    for at, (r, c) in enumerate(upper(tiles)):
        pairs.append((leaf_block(leaf, inn[1], inn[1], r, c, T), hh.at[pl.ds(at * T, T)]))
    run_copies(pairs, sem)


def cut_side(place, leaf):
    n_sym = len(upper(leaf.shape[1] // 4 // T))
    return call(
        cut_side_kernel,
        "cut_side",
        1000 * 10**6,
        [((n_sym * T, T), F32)],
        [(SMEM, place), (FAR, leaf)],
        [pltpu.SemaphoreType.DMA((n_sym,))],
    )[0]


def cut_second_kernel(place, leaf, swap, outer0, b, c, sem):
    e = leaf.shape[1] // 4
    tiles = e // T
    ext, inn = sides(place)
    n_sym = len(upper(tiles))
    pairs = [
        (leaf_block(leaf, inn[0], inn[1], 0, 0, e), b),
        (leaf_block(leaf, ext[0], inn[0], 0, 0, e), c.at[pl.ds(0, e)]),
        (leaf_block(leaf, ext[1], inn[0], 0, 0, e), c.at[pl.ds(e, e)]),
        (leaf_block(leaf, ext[0], inn[1], 0, 0, e), c.at[pl.ds(2 * e, e)]),
        (leaf_block(leaf, ext[1], inn[1], 0, 0, e), c.at[pl.ds(3 * e, e)]),
    ]
    for at, (r, k) in enumerate(upper(tiles)):
        pairs.append((leaf_block(leaf, inn[0], inn[0], r, k, T), swap.at[pl.ds(at * T, T)]))
    half = outer0.shape[0] // T
    second = []
    for at, (r, k) in enumerate(upper(2 * tiles)):
        source = leaf_block(leaf, ext[r // tiles], ext[k // tiles], r % tiles, k % tiles, T)
        if at < half:
            pairs.append((source, outer0.at[pl.ds(at * T, T)]))
        else:
            second.append((source, swap.at[pl.ds((n_sym + at - half) * T, T)]))
    run_copies(pairs, sem)
    same = place[0] == place[1]

    @pl.when(same)
    def _():
        cross = [
            (cross_tile(leaf, ext, inn, at), swap.at[pl.ds((n_sym + at) * T, T)])
            for at in range(half)
        ]
        run_copies(cross, sem)

    @pl.when(jnp.logical_not(same))
    def _():
        run_copies(second, sem)


def cut_second(place, leaf):
    e = leaf.shape[1] // 4
    n_sym = len(upper(e // T))
    half = len(upper(2 * (e // T))) // 2
    return call(
        cut_second_kernel,
        "cut_second",
        1000 * 10**6,
        [(((n_sym + half) * T, T), F32), ((half * T, T), F32), ((e, e), F32), ((4 * e, e), F32)],
        [(SMEM, place), (FAR, leaf)],
        [pltpu.SemaphoreType.DMA((n_sym + half + 5,))],
    )


def gauge_kernel(mine, along, b, b_out, factor):
    e = factor.shape[0]
    tiles = e // T
    factor[...] = unpack(mine, 0, tiles) + unpack(along, 0, tiles)
    inverse_factor(factor)
    b_out[...] = dot(b[...], factor[...], NT)


def gauge(mine, along, b):
    e = b.shape[0]
    return call(
        gauge_kernel,
        "gauge_side",
        8000 * 10**6,
        [((e, e), F32), ((e, e), F32)],
        [(VMEM, x) for x in (mine, along, b)],
        [],
    )


def scale_kernel(factor, c, c1, c2, rest):
    e = factor.shape[0]
    tiles = e // T
    scaled = dot3(split(c[2 * e :, :]), split(factor[...]), NT)
    total = 4 * tiles * tiles
    for at in range(FIRST, total):
        r, k = at // tiles * T, at % tiles * T
        tile = c[r : r + T, k : k + T] if r < 2 * e else scaled[r - 2 * e : r - 2 * e + T, k : k + T]
        if at < FIRST + SECOND:
            c1[(at - FIRST) * T : (at - FIRST + 1) * T, :] = tile
        else:
            c2[(at - FIRST - SECOND) * T : (at - FIRST - SECOND + 1) * T, :] = tile
        spot = at * T - (total * T - rest.shape[0])
        if spot >= 0:
            rest[spot : spot + T, :] = tile


def scale_cross(factor, c, swapped):
    e = factor.shape[0]
    total = 4 * e * e // T
    return call(
        scale_kernel,
        "scale_cross",
        2000 * 10**6,
        [((n, T), F32) for n in (SECOND * T, total - (FIRST + SECOND) * T, total - swapped * T)],
        [(VMEM, x) for x in (factor, c)],
        [],
    )


def couple(b):
    mine, across, along, corner = (ref[...] for ref in b)
    return jnp.concatenate(
        [jnp.concatenate([mine, across], axis=1), jnp.concatenate([along, corner], axis=1)], axis=0
    )


def factor_start_kernel(a0, a1, a2, a3, b0, b1, b2, b3, side):
    e = b0.shape[0]
    tiles = e // T
    coup = couple((b0, b1, b2, b3))
    side[...] = -dot(coup, coup, NT)
    side[:e, :e] = side[:e, :e] + (unpack(a0, 0, tiles) + unpack(a1, 0, tiles))
    side[e:, e:] = side[e:, e:] + (unpack(a2, 0, tiles) + unpack(a3, 0, tiles))
    sweep(side, 0, e)


def factor_start(a, b):
    e = b[0].shape[0]
    return call(
        factor_start_kernel,
        "factor_start",
        1000 * 10**6,
        [((2 * e, 2 * e), F32)],
        [(VMEM, x) for x in (*a, *b)],
        [],
    )[0]


def factor_end_kernel(place, side_in, b0, b1, b2, b3, high, low, side, full):
    e = b0.shape[0]
    side[...] = side_in[...]
    sweep(side, e, 2 * e)
    coup = split(couple((b0, b1, b2, b3)))
    away = dot3(split(side[...]), coup)
    shape = full.shape
    unit = lax.broadcasted_iota(jnp.int32, shape, 0) == lax.broadcasted_iota(jnp.int32, shape, 1)
    full[...] = dot3(coup, split(away), TN) + unit.astype(F32)

    def emit(value, rows, columns):
        high[rows, columns], low[rows, columns] = split(value)

    first, rest = slice(0, e), slice(e, 3 * e)
    emit(full[...], rest, rest)
    emit(-away[:e, :], first, rest)
    same = place[0] == place[1]

    @pl.when(same)
    def _():
        emit(side[:e, :e], first, first)
        emit(-away[:e, :].T, rest, first)

    @pl.when(jnp.logical_not(same))
    def _():
        emit(side[:e, e:], first, first)
        emit(-away[e:, :].T, rest, first)


def factor_end(place, side, b):
    e = b[0].shape[0]
    return call(
        factor_end_kernel,
        "factor_end",
        10000 * 10**6,
        [((3 * e, 3 * e), BF16)] * 2,
        [(SMEM, place), (VMEM, side)] + [(VMEM, x) for x in b],
        [pltpu.VMEM((2 * e, 2 * e), F32), pltpu.VMEM((2 * e, 2 * e), F32)],
    )


def cross_block(*pieces):
    held = []
    for ref, skip in pieces:
        for at in range(skip * T, ref.shape[0], T):
            held.append(ref[at : at + T, :])
    tiles = math.isqrt(len(held) // 4)
    rows = []
    for r in range(2 * tiles):
        side = r // tiles
        row = [held[((side + 2 * c) * tiles + r % tiles) * tiles + k] for c in range(2) for k in range(tiles)]
        rows.append(jnp.concatenate(row, axis=1))
    return jnp.concatenate(rows, axis=0)


def symmetric_tiles(e):
    return len(upper(e // T))


def zeros(tiles):
    return jnp.zeros((tiles * T, T), F32), 0


def times_inverse(cross, high, low, inner):
    e = cross.shape[1] // 2
    return dot3(split(cross[:, :e]), (high[:e], low[:e])) + dot3(
        split(cross[:, e:]), (high[inner], low[inner])
    )


def rows_kernel(
    place, leaf, high, low, a0, c01, c02, a1, c11, swapped, rest, top, bottom, block, part, col, own, sem
):
    e = leaf.shape[1] // 4
    n_sym = symmetric_tiles(e)
    ext, _ = sides(place)
    copies = []
    for r in range(2):
        for c in range(2):
            target = own.at[pl.ds(r * e, e), pl.ds(c * e, e)]
            source = leaf_block(leaf, ext[r], ext[c], 0, 0, e)
            copies.append(pltpu.make_async_copy(source, target, sem.at[2 * r + c]))
            copies[-1].start()
    same = place[0] == place[1]
    mine = cross_block((a0, n_sym), (c01, 0), (c02, 0))

    @pl.when(same)
    def _():
        col[...] = mine

    @pl.when(jnp.logical_not(same))
    def _():
        col[...] = cross_block((swapped, n_sym), (rest, 0))
        across = cross_block((a1, n_sym), (c11, 0), zeros(c02.shape[0] // T))
        part[...] = times_inverse(across, high[...], low[...], slice(2 * e, 3 * e))

    left = split(times_inverse(mine, high[...], low[...], slice(e, 2 * e)))
    top[...], bottom[...] = left
    left = [x[:, : 2 * e] for x in left]
    block[...] = -dot3(left, split(col[...]), NT)
    for copy in copies:
        copy.wait()

    @pl.when(same)
    def _():
        block[...] = block[...] + own[...]


def own_rows(place, leaf, high, low, a0, c01, c02, a1, c11, swapped, rest):
    e = leaf.shape[1] // 4
    return call(
        rows_kernel,
        "own_rows",
        500 * 10**6,
        [((2 * e, 3 * e), BF16)] * 2 + [((2 * e, 2 * e), F32), ((2 * e, 3 * e), F32)],
        [(SMEM, place), (FAR, leaf)]
        + [(VMEM, x) for x in (high, low, a0, c01, c02, a1, c11, swapped, rest)],
        [
            pltpu.VMEM((2 * e, 2 * e), F32),
            pltpu.VMEM((2 * e, 2 * e), F32),
            pltpu.SemaphoreType.DMA((4,)),
        ],
    )


def spot(place, e, side, which):
    x = place[0] if which == 0 else 1 - place[0]
    return pl.ds(pl.multiple_of((2 * side + x) * e, T), e)


def write(out, place, value, a, b):
    e = out.shape[1] // 4
    for r in range(2):
        for c in range(2):
            out[0, spot(place, e, r, a), spot(place, e, c, b)] = value[
                r * e : (r + 1) * e, c * e : (c + 1) * e
            ]


def pick(ref, rows, b):
    e = ref.shape[1] // 3
    return jnp.concatenate([ref[rows, :e], ref[rows, (1 + b) * e : (2 + b) * e]], axis=1)


def late_row(e):
    tiles = e // T
    return (2 * tiles * tiles - len(upper(2 * tiles)) // 2) // tiles * T


def products_kernel(
    n_mid, place, high, low, top, bottom, block, before, swapped, rest, a0, c01, c02, a1, c11, third,
    a3, c31, passed, out, part, scratch
):
    e = out.shape[1] // 4
    n_sym = symmetric_tiles(e)
    same = place[0] == place[1]
    write(out, place, block[...], 0, 0)
    everything = slice(0, 2 * e)

    @pl.when(same)
    def _():
        across = cross_block((a1, n_sym), (c11, 0), (third, 0))
        right = split(across)
        left = [pick(x, everything, 1) for x in (top, bottom)]
        write(out, place, -dot3(left, right, NT), 0, 1)
        scratch[...] = times_inverse(across, high[...], low[...], slice(2 * e, 3 * e))
        left = split(pick(scratch, everything, 0))
        mine = cross_block((a0, n_sym), (c01, 0), (c02, 0))
        write(out, place, -dot3(left, split(mine), NT), 1, 0)
        left = split(pick(scratch, everything, 1))
        part[:, : 2 * e] = -dot3(left, right, NT)

    @pl.when(jnp.logical_not(same))
    def _():
        cols = [
            split(cross_block((swapped, n_sym), (rest, 0))),
            split(cross_block((a3, n_sym), (c31, 0), (passed, 0))),
        ]
        left = [pick(x, everything, 1) for x in (top, bottom)]
        write(out, place, -dot3(left, cols[1], NT), 0, 1)
        n_last = 4 * (e // T) ** 2 - FIRST - SECOND - n_mid
        middle = cross_block(zeros(FIRST + SECOND), (third[: n_mid * T, :], 0), zeros(n_last))
        inner = slice(2 * e, 3 * e)
        part[:e, :] = before[:e, :] + dot3(split(middle[:e, e:]), (high[inner], low[inner]))
        part[e:, :] = before[e:, :]
        start = late_row(e)
        for b in range(2):
            value = -dot3(split(pick(part, slice(0, start), b)), cols[b], NT)
            for c in range(2):
                rows = pl.ds(spot(place, e, 0, 1).start, start)
                out[0, rows, spot(place, e, c, b)] = value[:, c * e : (c + 1) * e]


def products(n_mid, place, high, low, top, bottom, block, part, swapped, rest, mine, across, corner):
    e = block.shape[0] // 2
    return call(
        functools.partial(products_kernel, n_mid),
        "products",
        500 * 10**6,
        [((1, 4 * e, 4 * e), F32), ((2 * e, 3 * e), F32)],
        [(SMEM, place)]
        + [(VMEM, x) for x in (high, low, top, bottom, block, part, swapped, rest)]
        + [(VMEM, x) for x in (*mine, *across, *corner)],
        [pltpu.VMEM((2 * e, 3 * e), F32)],
    )


def finish_kernel(
    place, before, high, low, part, passed, last, swapped, rest, a3, c31, out, held, scratch, sem
):
    e = out.shape[1] // 4
    tiles = e // T
    n_sym = symmetric_tiles(e)

    def targets(b, start):
        pairs = []
        for r in range(2):
            skip = start if r == 0 else 0
            rows = pl.multiple_of(spot(place, e, r, 1).start + skip, T)
            for c in range(2):
                pairs.append(
                    (
                        held.at[pl.ds(r * e + skip, e - skip), pl.ds((2 * b + c) * e, e)],
                        out.at[0, pl.ds(rows, e - skip), spot(place, e, c, b)],
                    )
                )
        return pairs

    n_last = last.shape[0] // T

    @pl.when(place[0] == place[1])
    def _():
        skip = passed.shape[0] // T - n_last
        for at, (i, j) in enumerate(upper(2 * tiles)):
            ref, at = (last, at) if at < n_last else (passed, at - n_last + skip)
            piece = ref[at * T : (at + 1) * T, :]
            r, c = slice(i * T, (i + 1) * T), slice(j * T, (j + 1) * T)
            shift = 2 * e
            held[r, j * T + shift : (j + 1) * T + shift] = part[r, c] + piece
            if i != j:
                held[c, i * T + shift : (i + 1) * T + shift] = part[c, r] + piece.T
        run_copies(targets(1, 0), sem)

    @pl.when(place[0] != place[1])
    def _():
        start = late_row(e)
        late = cross_block(zeros(4 * tiles * tiles - n_last), (last, 0))[start:, e:]
        inner = slice(2 * e, 3 * e)
        scratch[start:, :] = part[start:, :] + dot3(split(late), (high[inner], low[inner]))
        copies = []
        for b in range(2):
            if b == 0:
                col = cross_block((swapped, n_sym), (rest, 0))
            else:
                col = cross_block((a3, n_sym), (c31, 0), (passed, 0))
            left = split(pick(scratch, slice(start, 2 * e), b))
            held[start:, 2 * e * b : 2 * e * (b + 1)] = -dot3(left, split(col), NT)
            for i, (source, target) in enumerate(targets(b, start)):
                copies.append(pltpu.make_async_copy(source, target, sem.at[4 * b + i]))
                copies[-1].start()
        for copy in copies:
            copy.wait()


def finish(place, before, high, low, part, passed, last, swapped, rest, a3, c31):
    e = before.shape[1] // 4
    return call(
        finish_kernel,
        "finish",
        500 * 10**6,
        [(before.shape, F32)],
        [(SMEM, place), (HBM, before)]
        + [(VMEM, x) for x in (high, low, part, passed, last, swapped, rest, a3, c31)],
        [
            pltpu.VMEM((2 * e, 4 * e), F32),
            pltpu.VMEM((2 * e, 3 * e), F32),
            pltpu.SemaphoreType.DMA((8,)),
        ],
        out_specs=[HBM],
        input_output_aliases={1: 0},
    )[0]


def tie(*values):
    return lax.optimization_barrier(values)


def solution(mesh):
    nx, ny = mesh.shape["gx"], mesh.shape["gy"]
    devices = [(x, y) for x in range(nx) for y in range(ny)]

    def is_same(x, y):
        return x // (nx // 2) == y // (ny // 2)

    def send(value, along_y, only=None):
        pairs = []
        for x, y in devices:
            if only is None or is_same(x, y) == only:
                to = (x, (y + ny // 2) % ny) if along_y else ((x + nx // 2) % nx, y)
                pairs.append((x * ny + y, to[0] * ny + to[1]))
        return lax.ppermute(value, ("gx", "gy"), pairs)

    def body(leaf):
        e = leaf.shape[1] // 4
        v = lax.axis_index("gx") // (nx // 2)
        u = lax.axis_index("gy") // (ny // 2)
        place = jnp.stack([v, u]).astype(jnp.int32)
        same = u == v
        a = cut_first(place, leaf)
        a_x = send(a, False)
        here, a = tie(place, a)
        hh = cut_side(here, leaf)
        hh_y = send(hh, True)
        swap, outer0, b, c = cut_second(place, leaf)
        swap, hh_y = tie(swap, hh_y)
        swapped = send(swap, True)
        b, factor = gauge(hh, hh_y, b)
        b_x = send(b, False)
        n_last = outer0.shape[0] // T
        c1, c2, rest = scale_cross(factor, c, n_last)
        b, a_x, c1, swapped = tie(b, a_x, c1, swapped)
        b_y = send(b, True)
        a_x, b_y = tie(a_x, b_y)
        a_d = send(a_x, True)
        c1, b_x = tie(c1, b_x)
        c1_x = send(c1, False)
        b_x, b_y = tie(b_x, b_y)
        b_d = send(b_x, True)
        rest, b_d, a_d = tie(rest, b_d, a_d)
        rest = send(rest, True, only=True)
        side = factor_start((a, a_x, swapped, a_d), (b, b_x, b_y, b_d))
        n_mid = c2.shape[0] // T - n_last
        theirs = jnp.concatenate([c2[: n_mid * T], swapped[-n_last * T :]])
        third, side = tie(jnp.where(same, theirs, c2), side)
        third = send(third, False)
        c1_d = send(c1_x, True, only=True)
        high, low = factor_end(place, side, (b, b_x, b_y, b_d))
        top, bottom, block, part = own_rows(
            place, leaf, high, low, a, c1, c2, a_x, c1_x, swapped, rest
        )
        last, block = tie(jnp.where(same, c2[n_mid * T :], outer0), block)
        last = send(last, False)
        third, block = tie(third, block)
        passed = send(third, True)
        mine, across, corner = (a, c1, c2), (a_x, c1_x, third), (a_d, c1_d, passed)
        out, part = products(
            n_mid, place, high, low, top, bottom, block, part, swapped, rest, mine, across, corner
        )
        return finish(place, out, high, low, part, passed, last, swapped, rest, a_d, c1_d)

    return jax.shard_map(
        body,
        mesh=mesh,
        in_specs=(P(None, "gy", "gx"),),
        out_specs=P(None, "gy", "gx"),
        check_vma=False,
    )
```

```python
import math

import jax
import jax.numpy as jnp
from jax import lax
from jax.experimental import pallas as pl
from jax.experimental.pallas import tpu as pltpu
from jax.sharding import PartitionSpec as P

F32 = jnp.float32
BF16 = jnp.bfloat16
T = 128
ALONE = 59
R = 16
FIRST = 1
SECOND = 10
HBM = pl.BlockSpec(memory_space=pl.ANY)
FAR = pl.BlockSpec(memory_space=pltpu.HBM)
VMEM = pl.BlockSpec(memory_space=pltpu.VMEM)
SMEM = pl.BlockSpec(memory_space=pltpu.SMEM)


def dot(a, b, dims=((1,), (0,))):
    return lax.dot_general(
        a, b, (dims, ((), ())), precision=lax.Precision.HIGHEST, preferred_element_type=F32
    )


def dot16(a, b, dims=((1,), (0,))):
    return lax.dot_general(a, b, (dims, ((), ())), preferred_element_type=F32)


def split(a):
    high = a.astype(BF16)
    return high, (a - high.astype(F32)).astype(BF16)


def dot3(a, b, dims=((1,), (0,))):
    return dot16(a[0], b[0], dims) + (dot16(a[0], b[1], dims) + dot16(a[1], b[0], dims))


NT = ((1,), (1,))
TN = ((0,), (0,))


def upper(n):
    return [(i, j) for i in range(n) for j in range(i, n)]


def across_lanes(x, k):
    return jnp.broadcast_to(x[:, k : k + 1], x.shape)


def across_rows(x, k):
    return jnp.broadcast_to(x[k : k + 1, :], x.shape)


def panel(rows, c0, lower):
    sub = lax.broadcasted_iota(jnp.int32, rows.shape, 0)
    lane = lax.broadcasted_iota(jnp.int32, rows.shape, 1)
    cols = [across_lanes(rows, c0 + k) for k in range(R)]
    out = jnp.where((lane >= c0) & (lane < c0 + R), (lane - c0 == sub).astype(F32), rows)
    half = out
    scale = jnp.ones_like(rows)
    for k in range(R):
        pivot = across_rows(cols[k], k)
        inv = 1.0 / pivot
        here = sub == k
        mult = cols[k]

        def step(x):
            row = across_rows(x, k) * inv
            return jnp.where(here, row, x - mult * row)

        if lower:
            scale = jnp.where(here, pivot, scale)
            half = half - jnp.where(sub > k, mult, 0.0) * (across_rows(half, k) * inv)
        out = step(out)
        for j in range(k + 1, R):
            cols[j] = step(cols[j])
    return out, half * lax.rsqrt(scale) if lower else None


def put_rows(matrix, rows, r0):
    parts = [matrix[:r0]] if r0 else []
    parts.append(rows)
    if r0 + rows.shape[0] < matrix.shape[0]:
        parts.append(matrix[r0 + rows.shape[0] :])
    return jnp.concatenate(parts, axis=0)


def invert_tile(m, lower=False):
    lane = lax.broadcasted_iota(jnp.int32, (T, T), 1)
    sub = lax.broadcasted_iota(jnp.int32, (T, T), 0)
    rows = m[:R]
    for c0 in range(0, T, R):
        swept, half = panel(rows, c0, lower)
        if c0 + R < T:
            old = m[c0 + R : c0 + 2 * R]
            inside = (lane[:R] >= c0) & (lane[:R] < c0 + R)
            rows = jnp.where(inside, 0.0, old)
            for k in range(R):
                rows = rows - across_lanes(old, c0 + k) * across_rows(swept, k)
        wide = put_rows(jnp.zeros((T, T), F32), swept, c0)
        rest = jnp.where((lane >= c0) & (lane < c0 + R), 0.0, m) - dot(m, wide)
        if lower:
            rest = jnp.where(sub < c0, m, rest)
        m = put_rows(rest, half if lower else swept, c0)
    return jnp.where(lane > sub, 0.0, m) if lower else m


def sweep(ref, start, stop):
    n = ref.shape[0]
    for p in range(start, stop, T):
        pivot = invert_tile(ref[p : p + T, p : p + T])
        rows = dot(pivot, ref[p : p + T, :])
        parts = ([rows[:, :p]] if p else []) + [pivot]
        if p + T < n:
            parts.append(rows[:, p + T :])
        rows = jnp.concatenate(parts, axis=1)
        for q in range(0, n, T):
            if q != p:
                change = dot(ref[q : q + T, p : p + T], rows)
                ref[q : q + T, p : p + T] = jnp.zeros((T, T), F32)
                ref[q : q + T, :] = ref[q : q + T, :] - change
        ref[p : p + T, :] = rows


def inverse_factor(ref):
    n = ref.shape[0]
    for p in range(0, n, T):
        pivot = invert_tile(ref[p : p + T, p : p + T], lower=True)
        scaled = dot(pivot, ref[p : p + T, :])
        for q in range(p + T, n, T):
            weight = scaled[:, q : q + T]
            ref[q : q + T, :] = ref[q : q + T, :] - dot(weight, scaled, TN)
            ref[q : q + T, p : p + T] = -dot(weight, pivot, TN)
        for q in range(0, n, T):
            if q < p:
                ref[p : p + T, q : q + T] = scaled[:, q : q + T]
            else:
                ref[p : p + T, q : q + T] = pivot if q == p else jnp.zeros((T, T), F32)


def leaf_block(leaf, side_r, side_c, r, c, size):
    e = leaf.shape[1] // 4
    return leaf.at[
        0,
        pl.ds(pl.multiple_of(side_r * e + r * size, T), size),
        pl.ds(pl.multiple_of(side_c * e + c * size, T), size),
    ]


def run_copies(pairs, sem):
    copies = [pltpu.make_async_copy(a, b, sem.at[i]) for i, (a, b) in enumerate(pairs)]
    for copy in copies:
        copy.start()
    for copy in copies:
        copy.wait()


def sides(place):
    v, u = place[0], place[1]
    return [v, 2 + u], [1 - v, 3 - u]


def unpack(ref, at, tiles):
    held = {}
    for r, c in upper(tiles):
        held[r, c] = ref[at : at + T, :]
        if c > r:
            held[c, r] = held[r, c].T
        at += T
    return jnp.concatenate(
        [jnp.concatenate([held[r, c] for c in range(tiles)], axis=1) for r in range(tiles)], axis=0
    )


def call(kernel, name, cost, outs, ins, scratch, room=32, **more):
    return pl.pallas_call(
        kernel,
        out_shape=[jax.ShapeDtypeStruct(shape, dtype) for shape, dtype in outs],
        in_specs=[spec for spec, _ in ins],
        out_specs=more.pop("out_specs", [VMEM] * len(outs)),
        scratch_shapes=scratch,
        compiler_params=pltpu.CompilerParams(vmem_limit_bytes=room * 2**20),
        cost_estimate=pl.CostEstimate(flops=cost, bytes_accessed=cost, transcendentals=0),
        name=name,
        **more,
    )(*[value for _, value in ins])


def block_tiles(leaf, side_r, side_c, at):
    tiles = leaf.shape[1] // 4 // T
    return leaf_block(leaf, side_r, side_c, at // tiles, at % tiles, T)


def cross_tile(leaf, ext, inn, at):
    n = (leaf.shape[1] // 4 // T) ** 2
    return block_tiles(leaf, ext[at // n % 2], inn[at // n // 2], at % n)


def cut_first_kernel(place, leaf, a, sem):
    tiles = leaf.shape[1] // 4 // T
    ext, inn = sides(place)
    n_sym = len(upper(tiles))
    pairs = []
    for at, (r, c) in enumerate(upper(tiles)):
        pairs.append((leaf_block(leaf, inn[0], inn[0], r, c, T), a.at[pl.ds(at * T, T)]))
    for at in range(FIRST):
        pairs.append(
            (cross_tile(leaf, ext, inn, at), a.at[pl.ds((n_sym + at) * T, T)])
        )
    run_copies(pairs, sem)


def cut_first(place, leaf):
    n_sym = len(upper(leaf.shape[1] // 4 // T))
    return call(
        cut_first_kernel,
        "cut_first",
        1000 * 10**6,
        [(((n_sym + FIRST) * T, T), F32)],
        [(SMEM, place), (FAR, leaf)],
        [pltpu.SemaphoreType.DMA((n_sym + FIRST,))],
        room=ALONE,
    )[0]


def cut_side_kernel(place, leaf, hh, sem):
    tiles = leaf.shape[1] // 4 // T
    _, inn = sides(place)
    pairs = []
    for at, (r, c) in enumerate(upper(tiles)):
        pairs.append((leaf_block(leaf, inn[1], inn[1], r, c, T), hh.at[pl.ds(at * T, T)]))
    run_copies(pairs, sem)


def cut_side(place, leaf):
    n_sym = len(upper(leaf.shape[1] // 4 // T))
    return call(
        cut_side_kernel,
        "cut_side",
        1000 * 10**6,
        [((n_sym * T, T), F32)],
        [(SMEM, place), (FAR, leaf)],
        [pltpu.SemaphoreType.DMA((n_sym,))],
        room=ALONE,
    )[0]


def cut_second_kernel(place, leaf, swap, outer0, b, c, sem):
    e = leaf.shape[1] // 4
    tiles = e // T
    ext, inn = sides(place)
    n_sym = len(upper(tiles))
    pairs = [
        (leaf_block(leaf, inn[0], inn[1], 0, 0, e), b),
        (leaf_block(leaf, ext[0], inn[0], 0, 0, e), c.at[pl.ds(0, e)]),
        (leaf_block(leaf, ext[1], inn[0], 0, 0, e), c.at[pl.ds(e, e)]),
        (leaf_block(leaf, ext[0], inn[1], 0, 0, e), c.at[pl.ds(2 * e, e)]),
        (leaf_block(leaf, ext[1], inn[1], 0, 0, e), c.at[pl.ds(3 * e, e)]),
    ]
    for at, (r, k) in enumerate(upper(tiles)):
        pairs.append((leaf_block(leaf, inn[0], inn[0], r, k, T), swap.at[pl.ds(at * T, T)]))
    half = outer0.shape[0] // T
    second = []
    for at, (r, k) in enumerate(upper(2 * tiles)):
        source = leaf_block(leaf, ext[r // tiles], ext[k // tiles], r % tiles, k % tiles, T)
        if at < half:
            pairs.append((source, outer0.at[pl.ds(at * T, T)]))
        else:
            second.append((source, swap.at[pl.ds((n_sym + at - half) * T, T)]))
    run_copies(pairs, sem)
    same = place[0] == place[1]

    @pl.when(same)
    def _():
        cross = [
            (cross_tile(leaf, ext, inn, at), swap.at[pl.ds((n_sym + at) * T, T)])
            for at in range(half)
        ]
        run_copies(cross, sem)

    @pl.when(jnp.logical_not(same))
    def _():
        run_copies(second, sem)


def cut_second(place, leaf):
    e = leaf.shape[1] // 4
    n_sym = len(upper(e // T))
    half = len(upper(2 * (e // T))) // 2
    return call(
        cut_second_kernel,
        "cut_second",
        1000 * 10**6,
        [(((n_sym + half) * T, T), F32), ((half * T, T), F32), ((e, e), F32), ((4 * e, e), F32)],
        [(SMEM, place), (HBM, leaf)],
        [pltpu.SemaphoreType.DMA((n_sym + half + 5,))],
    )


def gauge_kernel(mine, along, b, b_out, factor):
    e = factor.shape[0]
    tiles = e // T
    factor[...] = unpack(mine, 0, tiles) + unpack(along, 0, tiles)
    inverse_factor(factor)
    b_out[...] = dot(b[...], factor[...], NT)


def gauge(mine, along, b):
    e = b.shape[0]
    return call(
        gauge_kernel,
        "gauge_side",
        8000 * 10**6,
        [((e, e), F32), ((e, e), F32)],
        [(VMEM, x) for x in (mine, along, b)],
        [],
    )


def scale_kernel(factor, c, c1, c2, rest):
    e = factor.shape[0]
    tiles = e // T
    scaled = dot3(split(c[2 * e :, :]), split(factor[...]), NT)
    total = 4 * tiles * tiles
    for at in range(FIRST, total):
        r, k = at // tiles * T, at % tiles * T
        tile = c[r : r + T, k : k + T] if r < 2 * e else scaled[r - 2 * e : r - 2 * e + T, k : k + T]
        if at < FIRST + SECOND:
            c1[(at - FIRST) * T : (at - FIRST + 1) * T, :] = tile
        else:
            c2[(at - FIRST - SECOND) * T : (at - FIRST - SECOND + 1) * T, :] = tile
        spot = at * T - (total * T - rest.shape[0])
        if spot >= 0:
            rest[spot : spot + T, :] = tile


def scale_cross(factor, c, swapped):
    e = factor.shape[0]
    total = 4 * e * e // T
    return call(
        scale_kernel,
        "scale_cross",
        2000 * 10**6,
        [((n, T), F32) for n in (SECOND * T, total - (FIRST + SECOND) * T, total - swapped * T)],
        [(VMEM, x) for x in (factor, c)],
        [],
    )


def couple(b):
    mine, across, along, corner = (ref[...] for ref in b)
    return jnp.concatenate(
        [jnp.concatenate([mine, across], axis=1), jnp.concatenate([along, corner], axis=1)], axis=0
    )


def factor_start_kernel(a0, a1, a2, a3, b0, b1, b2, b3, side):
    e = b0.shape[0]
    tiles = e // T
    coup = couple((b0, b1, b2, b3))
    side[...] = -dot(coup, coup, NT)
    side[:e, :e] = side[:e, :e] + (unpack(a0, 0, tiles) + unpack(a1, 0, tiles))
    side[e:, e:] = side[e:, e:] + (unpack(a2, 0, tiles) + unpack(a3, 0, tiles))
    sweep(side, 0, e)


def factor_start(a, b):
    e = b[0].shape[0]
    return call(
        factor_start_kernel,
        "factor_start",
        3500 * 10**6,
        [((2 * e, 2 * e), F32)],
        [(VMEM, x) for x in (*a, *b)],
        [],
    )[0]


def factor_end_kernel(place, side_in, b0, b1, b2, b3, high, low, side, full):
    e = b0.shape[0]
    side[...] = side_in[...]
    sweep(side, e, 2 * e)
    coup = split(couple((b0, b1, b2, b3)))
    away = dot3(split(side[...]), coup)
    shape = full.shape
    unit = lax.broadcasted_iota(jnp.int32, shape, 0) == lax.broadcasted_iota(jnp.int32, shape, 1)
    full[...] = dot3(coup, split(away), TN) + unit.astype(F32)

    def emit(value, rows, columns):
        high[rows, columns], low[rows, columns] = split(value)

    first, rest = slice(0, e), slice(e, 3 * e)
    emit(full[...], rest, rest)
    emit(-away[:e, :], first, rest)
    same = place[0] == place[1]

    @pl.when(same)
    def _():
        emit(side[:e, :e], first, first)
        emit(-away[:e, :].T, rest, first)

    @pl.when(jnp.logical_not(same))
    def _():
        emit(side[:e, e:], first, first)
        emit(-away[e:, :].T, rest, first)


def factor_end(place, side, b):
    e = b[0].shape[0]
    return call(
        factor_end_kernel,
        "factor_end",
        10000 * 10**6,
        [((3 * e, 3 * e), BF16)] * 2,
        [(SMEM, place), (VMEM, side)] + [(VMEM, x) for x in b],
        [pltpu.VMEM((2 * e, 2 * e), F32), pltpu.VMEM((2 * e, 2 * e), F32)],
    )


def cross_block(*pieces):
    held = []
    for ref, skip in pieces:
        for at in range(skip * T, ref.shape[0], T):
            held.append(ref[at : at + T, :])
    tiles = math.isqrt(len(held) // 4)
    rows = []
    for r in range(2 * tiles):
        side = r // tiles
        row = [held[((side + 2 * c) * tiles + r % tiles) * tiles + k] for c in range(2) for k in range(tiles)]
        rows.append(jnp.concatenate(row, axis=1))
    return jnp.concatenate(rows, axis=0)


def symmetric_tiles(e):
    return len(upper(e // T))


def zeros(tiles):
    return jnp.zeros((tiles * T, T), F32), 0


def times_inverse(cross, high, low, inner):
    e = cross.shape[1] // 2
    return dot3(split(cross[:, :e]), (high[:e], low[:e])) + dot3(
        split(cross[:, e:]), (high[inner], low[inner])
    )


def spot(place, e, side, which):
    x = place[0] if which == 0 else 1 - place[0]
    return pl.ds(pl.multiple_of((2 * side + x) * e, T), e)


def put(out, place, held, a, b, sem):
    e = out.shape[1] // 4
    copies = []
    for r in range(2):
        for c in range(2):
            source = held.at[pl.ds(r * e, e), pl.ds(c * e, e)]
            target = out.at[0, spot(place, e, r, a), spot(place, e, c, b)]
            copies.append(pltpu.make_async_copy(source, target, sem.at[2 * r + c]))
            copies[-1].start()
    return copies


def wait(copies):
    for copy in copies:
        copy.wait()


def pick(ref, b):
    e = ref.shape[1] // 3
    return jnp.concatenate([ref[:, :e], ref[:, (1 + b) * e : (2 + b) * e]], axis=1)


def rows_kernel(
    place, leaf, high, low, a0, c01, c02, a1, c11, third, swapped, rest, out, top, bottom, part, col, own, held, sem
):
    e = leaf.shape[1] // 4
    n_sym = symmetric_tiles(e)
    ext, _ = sides(place)
    fetch = []
    for r in range(2):
        for c in range(2):
            target = own.at[pl.ds(r * e, e), pl.ds(c * e, e)]
            source = leaf_block(leaf, ext[r], ext[c], 0, 0, e)
            fetch.append(pltpu.make_async_copy(source, target, sem.at[3, 2 * r + c]))
            fetch[-1].start()
    same = place[0] == place[1]
    mine = cross_block((a0, n_sym), (c01, 0), (c02, 0))
    left = split(times_inverse(mine, high[...], low[...], slice(e, 2 * e)))
    top[...], bottom[...] = left
    left = [[pick(x, b) for x in left] for b in range(2)]
    wait(fetch)

    @pl.when(same)
    def _():
        right = split(mine)
        held[0] = own[...] - dot3(left[0], right, NT)
        copies = put(out, place, held.at[0], 0, 0, sem.at[0])
        across = cross_block((a1, n_sym), (c11, 0), (third, 0))
        other = split(across)
        held[1] = -dot3(left[1], other, NT)
        copies += put(out, place, held.at[1], 0, 1, sem.at[1])
        value = times_inverse(across, high[...], low[...], slice(2 * e, 3 * e))
        held[2] = -dot3(split(pick(value, 0)), right, NT)
        copies += put(out, place, held.at[2], 1, 0, sem.at[2])
        part[:, : 2 * e] = -dot3(split(pick(value, 1)), other, NT)
        wait(copies)

    @pl.when(jnp.logical_not(same))
    def _():
        col[...] = cross_block((swapped, n_sym), (rest, 0))
        held[0] = -dot3(left[0], split(col[...]), NT)
        copies = put(out, place, held.at[0], 0, 0, sem.at[0])
        across = cross_block((a1, n_sym), (c11, 0), zeros(third.shape[0] // T))
        part[...] = times_inverse(across, high[...], low[...], slice(2 * e, 3 * e))
        wait(copies)


def first_rows(place, leaf, high, low, mine, across, swapped, rest):
    e = leaf.shape[1] // 4
    block = pltpu.VMEM((2 * e, 2 * e), F32)
    return call(
        rows_kernel,
        "first_rows",
        500 * 10**6,
        [(leaf.shape, F32)] + [((2 * e, 3 * e), BF16)] * 2 + [((2 * e, 3 * e), F32)],
        [(SMEM, place), (HBM, leaf)]
        + [(VMEM, x) for x in (high, low, *mine, *across, swapped, rest)],
        [block, block, pltpu.VMEM((3, 2 * e, 2 * e), F32), pltpu.SemaphoreType.DMA((4, 4))],
        out_specs=[HBM] + [VMEM] * 3,
    )


def corner_kernel(place, before, top, bottom, a3, c31, passed, out, held, sem):
    n_sym = symmetric_tiles(out.shape[1] // 4)

    @pl.when(place[0] != place[1])
    def _():
        right = split(cross_block((a3, n_sym), (c31, 0), (passed, 0)))
        held[...] = -dot3([pick(x, 1) for x in (top, bottom)], right, NT)
        wait(put(out, place, held, 0, 1, sem))


def corner_block(place, before, top, bottom, a3, c31, passed):
    e = before.shape[1] // 4
    return call(
        corner_kernel,
        "corner_block",
        500 * 10**6,
        [(before.shape, F32)],
        [(SMEM, place), (HBM, before)] + [(VMEM, x) for x in (top, bottom, a3, c31, passed)],
        [pltpu.VMEM((2 * e, 2 * e), F32), pltpu.SemaphoreType.DMA((4,))],
        out_specs=[HBM],
        input_output_aliases={1: 0},
    )[0]


def finish_kernel(
    place, before, high, low, part, passed, last, swapped, rest, a3, c31, out, held, scratch, sem
):
    e = out.shape[1] // 4
    tiles = e // T
    n_sym = symmetric_tiles(e)
    n_last = last.shape[0] // T

    @pl.when(place[0] == place[1])
    def _():
        for at, (i, j) in enumerate(upper(2 * tiles)):
            ref, at = (last, at) if at < n_last else (passed, at - n_last)
            piece = ref[at * T : (at + 1) * T, :]
            r, c = slice(i * T, (i + 1) * T), slice(j * T, (j + 1) * T)
            held[0, r, c] = part[r, c] + piece
            if i != j:
                held[0, c, r] = part[c, r] + piece.T
        wait(put(out, place, held.at[0], 1, 1, sem.at[0]))

    @pl.when(place[0] != place[1])
    def _():
        late = cross_block(zeros(FIRST + SECOND), (last, 0))[:, e:]
        inner = slice(2 * e, 3 * e)
        start = (2 * tiles * tiles - n_last) // tiles * T
        scratch[:start, :] = part[:start, :]
        scratch[start:, :] = part[start:, :] + dot3(split(late[start:]), (high[inner], low[inner]))
        copies = []
        for b in range(2):
            if b == 0:
                col = cross_block((swapped, n_sym), (rest, 0))
            else:
                col = cross_block((a3, n_sym), (c31, 0), (passed, 0))
            held[b] = -dot3(split(pick(scratch, b)), split(col), NT)
            copies += put(out, place, held.at[b], 1, b, sem.at[b])
        wait(copies)


def finish(place, before, high, low, part, passed, last, swapped, rest, a3, c31):
    e = before.shape[1] // 4
    return call(
        finish_kernel,
        "finish",
        500 * 10**6,
        [(before.shape, F32)],
        [(SMEM, place), (HBM, before)]
        + [(VMEM, x) for x in (high, low, part, passed, last, swapped, rest, a3, c31)],
        [
            pltpu.VMEM((2, 2 * e, 2 * e), F32),
            pltpu.VMEM((2 * e, 3 * e), F32),
            pltpu.SemaphoreType.DMA((2, 4)),
        ],
        out_specs=[HBM],
        input_output_aliases={1: 0},
    )[0]


def tie(*values):
    return lax.optimization_barrier(values)


def solution(mesh):
    nx, ny = mesh.shape["gx"], mesh.shape["gy"]
    devices = [(x, y) for x in range(nx) for y in range(ny)]

    def is_same(x, y):
        return x // (nx // 2) == y // (ny // 2)

    def send(value, along_y, only=None):
        pairs = []
        for x, y in devices:
            if only is None or is_same(x, y) == only:
                to = (x, (y + ny // 2) % ny) if along_y else ((x + nx // 2) % nx, y)
                pairs.append((x * ny + y, to[0] * ny + to[1]))
        return lax.ppermute(value, ("gx", "gy"), pairs)

    def body(leaf):
        e = leaf.shape[1] // 4
        v = lax.axis_index("gx") // (nx // 2)
        u = lax.axis_index("gy") // (ny // 2)
        place = jnp.stack([v, u]).astype(jnp.int32)
        same = u == v
        a = cut_first(place, leaf)
        a_x = send(a, False)
        here, a = tie(place, a)
        hh = cut_side(here, leaf)
        hh_y = send(hh, True)
        swap, outer0, b, c = cut_second(place, leaf)
        swapped = send(swap, True)
        b, factor = gauge(hh, hh_y, b)
        b_x = send(b, False)
        n_last = outer0.shape[0] // T
        c1, c2, rest = scale_cross(factor, c, n_last)
        b, a_x, c1, swapped = tie(b, a_x, c1, swapped)
        b_y = send(b, True)
        a_x, b_y = tie(a_x, b_y)
        a_d = send(a_x, True)
        c1, b_x = tie(c1, b_x)
        c1_x = send(c1, False)
        b_x, b_y = tie(b_x, b_y)
        b_d = send(b_x, True)
        rest, b_d = tie(rest, b_d)
        rest = send(rest, True, only=True)
        side = factor_start((a, a_x, swapped, a_d), (b, b_x, b_y, b_d))
        third, side = tie(jnp.where(same, swapped[-n_last * T :], c2), side)
        third = send(third, False)
        c1_d = send(c1_x, True, only=True)
        high, low = factor_end(place, side, (b, b_x, b_y, b_d))
        last, third, high = tie(jnp.where(same, c2, outer0), third, high)
        last = send(last, False)
        passed = send(third, True)
        out, top, bottom, part = first_rows(
            place, leaf, high, low, (a, c1, c2), (a_x, c1_x, third), swapped, rest
        )
        out = corner_block(place, out, top, bottom, a_d, c1_d, passed)
        return finish(place, out, high, low, part, passed, last, swapped, rest, a_d, c1_d)

    return jax.shard_map(
        body,
        mesh=mesh,
        in_specs=(P(None, "gy", "gx"),),
        out_specs=P(None, "gy", "gx"),
        check_vma=False,
    )
```

```python
import math

import jax
import jax.numpy as jnp
from jax import lax
from jax.experimental import pallas as pl
from jax.experimental.pallas import tpu as pltpu
from jax.sharding import PartitionSpec as P

F32 = jnp.float32
BF16 = jnp.bfloat16
T = 128
R = 16
FIRST = 1
SECOND = 10
HBM = pl.BlockSpec(memory_space=pl.ANY)
FAR = pl.BlockSpec(memory_space=pltpu.HBM)
VMEM = pl.BlockSpec(memory_space=pltpu.VMEM)
SMEM = pl.BlockSpec(memory_space=pltpu.SMEM)


def dot(a, b, dims=((1,), (0,))):
    return lax.dot_general(
        a, b, (dims, ((), ())), precision=lax.Precision.HIGHEST, preferred_element_type=F32
    )


def dot16(a, b, dims=((1,), (0,))):
    return lax.dot_general(a, b, (dims, ((), ())), preferred_element_type=F32)


def split(a):
    high = a.astype(BF16)
    return high, (a - high.astype(F32)).astype(BF16)


def dot3(a, b, dims=((1,), (0,))):
    return dot16(a[0], b[0], dims) + (dot16(a[0], b[1], dims) + dot16(a[1], b[0], dims))


NT = ((1,), (1,))
TN = ((0,), (0,))


def upper(n):
    return [(i, j) for i in range(n) for j in range(i, n)]


def across_lanes(x, k):
    return jnp.broadcast_to(x[:, k : k + 1], x.shape)


def across_rows(x, k):
    return jnp.broadcast_to(x[k : k + 1, :], x.shape)


def panel(rows, c0, lower):
    sub = lax.broadcasted_iota(jnp.int32, rows.shape, 0)
    lane = lax.broadcasted_iota(jnp.int32, rows.shape, 1)
    cols = [across_lanes(rows, c0 + k) for k in range(R)]
    out = jnp.where((lane >= c0) & (lane < c0 + R), (lane - c0 == sub).astype(F32), rows)
    half = out
    scale = jnp.ones_like(rows)
    for k in range(R):
        pivot = across_rows(cols[k], k)
        inv = 1.0 / pivot
        here = sub == k
        mult = cols[k]

        def step(x):
            row = across_rows(x, k) * inv
            return jnp.where(here, row, x - mult * row)

        if lower:
            scale = jnp.where(here, pivot, scale)
            half = half - jnp.where(sub > k, mult, 0.0) * (across_rows(half, k) * inv)
        out = step(out)
        for j in range(k + 1, R):
            cols[j] = step(cols[j])
    return out, half * lax.rsqrt(scale) if lower else None


def put_rows(matrix, rows, r0):
    parts = [matrix[:r0]] if r0 else []
    parts.append(rows)
    if r0 + rows.shape[0] < matrix.shape[0]:
        parts.append(matrix[r0 + rows.shape[0] :])
    return jnp.concatenate(parts, axis=0)


def invert_tile(m, lower=False):
    lane = lax.broadcasted_iota(jnp.int32, (T, T), 1)
    sub = lax.broadcasted_iota(jnp.int32, (T, T), 0)
    rows = m[:R]
    for c0 in range(0, T, R):
        swept, half = panel(rows, c0, lower)
        if c0 + R < T:
            old = m[c0 + R : c0 + 2 * R]
            inside = (lane[:R] >= c0) & (lane[:R] < c0 + R)
            rows = jnp.where(inside, 0.0, old)
            for k in range(R):
                rows = rows - across_lanes(old, c0 + k) * across_rows(swept, k)
        wide = put_rows(jnp.zeros((T, T), F32), swept, c0)
        rest = jnp.where((lane >= c0) & (lane < c0 + R), 0.0, m) - dot(m, wide)
        if lower:
            rest = jnp.where(sub < c0, m, rest)
        m = put_rows(rest, half if lower else swept, c0)
    return jnp.where(lane > sub, 0.0, m) if lower else m


def sweep(ref, start, stop):
    n = ref.shape[0]
    for p in range(start, stop, T):
        pivot = invert_tile(ref[p : p + T, p : p + T])
        rows = dot(pivot, ref[p : p + T, :])
        parts = ([rows[:, :p]] if p else []) + [pivot]
        if p + T < n:
            parts.append(rows[:, p + T :])
        rows = jnp.concatenate(parts, axis=1)
        for q in range(0, n, T):
            if q != p:
                change = dot(ref[q : q + T, p : p + T], rows)
                ref[q : q + T, p : p + T] = jnp.zeros((T, T), F32)
                ref[q : q + T, :] = ref[q : q + T, :] - change
        ref[p : p + T, :] = rows


def inverse_factor(ref):
    n = ref.shape[0]
    for p in range(0, n, T):
        pivot = invert_tile(ref[p : p + T, p : p + T], lower=True)
        scaled = dot(pivot, ref[p : p + T, :])
        for q in range(p + T, n, T):
            weight = scaled[:, q : q + T]
            ref[q : q + T, :] = ref[q : q + T, :] - dot(weight, scaled, TN)
            ref[q : q + T, p : p + T] = -dot(weight, pivot, TN)
        for q in range(0, n, T):
            if q < p:
                ref[p : p + T, q : q + T] = scaled[:, q : q + T]
            else:
                ref[p : p + T, q : q + T] = pivot if q == p else jnp.zeros((T, T), F32)


def leaf_block(leaf, side_r, side_c, r, c, size):
    e = leaf.shape[1] // 4
    return leaf.at[
        0,
        pl.ds(pl.multiple_of(side_r * e + r * size, T), size),
        pl.ds(pl.multiple_of(side_c * e + c * size, T), size),
    ]


def run_copies(pairs, sem):
    copies = [pltpu.make_async_copy(a, b, sem.at[i]) for i, (a, b) in enumerate(pairs)]
    for copy in copies:
        copy.start()
    for copy in copies:
        copy.wait()


def sides(place):
    v, u = place[0], place[1]
    return [v, 2 + u], [1 - v, 3 - u]


def unpack(ref, at, tiles):
    held = {}
    for r, c in upper(tiles):
        held[r, c] = ref[at : at + T, :]
        if c > r:
            held[c, r] = held[r, c].T
        at += T
    return jnp.concatenate(
        [jnp.concatenate([held[r, c] for c in range(tiles)], axis=1) for r in range(tiles)], axis=0
    )


def call(kernel, name, cost, outs, ins, scratch, **more):
    return pl.pallas_call(
        kernel,
        out_shape=[jax.ShapeDtypeStruct(shape, dtype) for shape, dtype in outs],
        in_specs=[spec for spec, _ in ins],
        out_specs=more.pop("out_specs", [VMEM] * len(outs)),
        scratch_shapes=scratch,
        compiler_params=pltpu.CompilerParams(vmem_limit_bytes=32 * 2**20),
        cost_estimate=pl.CostEstimate(flops=cost, bytes_accessed=cost, transcendentals=0),
        name=name,
        **more,
    )(*[value for _, value in ins])


def block_tiles(leaf, side_r, side_c, at):
    tiles = leaf.shape[1] // 4 // T
    return leaf_block(leaf, side_r, side_c, at // tiles, at % tiles, T)


def cross_tile(leaf, ext, inn, at):
    n = (leaf.shape[1] // 4 // T) ** 2
    return block_tiles(leaf, ext[at // n % 2], inn[at // n // 2], at % n)


def cut_first_kernel(place, leaf, a, sem):
    tiles = leaf.shape[1] // 4 // T
    ext, inn = sides(place)
    n_sym = len(upper(tiles))
    pairs = []
    for at, (r, c) in enumerate(upper(tiles)):
        pairs.append((leaf_block(leaf, inn[0], inn[0], r, c, T), a.at[pl.ds(at * T, T)]))
    for at in range(FIRST):
        pairs.append(
            (cross_tile(leaf, ext, inn, at), a.at[pl.ds((n_sym + at) * T, T)])
        )
    run_copies(pairs, sem)


def cut_first(place, leaf):
    n_sym = len(upper(leaf.shape[1] // 4 // T))
    return call(
        cut_first_kernel,
        "cut_first",
        1000 * 10**6,
        [(((n_sym + FIRST) * T, T), F32)],
        [(SMEM, place), (FAR, leaf)],
        [pltpu.SemaphoreType.DMA((n_sym + FIRST,))],
    )[0]


def cut_side_kernel(place, leaf, hh, sem):
    tiles = leaf.shape[1] // 4 // T
    _, inn = sides(place)
    pairs = []
    for at, (r, c) in enumerate(upper(tiles)):
        pairs.append((leaf_block(leaf, inn[1], inn[1], r, c, T), hh.at[pl.ds(at * T, T)]))
    run_copies(pairs, sem)


def cut_side(place, leaf):
    n_sym = len(upper(leaf.shape[1] // 4 // T))
    return call(
        cut_side_kernel,
        "cut_side",
        1000 * 10**6,
        [((n_sym * T, T), F32)],
        [(SMEM, place), (FAR, leaf)],
        [pltpu.SemaphoreType.DMA((n_sym,))],
    )[0]


def cut_second_kernel(place, leaf, swap, outer0, b, c, sem):
    e = leaf.shape[1] // 4
    tiles = e // T
    ext, inn = sides(place)
    n_sym = len(upper(tiles))
    pairs = [
        (leaf_block(leaf, inn[0], inn[1], 0, 0, e), b),
        (leaf_block(leaf, ext[0], inn[0], 0, 0, e), c.at[pl.ds(0, e)]),
        (leaf_block(leaf, ext[1], inn[0], 0, 0, e), c.at[pl.ds(e, e)]),
        (leaf_block(leaf, ext[0], inn[1], 0, 0, e), c.at[pl.ds(2 * e, e)]),
        (leaf_block(leaf, ext[1], inn[1], 0, 0, e), c.at[pl.ds(3 * e, e)]),
    ]
    for at, (r, k) in enumerate(upper(tiles)):
        pairs.append((leaf_block(leaf, inn[0], inn[0], r, k, T), swap.at[pl.ds(at * T, T)]))
    half = outer0.shape[0] // T
    second = []
    for at, (r, k) in enumerate(upper(2 * tiles)):
        source = leaf_block(leaf, ext[r // tiles], ext[k // tiles], r % tiles, k % tiles, T)
        if at < half:
            pairs.append((source, outer0.at[pl.ds(at * T, T)]))
        else:
            second.append((source, swap.at[pl.ds((n_sym + at - half) * T, T)]))
    run_copies(pairs, sem)
    same = place[0] == place[1]

    @pl.when(same)
    def _():
        cross = [
            (cross_tile(leaf, ext, inn, at), swap.at[pl.ds((n_sym + at) * T, T)])
            for at in range(half)
        ]
        run_copies(cross, sem)

    @pl.when(jnp.logical_not(same))
    def _():
        run_copies(second, sem)


def cut_second(place, leaf):
    e = leaf.shape[1] // 4
    n_sym = len(upper(e // T))
    half = len(upper(2 * (e // T))) // 2
    return call(
        cut_second_kernel,
        "cut_second",
        1000 * 10**6,
        [(((n_sym + half) * T, T), F32), ((half * T, T), F32), ((e, e), F32), ((4 * e, e), F32)],
        [(SMEM, place), (HBM, leaf)],
        [pltpu.SemaphoreType.DMA((n_sym + half + 5,))],
    )


def gauge_kernel(mine, along, b, b_out, factor):
    e = factor.shape[0]
    tiles = e // T
    factor[...] = unpack(mine, 0, tiles) + unpack(along, 0, tiles)
    inverse_factor(factor)
    b_out[...] = dot(b[...], factor[...], NT)


def gauge(mine, along, b):
    e = b.shape[0]
    return call(
        gauge_kernel,
        "gauge_side",
        8000 * 10**6,
        [((e, e), F32), ((e, e), F32)],
        [(VMEM, x) for x in (mine, along, b)],
        [],
    )


def scale_kernel(factor, c, c1, c2, rest):
    e = factor.shape[0]
    tiles = e // T
    scaled = dot3(split(c[2 * e :, :]), split(factor[...]), NT)
    total = 4 * tiles * tiles
    for at in range(FIRST, total):
        r, k = at // tiles * T, at % tiles * T
        tile = c[r : r + T, k : k + T] if r < 2 * e else scaled[r - 2 * e : r - 2 * e + T, k : k + T]
        if at < FIRST + SECOND:
            c1[(at - FIRST) * T : (at - FIRST + 1) * T, :] = tile
        else:
            c2[(at - FIRST - SECOND) * T : (at - FIRST - SECOND + 1) * T, :] = tile
        spot = at * T - (total * T - rest.shape[0])
        if spot >= 0:
            rest[spot : spot + T, :] = tile


def scale_cross(factor, c, swapped):
    e = factor.shape[0]
    total = 4 * e * e // T
    return call(
        scale_kernel,
        "scale_cross",
        2000 * 10**6,
        [((n, T), F32) for n in (SECOND * T, total - (FIRST + SECOND) * T, total - swapped * T)],
        [(VMEM, x) for x in (factor, c)],
        [],
    )


def couple(b):
    mine, across, along, corner = (ref[...] for ref in b)
    return jnp.concatenate(
        [jnp.concatenate([mine, across], axis=1), jnp.concatenate([along, corner], axis=1)], axis=0
    )


def factor_start_kernel(a0, a1, a2, a3, b0, b1, b2, b3, side):
    e = b0.shape[0]
    tiles = e // T
    coup = couple((b0, b1, b2, b3))
    side[...] = -dot(coup, coup, NT)
    side[:e, :e] = side[:e, :e] + (unpack(a0, 0, tiles) + unpack(a1, 0, tiles))
    side[e:, e:] = side[e:, e:] + (unpack(a2, 0, tiles) + unpack(a3, 0, tiles))
    sweep(side, 0, e)


def factor_start(a, b):
    e = b[0].shape[0]
    return call(
        factor_start_kernel,
        "factor_start",
        3500 * 10**6,
        [((2 * e, 2 * e), F32)],
        [(VMEM, x) for x in (*a, *b)],
        [],
    )[0]


def factor_middle_kernel(before, side):
    side[...] = before[...]
    half = side.shape[0] // 2
    sweep(side, half, half + T)


def factor_middle(side):
    return call(
        factor_middle_kernel,
        "factor_middle",
        4000 * 10**6,
        [(side.shape, F32)],
        [(VMEM, side)],
        [],
    )[0]


def factor_end_kernel(place, side_in, b0, b1, b2, b3, high, low, side, full):
    e = b0.shape[0]
    side[...] = side_in[...]
    sweep(side, e + T, 2 * e)
    coup = split(couple((b0, b1, b2, b3)))
    away = dot3(split(side[...]), coup)
    shape = full.shape
    unit = lax.broadcasted_iota(jnp.int32, shape, 0) == lax.broadcasted_iota(jnp.int32, shape, 1)
    full[...] = dot3(coup, split(away), TN) + unit.astype(F32)

    def emit(value, rows, columns):
        high[rows, columns], low[rows, columns] = split(value)

    first, rest = slice(0, e), slice(e, 3 * e)
    emit(full[...], rest, rest)
    emit(-away[:e, :], first, rest)
    same = place[0] == place[1]

    @pl.when(same)
    def _():
        emit(side[:e, :e], first, first)
        emit(-away[:e, :].T, rest, first)

    @pl.when(jnp.logical_not(same))
    def _():
        emit(side[:e, e:], first, first)
        emit(-away[e:, :].T, rest, first)


def factor_end(place, side, b):
    e = b[0].shape[0]
    return call(
        factor_end_kernel,
        "factor_end",
        3000 * 10**6,
        [((3 * e, 3 * e), BF16)] * 2,
        [(SMEM, place), (VMEM, side)] + [(VMEM, x) for x in b],
        [pltpu.VMEM((2 * e, 2 * e), F32), pltpu.VMEM((2 * e, 2 * e), F32)],
    )


def cross_block(*pieces):
    held = []
    for ref, skip in pieces:
        for at in range(skip * T, ref.shape[0], T):
            held.append(ref[at : at + T, :])
    tiles = math.isqrt(len(held) // 4)
    rows = []
    for r in range(2 * tiles):
        side = r // tiles
        row = [held[((side + 2 * c) * tiles + r % tiles) * tiles + k] for c in range(2) for k in range(tiles)]
        rows.append(jnp.concatenate(row, axis=1))
    return jnp.concatenate(rows, axis=0)


def symmetric_tiles(e):
    return len(upper(e // T))


def zeros(tiles):
    return jnp.zeros((tiles * T, T), F32), 0


def times_inverse(cross, high, low, inner):
    e = cross.shape[1] // 2
    return dot3(split(cross[:, :e]), (high[:e], low[:e])) + dot3(
        split(cross[:, e:]), (high[inner], low[inner])
    )


def spot(place, e, side, which):
    x = place[0] if which == 0 else 1 - place[0]
    return pl.ds(pl.multiple_of((2 * side + x) * e, T), e)


def put(out, place, held, a, b, sem):
    e = out.shape[1] // 4
    copies = []
    for r in range(2):
        for c in range(2):
            source = held.at[pl.ds(r * e, e), pl.ds(c * e, e)]
            target = out.at[0, spot(place, e, r, a), spot(place, e, c, b)]
            copies.append(pltpu.make_async_copy(source, target, sem.at[2 * r + c]))
            copies[-1].start()
    return copies


def wait(copies):
    for copy in copies:
        copy.wait()


def pick(ref, b):
    e = ref.shape[1] // 3
    return jnp.concatenate([ref[:, :e], ref[:, (1 + b) * e : (2 + b) * e]], axis=1)


def rows_kernel(
    place, leaf, high, low, a0, c01, c02, a1, c11, third, swapped, rest, out, top, bottom, part, col, own, held, sem
):
    e = leaf.shape[1] // 4
    n_sym = symmetric_tiles(e)
    ext, _ = sides(place)
    fetch = []
    for r in range(2):
        for c in range(2):
            target = own.at[pl.ds(r * e, e), pl.ds(c * e, e)]
            source = leaf_block(leaf, ext[r], ext[c], 0, 0, e)
            fetch.append(pltpu.make_async_copy(source, target, sem.at[3, 2 * r + c]))
            fetch[-1].start()
    same = place[0] == place[1]
    mine = cross_block((a0, n_sym), (c01, 0), (c02, 0))
    left = split(times_inverse(mine, high[...], low[...], slice(e, 2 * e)))
    top[...], bottom[...] = left
    left = [[pick(x, b) for x in left] for b in range(2)]
    wait(fetch)

    @pl.when(same)
    def _():
        right = split(mine)
        held[0] = own[...] - dot3(left[0], right, NT)
        copies = put(out, place, held.at[0], 0, 0, sem.at[0])
        across = cross_block((a1, n_sym), (c11, 0), (third, 0))
        other = split(across)
        held[1] = -dot3(left[1], other, NT)
        copies += put(out, place, held.at[1], 0, 1, sem.at[1])
        value = times_inverse(across, high[...], low[...], slice(2 * e, 3 * e))
        held[2] = -dot3(split(pick(value, 0)), right, NT)
        copies += put(out, place, held.at[2], 1, 0, sem.at[2])
        part[:, : 2 * e] = -dot3(split(pick(value, 1)), other, NT)
        wait(copies)

    @pl.when(jnp.logical_not(same))
    def _():
        col[...] = cross_block((swapped, n_sym), (rest, 0))
        held[0] = -dot3(left[0], split(col[...]), NT)
        copies = put(out, place, held.at[0], 0, 0, sem.at[0])
        across = cross_block((a1, n_sym), (c11, 0), zeros(third.shape[0] // T))
        part[...] = times_inverse(across, high[...], low[...], slice(2 * e, 3 * e))
        wait(copies)


def first_rows(place, leaf, high, low, mine, across, swapped, rest):
    e = leaf.shape[1] // 4
    block = pltpu.VMEM((2 * e, 2 * e), F32)
    return call(
        rows_kernel,
        "first_rows",
        500 * 10**6,
        [(leaf.shape, F32)] + [((2 * e, 3 * e), BF16)] * 2 + [((2 * e, 3 * e), F32)],
        [(SMEM, place), (HBM, leaf)]
        + [(VMEM, x) for x in (high, low, *mine, *across, swapped, rest)],
        [block, block, pltpu.VMEM((3, 2 * e, 2 * e), F32), pltpu.SemaphoreType.DMA((4, 4))],
        out_specs=[HBM] + [VMEM] * 3,
    )


def corner_kernel(place, before, top, bottom, a3, c31, passed, out, held, sem):
    n_sym = symmetric_tiles(out.shape[1] // 4)

    @pl.when(place[0] != place[1])
    def _():
        right = split(cross_block((a3, n_sym), (c31, 0), (passed, 0)))
        held[...] = -dot3([pick(x, 1) for x in (top, bottom)], right, NT)
        wait(put(out, place, held, 0, 1, sem))


def corner_block(place, before, top, bottom, a3, c31, passed):
    e = before.shape[1] // 4
    return call(
        corner_kernel,
        "corner_block",
        500 * 10**6,
        [(before.shape, F32)],
        [(SMEM, place), (HBM, before)] + [(VMEM, x) for x in (top, bottom, a3, c31, passed)],
        [pltpu.VMEM((2 * e, 2 * e), F32), pltpu.SemaphoreType.DMA((4,))],
        out_specs=[HBM],
        input_output_aliases={1: 0},
    )[0]


def finish_kernel(
    place, before, high, low, part, passed, last, swapped, rest, a3, c31, out, held, scratch, sem
):
    e = out.shape[1] // 4
    tiles = e // T
    n_sym = symmetric_tiles(e)
    n_last = last.shape[0] // T

    @pl.when(place[0] == place[1])
    def _():
        for at, (i, j) in enumerate(upper(2 * tiles)):
            ref, at = (last, at) if at < n_last else (passed, at - n_last)
            piece = ref[at * T : (at + 1) * T, :]
            r, c = slice(i * T, (i + 1) * T), slice(j * T, (j + 1) * T)
            held[0, r, c] = part[r, c] + piece
            if i != j:
                held[0, c, r] = part[c, r] + piece.T
        wait(put(out, place, held.at[0], 1, 1, sem.at[0]))

    @pl.when(place[0] != place[1])
    def _():
        late = cross_block(zeros(FIRST + SECOND), (last, 0))[:, e:]
        inner = slice(2 * e, 3 * e)
        start = (2 * tiles * tiles - n_last) // tiles * T
        scratch[:start, :] = part[:start, :]
        scratch[start:, :] = part[start:, :] + dot3(split(late[start:]), (high[inner], low[inner]))
        copies = []
        for b in range(2):
            if b == 0:
                col = cross_block((swapped, n_sym), (rest, 0))
            else:
                col = cross_block((a3, n_sym), (c31, 0), (passed, 0))
            held[b] = -dot3(split(pick(scratch, b)), split(col), NT)
            copies += put(out, place, held.at[b], 1, b, sem.at[b])
        wait(copies)


def finish(place, before, high, low, part, passed, last, swapped, rest, a3, c31):
    e = before.shape[1] // 4
    return call(
        finish_kernel,
        "finish",
        500 * 10**6,
        [(before.shape, F32)],
        [(SMEM, place), (HBM, before)]
        + [(VMEM, x) for x in (high, low, part, passed, last, swapped, rest, a3, c31)],
        [
            pltpu.VMEM((2, 2 * e, 2 * e), F32),
            pltpu.VMEM((2 * e, 3 * e), F32),
            pltpu.SemaphoreType.DMA((2, 4)),
        ],
        out_specs=[HBM],
        input_output_aliases={1: 0},
    )[0]


def tie(*values):
    return lax.optimization_barrier(values)


def solution(mesh):
    nx, ny = mesh.shape["gx"], mesh.shape["gy"]
    devices = [(x, y) for x in range(nx) for y in range(ny)]

    def is_same(x, y):
        return x // (nx // 2) == y // (ny // 2)

    def send(value, along_y, only=None):
        pairs = []
        for x, y in devices:
            if only is None or is_same(x, y) == only:
                to = (x, (y + ny // 2) % ny) if along_y else ((x + nx // 2) % nx, y)
                pairs.append((x * ny + y, to[0] * ny + to[1]))
        return lax.ppermute(value, ("gx", "gy"), pairs)

    def body(leaf):
        e = leaf.shape[1] // 4
        v = lax.axis_index("gx") // (nx // 2)
        u = lax.axis_index("gy") // (ny // 2)
        place = jnp.stack([v, u]).astype(jnp.int32)
        same = u == v
        a = cut_first(place, leaf)
        a_x = send(a, False)
        here, a = tie(place, a)
        hh = cut_side(here, leaf)
        hh_y = send(hh, True)
        swap, outer0, b, c = cut_second(place, leaf)
        swapped = send(swap, True)
        b, factor = gauge(hh, hh_y, b)
        b_x = send(b, False)
        n_last = outer0.shape[0] // T
        c1, c2, rest = scale_cross(factor, c, n_last)
        b, a_x, c1, swapped = tie(b, a_x, c1, swapped)
        b_y = send(b, True)
        a_d = send(a_x, True)
        c1, b_x = tie(c1, b_x)
        c1_x = send(c1, False)
        b_x, b_y, a_d = tie(b_x, b_y, a_d)
        b_d = send(b_x, True)
        rest, b_d = tie(rest, b_d)
        rest = send(rest, True, only=True)
        side = factor_start((a, a_x, swapped, a_d), (b, b_x, b_y, b_d))
        side = factor_middle(side)
        third, side = tie(jnp.where(same, swapped[-n_last * T :], c2), side)
        third = send(third, False)
        c1_x, side = tie(c1_x, side)
        c1_d = send(c1_x, True, only=True)
        high, low = factor_end(place, side, (b, b_x, b_y, b_d))
        last, third, high = tie(jnp.where(same, c2, outer0), third, high)
        last = send(last, False)
        passed = send(third, True)
        out, top, bottom, part = first_rows(
            place, leaf, high, low, (a, c1, c2), (a_x, c1_x, third), swapped, rest
        )
        out = corner_block(place, out, top, bottom, a_d, c1_d, passed)
        return finish(place, out, high, low, part, passed, last, swapped, rest, a_d, c1_d)

    return jax.shard_map(
        body,
        mesh=mesh,
        in_specs=(P(None, "gy", "gx"),),
        out_specs=P(None, "gy", "gx"),
        check_vma=False,
    )
```

```python
import functools
import math

import jax
import jax.numpy as jnp
from jax import lax
from jax.experimental import pallas as pl
from jax.experimental.pallas import tpu as pltpu
from jax.sharding import PartitionSpec as P

F32 = jnp.float32
BF16 = jnp.bfloat16
T = 128
R = 16
FIRST = 1
SECOND = 9
HBM = pl.BlockSpec(memory_space=pl.ANY)
FAR = pl.BlockSpec(memory_space=pltpu.HBM)
VMEM = pl.BlockSpec(memory_space=pltpu.VMEM)
SMEM = pl.BlockSpec(memory_space=pltpu.SMEM)


def dot(a, b, dims=((1,), (0,))):
    return lax.dot_general(
        a, b, (dims, ((), ())), precision=lax.Precision.HIGHEST, preferred_element_type=F32
    )


def dot16(a, b, dims=((1,), (0,))):
    return lax.dot_general(a, b, (dims, ((), ())), preferred_element_type=F32)


def split(a):
    high = a.astype(BF16)
    return high, (a - high.astype(F32)).astype(BF16)


def dot3(a, b, dims=((1,), (0,))):
    return dot16(a[0], b[0], dims) + (dot16(a[0], b[1], dims) + dot16(a[1], b[0], dims))


NT = ((1,), (1,))
TN = ((0,), (0,))


def upper(n):
    return [(i, j) for i in range(n) for j in range(i, n)]


def across_lanes(x, k):
    return jnp.broadcast_to(x[:, k : k + 1], x.shape)


def across_rows(x, k):
    return jnp.broadcast_to(x[k : k + 1, :], x.shape)


def panel(rows, c0, lower):
    sub = lax.broadcasted_iota(jnp.int32, rows.shape, 0)
    lane = lax.broadcasted_iota(jnp.int32, rows.shape, 1)
    cols = [across_lanes(rows, c0 + k) for k in range(R)]
    out = jnp.where((lane >= c0) & (lane < c0 + R), (lane - c0 == sub).astype(F32), rows)
    half = out
    scale = jnp.ones_like(rows)
    for k in range(R):
        pivot = across_rows(cols[k], k)
        inv = 1.0 / pivot
        here = sub == k
        mult = cols[k]

        def step(x):
            row = across_rows(x, k) * inv
            return jnp.where(here, row, x - mult * row)

        if lower:
            scale = jnp.where(here, pivot, scale)
            half = half - jnp.where(sub > k, mult, 0.0) * (across_rows(half, k) * inv)
        out = step(out)
        for j in range(k + 1, R):
            cols[j] = step(cols[j])
    return out, half * lax.rsqrt(scale) if lower else None


def put_rows(matrix, rows, r0):
    parts = [matrix[:r0]] if r0 else []
    parts.append(rows)
    if r0 + rows.shape[0] < matrix.shape[0]:
        parts.append(matrix[r0 + rows.shape[0] :])
    return jnp.concatenate(parts, axis=0)


def invert_tile(m, lower=False):
    lane = lax.broadcasted_iota(jnp.int32, (T, T), 1)
    sub = lax.broadcasted_iota(jnp.int32, (T, T), 0)
    rows = m[:R]
    for c0 in range(0, T, R):
        swept, half = panel(rows, c0, lower)
        if c0 + R < T:
            old = m[c0 + R : c0 + 2 * R]
            inside = (lane[:R] >= c0) & (lane[:R] < c0 + R)
            sums = [jnp.where(inside, 0.0, old)] + [None] * 3
            for k in range(R):
                term = across_lanes(old, c0 + k) * across_rows(swept, k)
                sums[k % 4] = -term if sums[k % 4] is None else sums[k % 4] - term
            rows = (sums[0] + sums[1]) + (sums[2] + sums[3])
        wide = put_rows(jnp.zeros((T, T), F32), swept, c0)
        rest = jnp.where((lane >= c0) & (lane < c0 + R), 0.0, m) - dot(m, wide)
        if lower:
            rest = jnp.where(sub < c0, m, rest)
        m = put_rows(rest, half if lower else swept, c0)
    return jnp.where(lane > sub, 0.0, m) if lower else m


def sweep(ref, start, stop):
    n = ref.shape[0]
    for p in range(start, stop, T):
        pivot = invert_tile(ref[p : p + T, p : p + T])
        rows = dot(pivot, ref[p : p + T, :])
        parts = ([rows[:, :p]] if p else []) + [pivot]
        if p + T < n:
            parts.append(rows[:, p + T :])
        rows = jnp.concatenate(parts, axis=1)
        for q in range(0, n, T):
            if q != p:
                change = dot(ref[q : q + T, p : p + T], rows)
                ref[q : q + T, p : p + T] = jnp.zeros((T, T), F32)
                ref[q : q + T, :] = ref[q : q + T, :] - change
        ref[p : p + T, :] = rows


def inverse_factor(ref):
    n = ref.shape[0]
    for p in range(0, n, T):
        pivot = invert_tile(ref[p : p + T, p : p + T], lower=True)
        scaled = dot(pivot, ref[p : p + T, :])
        for q in range(p + T, n, T):
            weight = scaled[:, q : q + T]
            ref[q : q + T, :] = ref[q : q + T, :] - dot(weight, scaled, TN)
            ref[q : q + T, p : p + T] = -dot(weight, pivot, TN)
        for q in range(0, n, T):
            if q < p:
                ref[p : p + T, q : q + T] = scaled[:, q : q + T]
            else:
                ref[p : p + T, q : q + T] = pivot if q == p else jnp.zeros((T, T), F32)


def leaf_block(leaf, side_r, side_c, r, c, size):
    e = leaf.shape[1] // 4
    return leaf.at[
        0,
        pl.ds(pl.multiple_of(side_r * e + r * size, T), size),
        pl.ds(pl.multiple_of(side_c * e + c * size, T), size),
    ]


def run_copies(pairs, sem):
    copies = [pltpu.make_async_copy(a, b, sem.at[i]) for i, (a, b) in enumerate(pairs)]
    for copy in copies:
        copy.start()
    for copy in copies:
        copy.wait()


def sides(place):
    v, u = place[0], place[1]
    return [v, 2 + u], [1 - v, 3 - u]


def unpack(ref, at, tiles):
    held = {}
    for r, c in upper(tiles):
        held[r, c] = ref[at : at + T, :]
        if c > r:
            held[c, r] = held[r, c].T
        at += T
    return jnp.concatenate(
        [jnp.concatenate([held[r, c] for c in range(tiles)], axis=1) for r in range(tiles)], axis=0
    )


def call(kernel, name, cost, outs, ins, scratch, **more):
    return pl.pallas_call(
        kernel,
        out_shape=[jax.ShapeDtypeStruct(shape, dtype) for shape, dtype in outs],
        in_specs=[spec for spec, _ in ins],
        out_specs=more.pop("out_specs", [VMEM] * len(outs)),
        scratch_shapes=scratch,
        compiler_params=pltpu.CompilerParams(vmem_limit_bytes=32 * 2**20),
        cost_estimate=pl.CostEstimate(flops=cost, bytes_accessed=cost, transcendentals=0),
        name=name,
        **more,
    )(*[value for _, value in ins])


def block_tiles(leaf, side_r, side_c, at):
    tiles = leaf.shape[1] // 4 // T
    return leaf_block(leaf, side_r, side_c, at // tiles, at % tiles, T)


def cross_tile(leaf, ext, inn, at):
    n = (leaf.shape[1] // 4 // T) ** 2
    return block_tiles(leaf, ext[at // n % 2], inn[at // n // 2], at % n)


def cut_first_kernel(place, leaf, a, sem):
    tiles = leaf.shape[1] // 4 // T
    ext, inn = sides(place)
    n_sym = len(upper(tiles))
    pairs = []
    for at, (r, c) in enumerate(upper(tiles)):
        pairs.append((leaf_block(leaf, inn[0], inn[0], r, c, T), a.at[pl.ds(at * T, T)]))
    for at in range(FIRST):
        pairs.append(
            (cross_tile(leaf, ext, inn, at), a.at[pl.ds((n_sym + at) * T, T)])
        )
    run_copies(pairs, sem)


def cut_first(place, leaf):
    n_sym = len(upper(leaf.shape[1] // 4 // T))
    return call(
        cut_first_kernel,
        "cut_first",
        1000 * 10**6,
        [(((n_sym + FIRST) * T, T), F32)],
        [(SMEM, place), (FAR, leaf)],
        [pltpu.SemaphoreType.DMA((n_sym + FIRST,))],
    )[0]


def cut_side_kernel(place, leaf, hh, sem):
    tiles = leaf.shape[1] // 4 // T
    _, inn = sides(place)
    pairs = []
    for at, (r, c) in enumerate(upper(tiles)):
        pairs.append((leaf_block(leaf, inn[1], inn[1], r, c, T), hh.at[pl.ds(at * T, T)]))
    run_copies(pairs, sem)


def cut_side(place, leaf):
    n_sym = len(upper(leaf.shape[1] // 4 // T))
    return call(
        cut_side_kernel,
        "cut_side",
        1000 * 10**6,
        [((n_sym * T, T), F32)],
        [(SMEM, place), (FAR, leaf)],
        [pltpu.SemaphoreType.DMA((n_sym,))],
    )[0]


def cut_second_kernel(place, leaf, swap, outer0, b, c, sem):
    e = leaf.shape[1] // 4
    tiles = e // T
    ext, inn = sides(place)
    n_sym = len(upper(tiles))
    pairs = [
        (leaf_block(leaf, inn[0], inn[1], 0, 0, e), b),
        (leaf_block(leaf, ext[0], inn[0], 0, 0, e), c.at[pl.ds(0, e)]),
        (leaf_block(leaf, ext[1], inn[0], 0, 0, e), c.at[pl.ds(e, e)]),
        (leaf_block(leaf, ext[0], inn[1], 0, 0, e), c.at[pl.ds(2 * e, e)]),
        (leaf_block(leaf, ext[1], inn[1], 0, 0, e), c.at[pl.ds(3 * e, e)]),
    ]
    for at, (r, k) in enumerate(upper(tiles)):
        pairs.append((leaf_block(leaf, inn[0], inn[0], r, k, T), swap.at[pl.ds(at * T, T)]))
    half = outer0.shape[0] // T
    second = []
    for at, (r, k) in enumerate(upper(2 * tiles)):
        source = leaf_block(leaf, ext[r // tiles], ext[k // tiles], r % tiles, k % tiles, T)
        if at < half:
            pairs.append((source, outer0.at[pl.ds(at * T, T)]))
        else:
            second.append((source, swap.at[pl.ds((n_sym + at - half) * T, T)]))
    run_copies(pairs, sem)
    same = place[0] == place[1]

    @pl.when(same)
    def _():
        cross = [
            (cross_tile(leaf, ext, inn, at), swap.at[pl.ds((n_sym + at) * T, T)])
            for at in range(half)
        ]
        run_copies(cross, sem)

    @pl.when(jnp.logical_not(same))
    def _():
        run_copies(second, sem)


def cut_second(place, leaf):
    e = leaf.shape[1] // 4
    n_sym = len(upper(e // T))
    half = len(upper(2 * (e // T))) // 2
    return call(
        cut_second_kernel,
        "cut_second",
        1000 * 10**6,
        [(((n_sym + half) * T, T), F32), ((half * T, T), F32), ((e, e), F32), ((4 * e, e), F32)],
        [(SMEM, place), (HBM, leaf)],
        [pltpu.SemaphoreType.DMA((n_sym + half + 5,))],
    )


def gauge_kernel(mine, along, b, b_out, factor):
    e = factor.shape[0]
    tiles = e // T
    factor[...] = unpack(mine, 0, tiles) + unpack(along, 0, tiles)
    inverse_factor(factor)
    b_out[...] = dot(b[...], factor[...], NT)


def gauge(mine, along, b):
    e = b.shape[0]
    return call(
        gauge_kernel,
        "gauge_side",
        8000 * 10**6,
        [((e, e), F32), ((e, e), F32)],
        [(VMEM, x) for x in (mine, along, b)],
        [],
    )


def scale_kernel(factor, c, c1, c2, rest):
    e = factor.shape[0]
    tiles = e // T
    scaled = dot3(split(c[2 * e :, :]), split(factor[...]), NT)
    total = 4 * tiles * tiles
    for at in range(FIRST, total):
        r, k = at // tiles * T, at % tiles * T
        tile = c[r : r + T, k : k + T] if r < 2 * e else scaled[r - 2 * e : r - 2 * e + T, k : k + T]
        if at < FIRST + SECOND:
            c1[(at - FIRST) * T : (at - FIRST + 1) * T, :] = tile
        else:
            c2[(at - FIRST - SECOND) * T : (at - FIRST - SECOND + 1) * T, :] = tile
        spot = at * T - (total * T - rest.shape[0])
        if spot >= 0:
            rest[spot : spot + T, :] = tile


def scale_cross(factor, c, swapped):
    e = factor.shape[0]
    total = 4 * e * e // T
    return call(
        scale_kernel,
        "scale_cross",
        2000 * 10**6,
        [((n, T), F32) for n in (SECOND * T, total - (FIRST + SECOND) * T, total - swapped * T)],
        [(VMEM, x) for x in (factor, c)],
        [],
    )


def couple(b):
    mine, across, along, corner = (ref[...] for ref in b)
    return jnp.concatenate(
        [jnp.concatenate([mine, across], axis=1), jnp.concatenate([along, corner], axis=1)], axis=0
    )


def factor_start_kernel(a0, a1, a2, a3, b0, b1, b2, b3, side):
    e = b0.shape[0]
    tiles = e // T
    coup = couple((b0, b1, b2, b3))
    side[...] = -dot(coup, coup, NT)
    side[:e, :e] = side[:e, :e] + (unpack(a0, 0, tiles) + unpack(a1, 0, tiles))
    side[e:, e:] = side[e:, e:] + (unpack(a2, 0, tiles) + unpack(a3, 0, tiles))
    sweep(side, 0, e)


def factor_start(a, b):
    e = b[0].shape[0]
    return call(
        factor_start_kernel,
        "factor_start",
        100 * 10**6,
        [((2 * e, 2 * e), F32)],
        [(VMEM, x) for x in (*a, *b)],
        [],
    )[0]


def factor_middle_kernel(before, side):
    side[...] = before[...]
    half = side.shape[0] // 2
    sweep(side, half, half + T)


def factor_middle(side):
    return call(
        factor_middle_kernel,
        "factor_middle",
        100 * 10**6,
        [(side.shape, F32)],
        [(VMEM, side)],
        [],
    )[0]


def factor_end_kernel(place, side_in, b0, b1, b2, b3, high, low, side, full):
    e = b0.shape[0]
    side[...] = side_in[...]
    sweep(side, e + T, 2 * e)
    coup = split(couple((b0, b1, b2, b3)))
    away = dot3(split(side[...]), coup)
    shape = full.shape
    unit = lax.broadcasted_iota(jnp.int32, shape, 0) == lax.broadcasted_iota(jnp.int32, shape, 1)
    full[...] = dot3(coup, split(away), TN) + unit.astype(F32)

    def emit(value, rows, columns):
        high[rows, columns], low[rows, columns] = split(value)

    first, rest = slice(0, e), slice(e, 3 * e)
    emit(full[...], rest, rest)
    emit(-away[:e, :], first, rest)
    same = place[0] == place[1]

    @pl.when(same)
    def _():
        emit(side[:e, :e], first, first)
        emit(-away[:e, :].T, rest, first)

    @pl.when(jnp.logical_not(same))
    def _():
        emit(side[:e, e:], first, first)
        emit(-away[e:, :].T, rest, first)


def factor_end(place, side, b):
    e = b[0].shape[0]
    return call(
        factor_end_kernel,
        "factor_end",
        3000 * 10**6,
        [((3 * e, 3 * e), BF16)] * 2,
        [(SMEM, place), (VMEM, side)] + [(VMEM, x) for x in b],
        [pltpu.VMEM((2 * e, 2 * e), F32), pltpu.VMEM((2 * e, 2 * e), F32)],
    )


def cross_block(*pieces):
    held = []
    for ref, skip in pieces:
        for at in range(skip * T, ref.shape[0], T):
            held.append(ref[at : at + T, :])
    tiles = math.isqrt(len(held) // 4)
    rows = []
    for r in range(2 * tiles):
        side = r // tiles
        row = [held[((side + 2 * c) * tiles + r % tiles) * tiles + k] for c in range(2) for k in range(tiles)]
        rows.append(jnp.concatenate(row, axis=1))
    return jnp.concatenate(rows, axis=0)


def symmetric_tiles(e):
    return len(upper(e // T))


def zeros(tiles):
    return jnp.zeros((tiles * T, T), F32), 0


def times_inverse(cross, high, low, inner):
    e = cross.shape[1] // 2
    return dot3(split(cross[:, :e]), (high[:e], low[:e])) + dot3(
        split(cross[:, e:]), (high[inner], low[inner])
    )


def spot(place, e, side, which):
    x = place[0] if which == 0 else 1 - place[0]
    return pl.ds(pl.multiple_of((2 * side + x) * e, T), e)


def put(out, place, held, a, b, sem):
    e = out.shape[1] // 4
    copies = []
    for r in range(2):
        for c in range(2):
            source = held.at[pl.ds(r * e, e), pl.ds(c * e, e)]
            target = out.at[0, spot(place, e, r, a), spot(place, e, c, b)]
            copies.append(pltpu.make_async_copy(source, target, sem.at[2 * r + c]))
            copies[-1].start()
    return copies


def wait(copies):
    for copy in copies:
        copy.wait()


def pick(ref, b):
    e = ref.shape[1] // 3
    return jnp.concatenate([ref[:, :e], ref[:, (1 + b) * e : (2 + b) * e]], axis=1)


def rows_kernel(
    n_mid, place, leaf, high, low, a0, c01, c02, a1, c11, third, swapped, rest, out, top, bottom, part, col, own, held, sem
):
    e = leaf.shape[1] // 4
    n_sym = symmetric_tiles(e)
    ext, _ = sides(place)
    fetch = []
    for r in range(2):
        for c in range(2):
            target = own.at[pl.ds(r * e, e), pl.ds(c * e, e)]
            source = leaf_block(leaf, ext[r], ext[c], 0, 0, e)
            fetch.append(pltpu.make_async_copy(source, target, sem.at[3, 2 * r + c]))
            fetch[-1].start()
    same = place[0] == place[1]
    mine = cross_block((a0, n_sym), (c01, 0), (c02, 0))
    left = split(times_inverse(mine, high[...], low[...], slice(e, 2 * e)))
    top[...], bottom[...] = left
    left = [[pick(x, b) for x in left] for b in range(2)]
    wait(fetch)

    @pl.when(same)
    def _():
        right = split(mine)
        held[0] = own[...] - dot3(left[0], right, NT)
        copies = put(out, place, held.at[0], 0, 0, sem.at[0])
        across = cross_block((a1, n_sym), (c11, 0), (third, 0))
        other = split(across)
        held[1] = -dot3(left[1], other, NT)
        copies += put(out, place, held.at[1], 0, 1, sem.at[1])
        value = times_inverse(across, high[...], low[...], slice(2 * e, 3 * e))
        held[2] = -dot3(split(pick(value, 0)), right, NT)
        copies += put(out, place, held.at[2], 1, 0, sem.at[2])
        part[:, : 2 * e] = -dot3(split(pick(value, 1)), other, NT)
        wait(copies)

    @pl.when(jnp.logical_not(same))
    def _():
        col[...] = cross_block((swapped, n_sym), (rest, 0))
        held[0] = -dot3(left[0], split(col[...]), NT)
        copies = put(out, place, held.at[0], 0, 0, sem.at[0])
        across = cross_block(
            (a1, n_sym), (c11, 0), (third[: n_mid * T, :], 0), zeros(third.shape[0] // T - n_mid)
        )
        part[...] = times_inverse(across, high[...], low[...], slice(2 * e, 3 * e))
        wait(copies)


def first_rows(n_mid, place, leaf, high, low, mine, across, swapped, rest):
    e = leaf.shape[1] // 4
    block = pltpu.VMEM((2 * e, 2 * e), F32)
    return call(
        functools.partial(rows_kernel, n_mid),
        "first_rows",
        500 * 10**6,
        [(leaf.shape, F32)] + [((2 * e, 3 * e), BF16)] * 2 + [((2 * e, 3 * e), F32)],
        [(SMEM, place), (HBM, leaf)]
        + [(VMEM, x) for x in (high, low, *mine, *across, swapped, rest)],
        [block, block, pltpu.VMEM((3, 2 * e, 2 * e), F32), pltpu.SemaphoreType.DMA((4, 4))],
        out_specs=[HBM] + [VMEM] * 3,
    )


def corner_kernel(place, before, top, bottom, a3, c31, passed, out, held, sem):
    n_sym = symmetric_tiles(out.shape[1] // 4)

    @pl.when(place[0] != place[1])
    def _():
        right = split(cross_block((a3, n_sym), (c31, 0), (passed, 0)))
        held[...] = -dot3([pick(x, 1) for x in (top, bottom)], right, NT)
        wait(put(out, place, held, 0, 1, sem))


def corner_block(place, before, top, bottom, a3, c31, passed):
    e = before.shape[1] // 4
    return call(
        corner_kernel,
        "corner_block",
        500 * 10**6,
        [(before.shape, F32)],
        [(SMEM, place), (HBM, before)] + [(VMEM, x) for x in (top, bottom, a3, c31, passed)],
        [pltpu.VMEM((2 * e, 2 * e), F32), pltpu.SemaphoreType.DMA((4,))],
        out_specs=[HBM],
        input_output_aliases={1: 0},
    )[0]


def finish_kernel(
    place, before, high, low, part, passed, last, swapped, rest, a3, c31, out, held, scratch, sem
):
    e = out.shape[1] // 4
    tiles = e // T
    n_sym = symmetric_tiles(e)
    n_last = last.shape[0] // T
    n_mid = passed.shape[0] // T - n_last

    @pl.when(place[0] == place[1])
    def _():
        for at, (i, j) in enumerate(upper(2 * tiles)):
            ref, at = (last, at) if at < n_last else (passed, at - n_last + n_mid)
            piece = ref[at * T : (at + 1) * T, :]
            r, c = slice(i * T, (i + 1) * T), slice(j * T, (j + 1) * T)
            held[0, r, c] = part[r, c] + piece
            if i != j:
                held[0, c, r] = part[c, r] + piece.T
        wait(put(out, place, held.at[0], 1, 1, sem.at[0]))

    @pl.when(place[0] != place[1])
    def _():
        late = cross_block(zeros(4 * tiles * tiles - n_last), (last, 0))[:, e:]
        inner = slice(2 * e, 3 * e)
        start = (2 * tiles * tiles - n_last) // tiles * T
        scratch[:start, :] = part[:start, :]
        scratch[start:, :] = part[start:, :] + dot3(split(late[start:]), (high[inner], low[inner]))
        copies = []
        for b in range(2):
            if b == 0:
                col = cross_block((swapped, n_sym), (rest, 0))
            else:
                col = cross_block((a3, n_sym), (c31, 0), (passed, 0))
            held[b] = -dot3(split(pick(scratch, b)), split(col), NT)
            copies += put(out, place, held.at[b], 1, b, sem.at[b])
        wait(copies)


def finish(place, before, high, low, part, passed, last, swapped, rest, a3, c31):
    e = before.shape[1] // 4
    return call(
        finish_kernel,
        "finish",
        500 * 10**6,
        [(before.shape, F32)],
        [(SMEM, place), (HBM, before)]
        + [(VMEM, x) for x in (high, low, part, passed, last, swapped, rest, a3, c31)],
        [
            pltpu.VMEM((2, 2 * e, 2 * e), F32),
            pltpu.VMEM((2 * e, 3 * e), F32),
            pltpu.SemaphoreType.DMA((2, 4)),
        ],
        out_specs=[HBM],
        input_output_aliases={1: 0},
    )[0]


def tie(*values):
    return lax.optimization_barrier(values)


def solution(mesh):
    nx, ny = mesh.shape["gx"], mesh.shape["gy"]
    devices = [(x, y) for x in range(nx) for y in range(ny)]

    def is_same(x, y):
        return x // (nx // 2) == y // (ny // 2)

    def send(value, along_y, only=None):
        pairs = []
        for x, y in devices:
            if only is None or is_same(x, y) == only:
                to = (x, (y + ny // 2) % ny) if along_y else ((x + nx // 2) % nx, y)
                pairs.append((x * ny + y, to[0] * ny + to[1]))
        return lax.ppermute(value, ("gx", "gy"), pairs)

    def body(leaf):
        e = leaf.shape[1] // 4
        v = lax.axis_index("gx") // (nx // 2)
        u = lax.axis_index("gy") // (ny // 2)
        place = jnp.stack([v, u]).astype(jnp.int32)
        same = u == v
        a = cut_first(place, leaf)
        a_x = send(a, False)
        here, a = tie(place, a)
        hh = cut_side(here, leaf)
        hh_y = send(hh, True)
        swap, outer0, b, c = cut_second(place, leaf)
        swapped = send(swap, True)
        b, factor = gauge(hh, hh_y, b)
        b_x = send(b, False)
        n_last = outer0.shape[0] // T
        c1, c2, rest = scale_cross(factor, c, n_last)
        b, a_x, c1, swapped = tie(b, a_x, c1, swapped)
        b_y = send(b, True)
        a_d = send(a_x, True)
        c1, b_x = tie(c1, b_x)
        c1_x = send(c1, False)
        b_x, b_y, a_d = tie(b_x, b_y, a_d)
        b_d = send(b_x, True)
        rest, b_d = tie(rest, b_d)
        rest = send(rest, True, only=True)
        side = factor_start((a, a_x, swapped, a_d), (b, b_x, b_y, b_d))
        side = factor_middle(side)
        n_mid = c2.shape[0] // T - n_last
        theirs = jnp.concatenate([c2[: n_mid * T], swapped[-n_last * T :]])
        third, side = tie(jnp.where(same, theirs, c2), side)
        third = send(third, False)
        c1_x, side = tie(c1_x, side)
        c1_d = send(c1_x, True, only=True)
        high, low = factor_end(place, side, (b, b_x, b_y, b_d))
        last, third, high = tie(jnp.where(same, c2[n_mid * T :], outer0), third, high)
        last = send(last, False)
        passed = send(third, True)
        out, top, bottom, part = first_rows(
            n_mid, place, leaf, high, low, (a, c1, c2), (a_x, c1_x, third), swapped, rest
        )
        out = corner_block(place, out, top, bottom, a_d, c1_d, passed)
        return finish(place, out, high, low, part, passed, last, swapped, rest, a_d, c1_d)

    return jax.shard_map(
        body,
        mesh=mesh,
        in_specs=(P(None, "gy", "gx"),),
        out_specs=P(None, "gy", "gx"),
        check_vma=False,
    )
```

```python
import functools
import math

import jax
import jax.numpy as jnp
from jax import lax
from jax.experimental import pallas as pl
from jax.experimental.pallas import tpu as pltpu
from jax.sharding import PartitionSpec as P

F32 = jnp.float32
BF16 = jnp.bfloat16
T = 128
R = 16
FIRST = 1
SECOND = 8
HBM = pl.BlockSpec(memory_space=pl.ANY)
FAR = pl.BlockSpec(memory_space=pltpu.HBM)
VMEM = pl.BlockSpec(memory_space=pltpu.VMEM)
SMEM = pl.BlockSpec(memory_space=pltpu.SMEM)


def dot(a, b, dims=((1,), (0,))):
    return lax.dot_general(
        a, b, (dims, ((), ())), precision=lax.Precision.HIGHEST, preferred_element_type=F32
    )


def dot16(a, b, dims=((1,), (0,))):
    return lax.dot_general(a, b, (dims, ((), ())), preferred_element_type=F32)


def split(a):
    high = a.astype(BF16)
    return high, (a - high.astype(F32)).astype(BF16)


def dot3(a, b, dims=((1,), (0,))):
    return dot16(a[0], b[0], dims) + (dot16(a[0], b[1], dims) + dot16(a[1], b[0], dims))


NT = ((1,), (1,))
TN = ((0,), (0,))


def upper(n):
    return [(i, j) for i in range(n) for j in range(i, n)]


def across_lanes(x, k):
    return jnp.broadcast_to(x[:, k : k + 1], x.shape)


def across_rows(x, k):
    return jnp.broadcast_to(x[k : k + 1, :], x.shape)


def panel(rows, c0, lower):
    sub = lax.broadcasted_iota(jnp.int32, rows.shape, 0)
    lane = lax.broadcasted_iota(jnp.int32, rows.shape, 1)
    cols = [across_lanes(rows, c0 + k) for k in range(R)]
    out = jnp.where((lane >= c0) & (lane < c0 + R), (lane - c0 == sub).astype(F32), rows)
    half = out
    scale = jnp.ones_like(rows)
    for k in range(R):
        pivot = across_rows(cols[k], k)
        inv = 1.0 / pivot
        here = sub == k
        mult = cols[k]

        def step(x):
            row = across_rows(x, k) * inv
            return jnp.where(here, row, x - mult * row)

        if lower:
            scale = jnp.where(here, pivot, scale)
            half = half - jnp.where(sub > k, mult, 0.0) * (across_rows(half, k) * inv)
        out = step(out)
        for j in range(k + 1, R):
            cols[j] = step(cols[j])
    return out, half * lax.rsqrt(scale) if lower else None


def put_rows(matrix, rows, r0):
    parts = [matrix[:r0]] if r0 else []
    parts.append(rows)
    if r0 + rows.shape[0] < matrix.shape[0]:
        parts.append(matrix[r0 + rows.shape[0] :])
    return jnp.concatenate(parts, axis=0)


def invert_tile(m, lower=False):
    lane = lax.broadcasted_iota(jnp.int32, (T, T), 1)
    sub = lax.broadcasted_iota(jnp.int32, (T, T), 0)
    rows = m[:R]
    for c0 in range(0, T, R):
        swept, half = panel(rows, c0, lower)
        if c0 + R < T:
            old = m[c0 + R : c0 + 2 * R]
            inside = (lane[:R] >= c0) & (lane[:R] < c0 + R)
            sums = [jnp.where(inside, 0.0, old)] + [None] * 3
            for k in range(R):
                term = across_lanes(old, c0 + k) * across_rows(swept, k)
                sums[k % 4] = -term if sums[k % 4] is None else sums[k % 4] - term
            rows = (sums[0] + sums[1]) + (sums[2] + sums[3])
        wide = put_rows(jnp.zeros((T, T), F32), swept, c0)
        rest = jnp.where((lane >= c0) & (lane < c0 + R), 0.0, m) - dot(m, wide)
        if lower:
            rest = jnp.where(sub < c0, m, rest)
        m = put_rows(rest, half if lower else swept, c0)
    return jnp.where(lane > sub, 0.0, m) if lower else m


def sweep(ref, start, stop):
    n = ref.shape[0]
    for p in range(start, stop, T):
        pivot = invert_tile(ref[p : p + T, p : p + T])
        rows = dot(pivot, ref[p : p + T, :])
        parts = ([rows[:, :p]] if p else []) + [pivot]
        if p + T < n:
            parts.append(rows[:, p + T :])
        rows = jnp.concatenate(parts, axis=1)
        for q in range(0, n, T):
            if q != p:
                change = dot(ref[q : q + T, p : p + T], rows)
                ref[q : q + T, p : p + T] = jnp.zeros((T, T), F32)
                ref[q : q + T, :] = ref[q : q + T, :] - change
        ref[p : p + T, :] = rows


def inverse_factor(ref):
    n = ref.shape[0]
    for p in range(0, n, T):
        pivot = invert_tile(ref[p : p + T, p : p + T], lower=True)
        scaled = dot(pivot, ref[p : p + T, :])
        for q in range(p + T, n, T):
            weight = scaled[:, q : q + T]
            ref[q : q + T, :] = ref[q : q + T, :] - dot(weight, scaled, TN)
            ref[q : q + T, p : p + T] = -dot(weight, pivot, TN)
        for q in range(0, n, T):
            if q < p:
                ref[p : p + T, q : q + T] = scaled[:, q : q + T]
            else:
                ref[p : p + T, q : q + T] = pivot if q == p else jnp.zeros((T, T), F32)


def leaf_block(leaf, side_r, side_c, r, c, size):
    e = leaf.shape[1] // 4
    return leaf.at[
        0,
        pl.ds(pl.multiple_of(side_r * e + r * size, T), size),
        pl.ds(pl.multiple_of(side_c * e + c * size, T), size),
    ]


def run_copies(pairs, sem):
    copies = [pltpu.make_async_copy(a, b, sem.at[i]) for i, (a, b) in enumerate(pairs)]
    for copy in copies:
        copy.start()
    for copy in copies:
        copy.wait()


def sides(place):
    v, u = place[0], place[1]
    return [v, 2 + u], [1 - v, 3 - u]


def unpack(ref, at, tiles):
    held = {}
    for r, c in upper(tiles):
        held[r, c] = ref[at : at + T, :]
        if c > r:
            held[c, r] = held[r, c].T
        at += T
    return jnp.concatenate(
        [jnp.concatenate([held[r, c] for c in range(tiles)], axis=1) for r in range(tiles)], axis=0
    )


def call(kernel, name, cost, outs, ins, scratch, **more):
    return pl.pallas_call(
        kernel,
        out_shape=[jax.ShapeDtypeStruct(shape, dtype) for shape, dtype in outs],
        in_specs=[spec for spec, _ in ins],
        out_specs=more.pop("out_specs", [VMEM] * len(outs)),
        scratch_shapes=scratch,
        compiler_params=pltpu.CompilerParams(vmem_limit_bytes=32 * 2**20),
        cost_estimate=pl.CostEstimate(flops=cost, bytes_accessed=cost, transcendentals=0),
        name=name,
        **more,
    )(*[value for _, value in ins])


def block_tiles(leaf, side_r, side_c, at):
    tiles = leaf.shape[1] // 4 // T
    return leaf_block(leaf, side_r, side_c, at // tiles, at % tiles, T)


def cross_tile(leaf, ext, inn, at):
    n = (leaf.shape[1] // 4 // T) ** 2
    return block_tiles(leaf, ext[at // n % 2], inn[at // n // 2], at % n)


def cut_first_kernel(place, leaf, a, sem):
    tiles = leaf.shape[1] // 4 // T
    ext, inn = sides(place)
    n_sym = len(upper(tiles))
    pairs = []
    for at, (r, c) in enumerate(upper(tiles)):
        pairs.append((leaf_block(leaf, inn[0], inn[0], r, c, T), a.at[pl.ds(at * T, T)]))
    for at in range(FIRST):
        pairs.append(
            (cross_tile(leaf, ext, inn, at), a.at[pl.ds((n_sym + at) * T, T)])
        )
    run_copies(pairs, sem)


def cut_first(place, leaf):
    n_sym = len(upper(leaf.shape[1] // 4 // T))
    return call(
        cut_first_kernel,
        "cut_first",
        1000 * 10**6,
        [(((n_sym + FIRST) * T, T), F32)],
        [(SMEM, place), (FAR, leaf)],
        [pltpu.SemaphoreType.DMA((n_sym + FIRST,))],
    )[0]


def cut_side_kernel(place, leaf, hh, sem):
    tiles = leaf.shape[1] // 4 // T
    _, inn = sides(place)
    pairs = []
    for at, (r, c) in enumerate(upper(tiles)):
        pairs.append((leaf_block(leaf, inn[1], inn[1], r, c, T), hh.at[pl.ds(at * T, T)]))
    run_copies(pairs, sem)


def cut_side(place, leaf):
    n_sym = len(upper(leaf.shape[1] // 4 // T))
    return call(
        cut_side_kernel,
        "cut_side",
        1000 * 10**6,
        [((n_sym * T, T), F32)],
        [(SMEM, place), (FAR, leaf)],
        [pltpu.SemaphoreType.DMA((n_sym,))],
    )[0]


def cut_second_kernel(place, leaf, swap, outer0, b, c, sem):
    e = leaf.shape[1] // 4
    tiles = e // T
    ext, inn = sides(place)
    n_sym = len(upper(tiles))
    pairs = [
        (leaf_block(leaf, inn[0], inn[1], 0, 0, e), b),
        (leaf_block(leaf, ext[0], inn[0], 0, 0, e), c.at[pl.ds(0, e)]),
        (leaf_block(leaf, ext[1], inn[0], 0, 0, e), c.at[pl.ds(e, e)]),
        (leaf_block(leaf, ext[0], inn[1], 0, 0, e), c.at[pl.ds(2 * e, e)]),
        (leaf_block(leaf, ext[1], inn[1], 0, 0, e), c.at[pl.ds(3 * e, e)]),
    ]
    for at, (r, k) in enumerate(upper(tiles)):
        pairs.append((leaf_block(leaf, inn[0], inn[0], r, k, T), swap.at[pl.ds(at * T, T)]))
    half = outer0.shape[0] // T
    second = []
    for at, (r, k) in enumerate(upper(2 * tiles)):
        source = leaf_block(leaf, ext[r // tiles], ext[k // tiles], r % tiles, k % tiles, T)
        if at < half:
            pairs.append((source, outer0.at[pl.ds(at * T, T)]))
        else:
            second.append((source, swap.at[pl.ds((n_sym + at - half) * T, T)]))
    run_copies(pairs, sem)
    same = place[0] == place[1]

    @pl.when(same)
    def _():
        cross = [
            (cross_tile(leaf, ext, inn, at), swap.at[pl.ds((n_sym + at) * T, T)])
            for at in range(half)
        ]
        run_copies(cross, sem)

    @pl.when(jnp.logical_not(same))
    def _():
        run_copies(second, sem)


def cut_second(place, leaf):
    e = leaf.shape[1] // 4
    n_sym = len(upper(e // T))
    half = len(upper(2 * (e // T))) // 2
    return call(
        cut_second_kernel,
        "cut_second",
        1000 * 10**6,
        [(((n_sym + half) * T, T), F32), ((half * T, T), F32), ((e, e), F32), ((4 * e, e), F32)],
        [(SMEM, place), (HBM, leaf)],
        [pltpu.SemaphoreType.DMA((n_sym + half + 5,))],
    )


def gauge_kernel(mine, along, b, b_out, factor):
    e = factor.shape[0]
    tiles = e // T
    factor[...] = unpack(mine, 0, tiles) + unpack(along, 0, tiles)
    inverse_factor(factor)
    b_out[...] = dot(b[...], factor[...], NT)


def gauge(mine, along, b):
    e = b.shape[0]
    return call(
        gauge_kernel,
        "gauge_side",
        8000 * 10**6,
        [((e, e), F32), ((e, e), F32)],
        [(VMEM, x) for x in (mine, along, b)],
        [],
    )


def scale_kernel(factor, c, c1, c2, rest):
    e = factor.shape[0]
    tiles = e // T
    scaled = dot3(split(c[2 * e :, :]), split(factor[...]), NT)
    total = 4 * tiles * tiles
    for at in range(FIRST, total):
        r, k = at // tiles * T, at % tiles * T
        tile = c[r : r + T, k : k + T] if r < 2 * e else scaled[r - 2 * e : r - 2 * e + T, k : k + T]
        if at < FIRST + SECOND:
            c1[(at - FIRST) * T : (at - FIRST + 1) * T, :] = tile
        else:
            c2[(at - FIRST - SECOND) * T : (at - FIRST - SECOND + 1) * T, :] = tile
        spot = at * T - (total * T - rest.shape[0])
        if spot >= 0:
            rest[spot : spot + T, :] = tile


def scale_cross(factor, c, swapped):
    e = factor.shape[0]
    total = 4 * e * e // T
    return call(
        scale_kernel,
        "scale_cross",
        2000 * 10**6,
        [((n, T), F32) for n in (SECOND * T, total - (FIRST + SECOND) * T, total - swapped * T)],
        [(VMEM, x) for x in (factor, c)],
        [],
    )


def couple(b):
    mine, across, along, corner = (ref[...] for ref in b)
    return jnp.concatenate(
        [jnp.concatenate([mine, across], axis=1), jnp.concatenate([along, corner], axis=1)], axis=0
    )


def factor_start_kernel(a0, a1, a2, a3, b0, b1, b2, b3, side):
    e = b0.shape[0]
    tiles = e // T
    coup = couple((b0, b1, b2, b3))
    side[...] = -dot(coup, coup, NT)
    side[:e, :e] = side[:e, :e] + (unpack(a0, 0, tiles) + unpack(a1, 0, tiles))
    side[e:, e:] = side[e:, e:] + (unpack(a2, 0, tiles) + unpack(a3, 0, tiles))
    sweep(side, 0, e)


def factor_start(a, b):
    e = b[0].shape[0]
    return call(
        factor_start_kernel,
        "factor_start",
        1000 * 10**6,
        [((2 * e, 2 * e), F32)],
        [(VMEM, x) for x in (*a, *b)],
        [],
    )[0]


def factor_end_kernel(place, side_in, b0, b1, b2, b3, high, low, side, full):
    e = b0.shape[0]
    side[...] = side_in[...]
    sweep(side, e, 2 * e)
    coup = split(couple((b0, b1, b2, b3)))
    away = dot3(split(side[...]), coup)
    shape = full.shape
    unit = lax.broadcasted_iota(jnp.int32, shape, 0) == lax.broadcasted_iota(jnp.int32, shape, 1)
    full[...] = dot3(coup, split(away), TN) + unit.astype(F32)

    def emit(value, rows, columns):
        high[rows, columns], low[rows, columns] = split(value)

    first, rest = slice(0, e), slice(e, 3 * e)
    emit(full[...], rest, rest)
    emit(-away[:e, :], first, rest)
    same = place[0] == place[1]

    @pl.when(same)
    def _():
        emit(side[:e, :e], first, first)
        emit(-away[:e, :].T, rest, first)

    @pl.when(jnp.logical_not(same))
    def _():
        emit(side[:e, e:], first, first)
        emit(-away[e:, :].T, rest, first)


def factor_end(place, side, b):
    e = b[0].shape[0]
    return call(
        factor_end_kernel,
        "factor_end",
        10000 * 10**6,
        [((3 * e, 3 * e), BF16)] * 2,
        [(SMEM, place), (VMEM, side)] + [(VMEM, x) for x in b],
        [pltpu.VMEM((2 * e, 2 * e), F32), pltpu.VMEM((2 * e, 2 * e), F32)],
    )


def cross_block(*pieces):
    held = []
    for ref, skip in pieces:
        for at in range(skip * T, ref.shape[0], T):
            held.append(ref[at : at + T, :])
    tiles = math.isqrt(len(held) // 4)
    rows = []
    for r in range(2 * tiles):
        side = r // tiles
        row = [held[((side + 2 * c) * tiles + r % tiles) * tiles + k] for c in range(2) for k in range(tiles)]
        rows.append(jnp.concatenate(row, axis=1))
    return jnp.concatenate(rows, axis=0)


def symmetric_tiles(e):
    return len(upper(e // T))


def zeros(tiles):
    return jnp.zeros((tiles * T, T), F32), 0


def times_inverse(cross, high, low, inner):
    e = cross.shape[1] // 2
    return dot3(split(cross[:, :e]), (high[:e], low[:e])) + dot3(
        split(cross[:, e:]), (high[inner], low[inner])
    )


def spot(place, e, side, which):
    x = place[0] if which == 0 else 1 - place[0]
    return pl.ds(pl.multiple_of((2 * side + x) * e, T), e)


def put(out, place, held, a, b, sem):
    e = out.shape[1] // 4
    copies = []
    for r in range(2):
        for c in range(2):
            source = held.at[pl.ds(r * e, e), pl.ds(c * e, e)]
            target = out.at[0, spot(place, e, r, a), spot(place, e, c, b)]
            copies.append(pltpu.make_async_copy(source, target, sem.at[2 * r + c]))
            copies[-1].start()
    return copies


def wait(copies):
    for copy in copies:
        copy.wait()


def pick(ref, b):
    e = ref.shape[1] // 3
    return jnp.concatenate([ref[:, :e], ref[:, (1 + b) * e : (2 + b) * e]], axis=1)


def rows_kernel(
    n_mid, place, leaf, high, low, a0, c01, c02, a1, c11, third, swapped, rest, out, top, bottom, part, col, own, held, sem
):
    e = leaf.shape[1] // 4
    n_sym = symmetric_tiles(e)
    ext, _ = sides(place)
    fetch = []
    for r in range(2):
        for c in range(2):
            target = own.at[pl.ds(r * e, e), pl.ds(c * e, e)]
            source = leaf_block(leaf, ext[r], ext[c], 0, 0, e)
            fetch.append(pltpu.make_async_copy(source, target, sem.at[3, 2 * r + c]))
            fetch[-1].start()
    same = place[0] == place[1]
    mine = cross_block((a0, n_sym), (c01, 0), (c02, 0))
    left = split(times_inverse(mine, high[...], low[...], slice(e, 2 * e)))
    top[...], bottom[...] = left
    left = [[pick(x, b) for x in left] for b in range(2)]
    wait(fetch)

    @pl.when(same)
    def _():
        right = split(mine)
        held[0] = own[...] - dot3(left[0], right, NT)
        copies = put(out, place, held.at[0], 0, 0, sem.at[0])
        across = cross_block((a1, n_sym), (c11, 0), (third, 0))
        other = split(across)
        held[1] = -dot3(left[1], other, NT)
        copies += put(out, place, held.at[1], 0, 1, sem.at[1])
        value = times_inverse(across, high[...], low[...], slice(2 * e, 3 * e))
        held[2] = -dot3(split(pick(value, 0)), right, NT)
        copies += put(out, place, held.at[2], 1, 0, sem.at[2])
        part[:, : 2 * e] = -dot3(split(pick(value, 1)), other, NT)
        wait(copies)

    @pl.when(jnp.logical_not(same))
    def _():
        col[...] = cross_block((swapped, n_sym), (rest, 0))
        held[0] = -dot3(left[0], split(col[...]), NT)
        copies = put(out, place, held.at[0], 0, 0, sem.at[0])
        across = cross_block(
            (a1, n_sym), (c11, 0), (third[: n_mid * T, :], 0), zeros(third.shape[0] // T - n_mid)
        )
        part[...] = times_inverse(across, high[...], low[...], slice(2 * e, 3 * e))
        wait(copies)


def first_rows(n_mid, place, leaf, high, low, mine, across, swapped, rest):
    e = leaf.shape[1] // 4
    block = pltpu.VMEM((2 * e, 2 * e), F32)
    return call(
        functools.partial(rows_kernel, n_mid),
        "first_rows",
        500 * 10**6,
        [(leaf.shape, F32)] + [((2 * e, 3 * e), BF16)] * 2 + [((2 * e, 3 * e), F32)],
        [(SMEM, place), (HBM, leaf)]
        + [(VMEM, x) for x in (high, low, *mine, *across, swapped, rest)],
        [block, block, pltpu.VMEM((3, 2 * e, 2 * e), F32), pltpu.SemaphoreType.DMA((4, 4))],
        out_specs=[HBM] + [VMEM] * 3,
    )


def corner_kernel(place, before, top, bottom, a3, c31, passed, out, held, sem):
    n_sym = symmetric_tiles(out.shape[1] // 4)

    @pl.when(place[0] != place[1])
    def _():
        right = split(cross_block((a3, n_sym), (c31, 0), (passed, 0)))
        held[...] = -dot3([pick(x, 1) for x in (top, bottom)], right, NT)
        wait(put(out, place, held, 0, 1, sem))


def corner_block(place, before, top, bottom, a3, c31, passed):
    e = before.shape[1] // 4
    return call(
        corner_kernel,
        "corner_block",
        500 * 10**6,
        [(before.shape, F32)],
        [(SMEM, place), (HBM, before)] + [(VMEM, x) for x in (top, bottom, a3, c31, passed)],
        [pltpu.VMEM((2 * e, 2 * e), F32), pltpu.SemaphoreType.DMA((4,))],
        out_specs=[HBM],
        input_output_aliases={1: 0},
    )[0]


def finish_kernel(
    place, before, high, low, part, passed, last, swapped, rest, a3, c31, out, held, scratch, sem
):
    e = out.shape[1] // 4
    tiles = e // T
    n_sym = symmetric_tiles(e)
    n_last = last.shape[0] // T
    n_mid = passed.shape[0] // T - n_last

    @pl.when(place[0] == place[1])
    def _():
        for at, (i, j) in enumerate(upper(2 * tiles)):
            ref, at = (last, at) if at < n_last else (passed, at - n_last + n_mid)
            piece = ref[at * T : (at + 1) * T, :]
            r, c = slice(i * T, (i + 1) * T), slice(j * T, (j + 1) * T)
            held[0, r, c] = part[r, c] + piece
            if i != j:
                held[0, c, r] = part[c, r] + piece.T
        wait(put(out, place, held.at[0], 1, 1, sem.at[0]))

    @pl.when(place[0] != place[1])
    def _():
        late = cross_block(zeros(4 * tiles * tiles - n_last), (last, 0))[:, e:]
        inner = slice(2 * e, 3 * e)
        start = (2 * tiles * tiles - n_last) // tiles * T
        scratch[:start, :] = part[:start, :]
        scratch[start:, :] = part[start:, :] + dot3(split(late[start:]), (high[inner], low[inner]))
        copies = []
        for b in range(2):
            if b == 0:
                col = cross_block((swapped, n_sym), (rest, 0))
            else:
                col = cross_block((a3, n_sym), (c31, 0), (passed, 0))
            held[b] = -dot3(split(pick(scratch, b)), split(col), NT)
            copies += put(out, place, held.at[b], 1, b, sem.at[b])
        wait(copies)


def finish(place, before, high, low, part, passed, last, swapped, rest, a3, c31):
    e = before.shape[1] // 4
    return call(
        finish_kernel,
        "finish",
        500 * 10**6,
        [(before.shape, F32)],
        [(SMEM, place), (HBM, before)]
        + [(VMEM, x) for x in (high, low, part, passed, last, swapped, rest, a3, c31)],
        [
            pltpu.VMEM((2, 2 * e, 2 * e), F32),
            pltpu.VMEM((2 * e, 3 * e), F32),
            pltpu.SemaphoreType.DMA((2, 4)),
        ],
        out_specs=[HBM],
        input_output_aliases={1: 0},
    )[0]


def tie(*values):
    return lax.optimization_barrier(values)


def solution(mesh):
    nx, ny = mesh.shape["gx"], mesh.shape["gy"]
    devices = [(x, y) for x in range(nx) for y in range(ny)]

    def is_same(x, y):
        return x // (nx // 2) == y // (ny // 2)

    def send(value, along_y, only=None):
        pairs = []
        for x, y in devices:
            if only is None or is_same(x, y) == only:
                to = (x, (y + ny // 2) % ny) if along_y else ((x + nx // 2) % nx, y)
                pairs.append((x * ny + y, to[0] * ny + to[1]))
        return lax.ppermute(value, ("gx", "gy"), pairs)

    def body(leaf):
        e = leaf.shape[1] // 4
        v = lax.axis_index("gx") // (nx // 2)
        u = lax.axis_index("gy") // (ny // 2)
        place = jnp.stack([v, u]).astype(jnp.int32)
        same = u == v
        a = cut_first(place, leaf)
        a_x = send(a, False)
        here, a = tie(place, a)
        hh = cut_side(here, leaf)
        hh_y = send(hh, True)
        swap, outer0, b, c = cut_second(place, leaf)
        swapped = send(swap, True)
        b, factor = gauge(hh, hh_y, b)
        b_x = send(b, False)
        n_last = outer0.shape[0] // T
        c1, c2, rest = scale_cross(factor, c, n_last)
        b, a_x, c1, swapped = tie(b, a_x, c1, swapped)
        b_y = send(b, True)
        a_d = send(a_x, True)
        c1, b_x = tie(c1, b_x)
        c1_x = send(c1, False)
        b_x, b_y, a_d = tie(b_x, b_y, a_d)
        b_d = send(b_x, True)
        rest, b_d = tie(rest, b_d)
        rest = send(rest, True, only=True)
        side = factor_start((a, a_x, swapped, a_d), (b, b_x, b_y, b_d))
        n_mid = c2.shape[0] // T - n_last
        theirs = jnp.concatenate([c2[: n_mid * T], swapped[-n_last * T :]])
        third, side = tie(jnp.where(same, theirs, c2), side)
        third = send(third, False)
        c1_x, side = tie(c1_x, side)
        c1_d = send(c1_x, True, only=True)
        high, low = factor_end(place, side, (b, b_x, b_y, b_d))
        last, third, high = tie(jnp.where(same, c2[n_mid * T :], outer0), third, high)
        last = send(last, False)
        passed = send(third, True)
        out, top, bottom, part = first_rows(
            n_mid, place, leaf, high, low, (a, c1, c2), (a_x, c1_x, third), swapped, rest
        )
        out = corner_block(place, out, top, bottom, a_d, c1_d, passed)
        return finish(place, out, high, low, part, passed, last, swapped, rest, a_d, c1_d)

    return jax.shard_map(
        body,
        mesh=mesh,
        in_specs=(P(None, "gy", "gx"),),
        out_specs=P(None, "gy", "gx"),
        check_vma=False,
    )
```

```python
import math

import jax
import jax.numpy as jnp
from jax import lax
from jax.experimental import pallas as pl
from jax.experimental.pallas import tpu as pltpu
from jax.sharding import PartitionSpec as P

F32 = jnp.float32
BF16 = jnp.bfloat16
T = 128
R = 16
FIRST = 1
SECOND = 8
HBM = pl.BlockSpec(memory_space=pl.ANY)
FAR = pl.BlockSpec(memory_space=pltpu.HBM)
VMEM = pl.BlockSpec(memory_space=pltpu.VMEM)
SMEM = pl.BlockSpec(memory_space=pltpu.SMEM)
PARAMS = pltpu.CompilerParams(vmem_limit_bytes=32 * 2**20)


def dot(a, b, dims=((1,), (0,))):
    return lax.dot_general(
        a, b, (dims, ((), ())), precision=lax.Precision.HIGHEST, preferred_element_type=F32
    )


def dot16(a, b, dims=((1,), (0,))):
    return lax.dot_general(a, b, (dims, ((), ())), preferred_element_type=F32)


def split(a):
    high = a.astype(BF16)
    return high, (a - high.astype(F32)).astype(BF16)


def dot3(a, b, dims=((1,), (0,))):
    return dot16(a[0], b[0], dims) + (dot16(a[0], b[1], dims) + dot16(a[1], b[0], dims))


NT = ((1,), (1,))
TN = ((0,), (0,))


def upper(n):
    return [(i, j) for i in range(n) for j in range(i, n)]


def across_lanes(x, k):
    return jnp.broadcast_to(x[:, k : k + 1], x.shape)


def across_rows(x, k):
    return jnp.broadcast_to(x[k : k + 1, :], x.shape)


def panel(rows, c0, lower):
    sub = lax.broadcasted_iota(jnp.int32, rows.shape, 0)
    lane = lax.broadcasted_iota(jnp.int32, rows.shape, 1)
    cols = [across_lanes(rows, c0 + k) for k in range(R)]
    out = jnp.where((lane >= c0) & (lane < c0 + R), (lane - c0 == sub).astype(F32), rows)
    half = out
    scale = jnp.ones_like(rows)
    for k in range(R):
        pivot = across_rows(cols[k], k)
        inv = 1.0 / pivot
        here = sub == k
        mult = cols[k]

        def step(x):
            row = across_rows(x, k) * inv
            return jnp.where(here, row, x - mult * row)

        if lower:
            scale = jnp.where(here, pivot, scale)
            half = half - jnp.where(sub > k, mult, 0.0) * (across_rows(half, k) * inv)
        out = step(out)
        for j in range(k + 1, R):
            cols[j] = step(cols[j])
    return out, half * lax.rsqrt(scale) if lower else None


def put_rows(matrix, rows, r0):
    parts = [matrix[:r0]] if r0 else []
    parts.append(rows)
    if r0 + rows.shape[0] < matrix.shape[0]:
        parts.append(matrix[r0 + rows.shape[0] :])
    return jnp.concatenate(parts, axis=0)


def invert_tile(m, lower=False):
    lane = lax.broadcasted_iota(jnp.int32, (T, T), 1)
    sub = lax.broadcasted_iota(jnp.int32, (T, T), 0)
    rows = m[:R]
    for c0 in range(0, T, R):
        swept, half = panel(rows, c0, lower)
        if c0 + R < T:
            old = m[c0 + R : c0 + 2 * R]
            inside = (lane[:R] >= c0) & (lane[:R] < c0 + R)
            sums = [jnp.where(inside, 0.0, old)] + [None] * 3
            for k in range(R):
                term = across_lanes(old, c0 + k) * across_rows(swept, k)
                sums[k % 4] = -term if sums[k % 4] is None else sums[k % 4] - term
            rows = (sums[0] + sums[1]) + (sums[2] + sums[3])
        wide = put_rows(jnp.zeros((T, T), F32), swept, c0)
        rest = jnp.where((lane >= c0) & (lane < c0 + R), 0.0, m) - dot(m, wide)
        if lower:
            rest = jnp.where(sub < c0, m, rest)
        m = put_rows(rest, half if lower else swept, c0)
    return jnp.where(lane > sub, 0.0, m) if lower else m


def sweep(ref, start, stop):
    n = ref.shape[0]
    for p in range(start, stop, T):
        pivot = invert_tile(ref[p : p + T, p : p + T])
        rows = dot(pivot, ref[p : p + T, :])
        parts = ([rows[:, :p]] if p else []) + [pivot]
        if p + T < n:
            parts.append(rows[:, p + T :])
        rows = jnp.concatenate(parts, axis=1)
        for q in range(0, n, T):
            if q != p:
                change = dot(ref[q : q + T, p : p + T], rows)
                ref[q : q + T, p : p + T] = jnp.zeros((T, T), F32)
                ref[q : q + T, :] = ref[q : q + T, :] - change
        ref[p : p + T, :] = rows


def inverse_factor(ref):
    n = ref.shape[0]
    for p in range(0, n, T):
        pivot = invert_tile(ref[p : p + T, p : p + T], lower=True)
        scaled = dot(pivot, ref[p : p + T, :])
        for q in range(p + T, n, T):
            weight = scaled[:, q : q + T]
            ref[q : q + T, :] = ref[q : q + T, :] - dot(weight, scaled, TN)
            ref[q : q + T, p : p + T] = -dot(weight, pivot, TN)
        for q in range(0, n, T):
            if q < p:
                ref[p : p + T, q : q + T] = scaled[:, q : q + T]
            else:
                ref[p : p + T, q : q + T] = pivot if q == p else jnp.zeros((T, T), F32)


def leaf_block(leaf, side_r, side_c, r, c, size):
    e = leaf.shape[1] // 4
    return leaf.at[
        0,
        pl.ds(pl.multiple_of(side_r * e + r * size, T), size),
        pl.ds(pl.multiple_of(side_c * e + c * size, T), size),
    ]


def run_copies(pairs, sem):
    copies = [pltpu.make_async_copy(a, b, sem.at[i]) for i, (a, b) in enumerate(pairs)]
    for copy in copies:
        copy.start()
    for copy in copies:
        copy.wait()


def sides(place):
    v, u = place[0], place[1]
    return [v, 2 + u], [1 - v, 3 - u]


def unpack(ref, at, tiles):
    held = {}
    for r, c in upper(tiles):
        held[r, c] = ref[at : at + T, :]
        if c > r:
            held[c, r] = held[r, c].T
        at += T
    return jnp.concatenate(
        [jnp.concatenate([held[r, c] for c in range(tiles)], axis=1) for r in range(tiles)], axis=0
    )


def call(kernel, name, cost, outs, ins, scratch, **more):
    return pl.pallas_call(
        kernel,
        out_shape=[jax.ShapeDtypeStruct(shape, dtype) for shape, dtype in outs],
        in_specs=[spec for spec, _ in ins],
        out_specs=more.pop("out_specs", [VMEM] * len(outs)),
        scratch_shapes=scratch,
        compiler_params=PARAMS,
        cost_estimate=pl.CostEstimate(flops=cost, bytes_accessed=cost, transcendentals=0),
        name=name,
        **more,
    )(*[value for _, value in ins])


def block_tiles(leaf, side_r, side_c, at):
    tiles = leaf.shape[1] // 4 // T
    return leaf_block(leaf, side_r, side_c, at // tiles, at % tiles, T)


def cross_tile(leaf, ext, inn, at):
    n = (leaf.shape[1] // 4 // T) ** 2
    return block_tiles(leaf, ext[at // n % 2], inn[at // n // 2], at % n)


def cut_first_kernel(place, leaf, a, sem):
    tiles = leaf.shape[1] // 4 // T
    ext, inn = sides(place)
    n_sym = len(upper(tiles))
    pairs = []
    for at, (r, c) in enumerate(upper(tiles)):
        pairs.append((leaf_block(leaf, inn[0], inn[0], r, c, T), a.at[pl.ds(at * T, T)]))
    for at in range(FIRST):
        pairs.append(
            (cross_tile(leaf, ext, inn, at), a.at[pl.ds((n_sym + at) * T, T)])
        )
    run_copies(pairs, sem)


def cut_first(place, leaf):
    n_sym = len(upper(leaf.shape[1] // 4 // T))
    return call(
        cut_first_kernel,
        "cut_first",
        1000 * 10**6,
        [(((n_sym + FIRST) * T, T), F32)],
        [(SMEM, place), (FAR, leaf)],
        [pltpu.SemaphoreType.DMA((n_sym + FIRST,))],
    )[0]


def cut_side_kernel(place, leaf, hh, sem):
    tiles = leaf.shape[1] // 4 // T
    _, inn = sides(place)
    pairs = []
    for at, (r, c) in enumerate(upper(tiles)):
        pairs.append((leaf_block(leaf, inn[1], inn[1], r, c, T), hh.at[pl.ds(at * T, T)]))
    run_copies(pairs, sem)


def cut_side(place, leaf):
    n_sym = len(upper(leaf.shape[1] // 4 // T))
    return call(
        cut_side_kernel,
        "cut_side",
        1000 * 10**6,
        [((n_sym * T, T), F32)],
        [(SMEM, place), (FAR, leaf)],
        [pltpu.SemaphoreType.DMA((n_sym,))],
    )[0]


def cut_second_kernel(place, leaf, swap, outer0, b, c, sem):
    e = leaf.shape[1] // 4
    tiles = e // T
    ext, inn = sides(place)
    n_sym = len(upper(tiles))
    pairs = [
        (leaf_block(leaf, inn[0], inn[1], 0, 0, e), b),
        (leaf_block(leaf, ext[0], inn[0], 0, 0, e), c.at[pl.ds(0, e)]),
        (leaf_block(leaf, ext[1], inn[0], 0, 0, e), c.at[pl.ds(e, e)]),
        (leaf_block(leaf, ext[0], inn[1], 0, 0, e), c.at[pl.ds(2 * e, e)]),
        (leaf_block(leaf, ext[1], inn[1], 0, 0, e), c.at[pl.ds(3 * e, e)]),
    ]
    for at, (r, k) in enumerate(upper(tiles)):
        pairs.append((leaf_block(leaf, inn[0], inn[0], r, k, T), swap.at[pl.ds(at * T, T)]))
    half = outer0.shape[0] // T
    second = []
    for at, (r, k) in enumerate(upper(2 * tiles)):
        source = leaf_block(leaf, ext[r // tiles], ext[k // tiles], r % tiles, k % tiles, T)
        if at < half:
            pairs.append((source, outer0.at[pl.ds(at * T, T)]))
        else:
            second.append((source, swap.at[pl.ds((n_sym + at - half) * T, T)]))
    run_copies(pairs, sem)
    same = place[0] == place[1]

    @pl.when(same)
    def _():
        cross = [
            (cross_tile(leaf, ext, inn, at), swap.at[pl.ds((n_sym + at) * T, T)])
            for at in range(half)
        ]
        run_copies(cross, sem)

    @pl.when(jnp.logical_not(same))
    def _():
        run_copies(second, sem)


def cut_second(place, leaf):
    e = leaf.shape[1] // 4
    n_sym = len(upper(e // T))
    half = len(upper(2 * (e // T))) // 2
    return call(
        cut_second_kernel,
        "cut_second",
        1000 * 10**6,
        [(((n_sym + half) * T, T), F32), ((half * T, T), F32), ((e, e), F32), ((4 * e, e), F32)],
        [(SMEM, place), (HBM, leaf)],
        [pltpu.SemaphoreType.DMA((n_sym + half + 5,))],
    )


def gauge_kernel(mine, along, b, b_out, factor):
    e = factor.shape[0]
    tiles = e // T
    factor[...] = unpack(mine, 0, tiles) + unpack(along, 0, tiles)
    inverse_factor(factor)
    b_out[...] = dot(b[...], factor[...], NT)


def gauge(mine, along, b):
    e = b.shape[0]
    return call(
        gauge_kernel,
        "gauge_side",
        8000 * 10**6,
        [((e, e), F32), ((e, e), F32)],
        [(VMEM, x) for x in (mine, along, b)],
        [],
    )


def scale_kernel(factor, c, c1, c2, rest):
    e = factor.shape[0]
    tiles = e // T
    scaled = dot3(split(c[2 * e :, :]), split(factor[...]), NT)
    total = 4 * tiles * tiles
    for at in range(FIRST, total):
        r, k = at // tiles * T, at % tiles * T
        tile = c[r : r + T, k : k + T] if r < 2 * e else scaled[r - 2 * e : r - 2 * e + T, k : k + T]
        if at < FIRST + SECOND:
            c1[(at - FIRST) * T : (at - FIRST + 1) * T, :] = tile
        else:
            c2[(at - FIRST - SECOND) * T : (at - FIRST - SECOND + 1) * T, :] = tile
        spot = at * T - (total * T - rest.shape[0])
        if spot >= 0:
            rest[spot : spot + T, :] = tile


def scale_cross(factor, c, swapped):
    e = factor.shape[0]
    total = 4 * e * e // T
    return call(
        scale_kernel,
        "scale_cross",
        2000 * 10**6,
        [((n, T), F32) for n in (SECOND * T, total - (FIRST + SECOND) * T, total - swapped * T)],
        [(VMEM, x) for x in (factor, c)],
        [],
    )


def couple(b):
    mine, across, along, corner = (ref[...] for ref in b)
    return jnp.concatenate(
        [jnp.concatenate([mine, across], axis=1), jnp.concatenate([along, corner], axis=1)], axis=0
    )


def factor_start_kernel(a0, a1, a2, a3, b0, b1, b2, b3, side):
    e = b0.shape[0]
    tiles = e // T
    coup = couple((b0, b1, b2, b3))
    side[...] = -dot(coup, coup, NT)
    side[:e, :e] = side[:e, :e] + (unpack(a0, 0, tiles) + unpack(a1, 0, tiles))
    side[e:, e:] = side[e:, e:] + (unpack(a2, 0, tiles) + unpack(a3, 0, tiles))
    sweep(side, 0, e)


def factor_start(a, b):
    e = b[0].shape[0]
    return call(
        factor_start_kernel,
        "factor_start",
        1000 * 10**6,
        [((2 * e, 2 * e), F32)],
        [(VMEM, x) for x in (*a, *b)],
        [],
    )[0]


def factor_end_kernel(place, side_in, b0, b1, b2, b3, high, low, side, full):
    e = b0.shape[0]
    side[...] = side_in[...]
    sweep(side, e, 2 * e)
    coup = split(couple((b0, b1, b2, b3)))
    away = dot3(split(side[...]), coup)
    shape = full.shape
    unit = lax.broadcasted_iota(jnp.int32, shape, 0) == lax.broadcasted_iota(jnp.int32, shape, 1)
    full[...] = dot3(coup, split(away), TN) + unit.astype(F32)

    def emit(value, rows, columns):
        high[rows, columns], low[rows, columns] = split(value)

    first, rest = slice(0, e), slice(e, 3 * e)
    emit(full[...], rest, rest)
    emit(-away[:e, :], first, rest)
    same = place[0] == place[1]

    @pl.when(same)
    def _():
        emit(side[:e, :e], first, first)
        emit(-away[:e, :].T, rest, first)

    @pl.when(jnp.logical_not(same))
    def _():
        emit(side[:e, e:], first, first)
        emit(-away[e:, :].T, rest, first)


def factor_end(place, side, b):
    e = b[0].shape[0]
    return call(
        factor_end_kernel,
        "factor_end",
        10000 * 10**6,
        [((3 * e, 3 * e), BF16)] * 2,
        [(SMEM, place), (VMEM, side)] + [(VMEM, x) for x in b],
        [pltpu.VMEM((2 * e, 2 * e), F32), pltpu.VMEM((2 * e, 2 * e), F32)],
    )


def cross_block(*pieces):
    held = []
    for ref, skip in pieces:
        for at in range(skip * T, ref.shape[0], T):
            held.append(ref[at : at + T, :])
    tiles = math.isqrt(len(held) // 4)
    rows = []
    for r in range(2 * tiles):
        side = r // tiles
        row = [held[((side + 2 * c) * tiles + r % tiles) * tiles + k] for c in range(2) for k in range(tiles)]
        rows.append(jnp.concatenate(row, axis=1))
    return jnp.concatenate(rows, axis=0)


def symmetric_tiles(e):
    return len(upper(e // T))


def zeros(tiles):
    return jnp.zeros((tiles * T, T), F32), 0


def times_inverse(cross, high, low, inner):
    e = cross.shape[1] // 2
    return dot3(split(cross[:, :e]), (high[:e], low[:e])) + dot3(
        split(cross[:, e:]), (high[inner], low[inner])
    )


def rows_kernel(
    place, leaf, high, low, a0, c01, c02, a1, c11, swapped, rest, top, bottom, block, part, col, own, sem
):
    e = leaf.shape[1] // 4
    n_sym = symmetric_tiles(e)
    ext, _ = sides(place)
    copies = []
    for r in range(2):
        for c in range(2):
            target = own.at[pl.ds(r * e, e), pl.ds(c * e, e)]
            source = leaf_block(leaf, ext[r], ext[c], 0, 0, e)
            copies.append(pltpu.make_async_copy(source, target, sem.at[2 * r + c]))
            copies[-1].start()
    same = place[0] == place[1]
    mine = cross_block((a0, n_sym), (c01, 0), (c02, 0))

    @pl.when(same)
    def _():
        col[...] = mine

    @pl.when(jnp.logical_not(same))
    def _():
        col[...] = cross_block((swapped, n_sym), (rest, 0))
        across = cross_block((a1, n_sym), (c11, 0), zeros(c02.shape[0] // T))
        part[...] = times_inverse(across, high[...], low[...], slice(2 * e, 3 * e))

    left = split(times_inverse(mine, high[...], low[...], slice(e, 2 * e)))
    top[...], bottom[...] = left
    left = [x[:, : 2 * e] for x in left]
    block[...] = -dot3(left, split(col[...]), NT)
    for copy in copies:
        copy.wait()

    @pl.when(same)
    def _():
        block[...] = block[...] + own[...]


def own_rows(place, leaf, high, low, a0, c01, c02, a1, c11, swapped, rest):
    e = leaf.shape[1] // 4
    return call(
        rows_kernel,
        "own_rows",
        500 * 10**6,
        [((2 * e, 3 * e), BF16)] * 2 + [((2 * e, 2 * e), F32), ((2 * e, 3 * e), F32)],
        [(SMEM, place), (HBM, leaf)]
        + [(VMEM, x) for x in (high, low, a0, c01, c02, a1, c11, swapped, rest)],
        [
            pltpu.VMEM((2 * e, 2 * e), F32),
            pltpu.VMEM((2 * e, 2 * e), F32),
            pltpu.SemaphoreType.DMA((4,)),
        ],
    )


def spot(place, e, side, which):
    x = place[0] if which == 0 else 1 - place[0]
    return pl.ds(pl.multiple_of((2 * side + x) * e, T), e)


def write(out, place, value, a, b):
    e = out.shape[1] // 4
    for r in range(2):
        for c in range(2):
            out[0, spot(place, e, r, a), spot(place, e, c, b)] = value[
                r * e : (r + 1) * e, c * e : (c + 1) * e
            ]


def pick(ref, rows, b):
    e = ref.shape[1] // 3
    return jnp.concatenate([ref[rows, :e], ref[rows, (1 + b) * e : (2 + b) * e]], axis=1)


def products_kernel(
    place, high, low, top, bottom, block, a0, c01, c02, a1, c11, third, a3, c31, passed, out, part, scratch
):
    e = out.shape[1] // 4
    n_sym = symmetric_tiles(e)
    same = place[0] == place[1]
    write(out, place, block[...], 0, 0)
    everything = slice(0, 2 * e)

    @pl.when(same)
    def _():
        across = cross_block((a1, n_sym), (c11, 0), (third, 0))
        right = split(across)
        left = [pick(x, everything, 1) for x in (top, bottom)]
        write(out, place, -dot3(left, right, NT), 0, 1)
        scratch[...] = times_inverse(across, high[...], low[...], slice(2 * e, 3 * e))
        left = split(pick(scratch, everything, 0))
        mine = cross_block((a0, n_sym), (c01, 0), (c02, 0))
        write(out, place, -dot3(left, split(mine), NT), 1, 0)
        left = split(pick(scratch, everything, 1))
        part[...] = -dot3(left, right, NT)

    @pl.when(jnp.logical_not(same))
    def _():
        right = split(cross_block((a3, n_sym), (c31, 0), (passed, 0)))
        left = [pick(x, everything, 1) for x in (top, bottom)]
        write(out, place, -dot3(left, right, NT), 0, 1)


def products(place, high, low, top, bottom, block, mine, across, corner):
    e = block.shape[0] // 2
    return call(
        products_kernel,
        "products",
        500 * 10**6,
        [((1, 4 * e, 4 * e), F32), ((2 * e, 2 * e), F32)],
        [(SMEM, place)]
        + [(VMEM, x) for x in (high, low, top, bottom, block, *mine, *across, *corner)],
        [pltpu.VMEM((2 * e, 3 * e), F32)],
    )


def finish_kernel(
    place, before, high, low, block, part, third, passed, last, swapped, rest, a3, c31, out, held, scratch, sem
):
    e = out.shape[1] // 4
    tiles = e // T
    n_sym = symmetric_tiles(e)

    def targets(b):
        return [
            (
                held.at[pl.ds(r * e, e), pl.ds((2 * b + c) * e, e)],
                out.at[0, spot(place, e, r, 1), spot(place, e, c, b)],
            )
            for r in range(2)
            for c in range(2)
        ]

    n_last = last.shape[0] // T

    @pl.when(place[0] == place[1])
    def _():
        skip = passed.shape[0] // T - n_last
        for at, (i, j) in enumerate(upper(2 * tiles)):
            ref, at = (last, at) if at < n_last else (passed, at - n_last + skip)
            piece = ref[at * T : (at + 1) * T, :]
            r, c = slice(i * T, (i + 1) * T), slice(j * T, (j + 1) * T)
            shift = 2 * e
            held[r, j * T + shift : (j + 1) * T + shift] = block[r, c] + piece
            if i != j:
                held[c, i * T + shift : (i + 1) * T + shift] = block[c, r] + piece.T
        run_copies(targets(1), sem)

    @pl.when(place[0] != place[1])
    def _():
        first = third[: third.shape[0] - n_last * T, :]
        late = cross_block(zeros(FIRST + SECOND), (first, 0), (last, 0))[:, e:]
        inner = slice(2 * e, 3 * e)
        scratch[...] = part[...] + dot3(split(late), (high[inner], low[inner]))
        everything = slice(0, 2 * e)
        copies = []
        for b in range(2):
            if b == 0:
                col = cross_block((swapped, n_sym), (rest, 0))
            else:
                col = cross_block((a3, n_sym), (c31, 0), (passed, 0))
            left = split(pick(scratch, everything, b))
            held[:, 2 * e * b : 2 * e * (b + 1)] = -dot3(left, split(col), NT)
            for i, (source, target) in enumerate(targets(b)):
                copies.append(pltpu.make_async_copy(source, target, sem.at[4 * b + i]))
                copies[-1].start()
        for copy in copies:
            copy.wait()


def finish(place, before, high, low, block, part, third, passed, last, swapped, rest, a3, c31):
    e = before.shape[1] // 4
    return call(
        finish_kernel,
        "finish",
        500 * 10**6,
        [(before.shape, F32)],
        [(SMEM, place), (HBM, before)]
        + [
            (VMEM, x)
            for x in (high, low, block, part, third, passed, last, swapped, rest, a3, c31)
        ],
        [
            pltpu.VMEM((2 * e, 4 * e), F32),
            pltpu.VMEM((2 * e, 3 * e), F32),
            pltpu.SemaphoreType.DMA((8,)),
        ],
        out_specs=[HBM],
        input_output_aliases={1: 0},
    )[0]


def tie(*values):
    return lax.optimization_barrier(values)


def solution(mesh):
    nx, ny = mesh.shape["gx"], mesh.shape["gy"]
    devices = [(x, y) for x in range(nx) for y in range(ny)]

    def is_same(x, y):
        return x // (nx // 2) == y // (ny // 2)

    def send(value, along_y, only=None):
        pairs = []
        for x, y in devices:
            if only is None or is_same(x, y) == only:
                to = (x, (y + ny // 2) % ny) if along_y else ((x + nx // 2) % nx, y)
                pairs.append((x * ny + y, to[0] * ny + to[1]))
        return lax.ppermute(value, ("gx", "gy"), pairs)

    def body(leaf):
        e = leaf.shape[1] // 4
        v = lax.axis_index("gx") // (nx // 2)
        u = lax.axis_index("gy") // (ny // 2)
        place = jnp.stack([v, u]).astype(jnp.int32)
        same = u == v
        a = cut_first(place, leaf)
        a_x = send(a, False)
        here, a = tie(place, a)
        hh = cut_side(here, leaf)
        hh_y = send(hh, True)
        swap, outer0, b, c = cut_second(place, leaf)
        swapped = send(swap, True)
        b, factor = gauge(hh, hh_y, b)
        b_x = send(b, False)
        n_last = outer0.shape[0] // T
        c1, c2, rest = scale_cross(factor, c, n_last)
        b, a_x, c1, swapped = tie(b, a_x, c1, swapped)
        b_y = send(b, True)
        a_d = send(a_x, True)
        c1, b_x = tie(c1, b_x)
        c1_x = send(c1, False)
        b_x, b_y, a_d = tie(b_x, b_y, a_d)
        b_d = send(b_x, True)
        rest, b_d = tie(rest, b_d)
        rest = send(rest, True, only=True)
        side = factor_start((a, a_x, swapped, a_d), (b, b_x, b_y, b_d))
        n_mid = c2.shape[0] // T - n_last
        theirs = jnp.concatenate([c2[: n_mid * T], swapped[-n_last * T :]])
        third, side = tie(jnp.where(same, theirs, c2), side)
        third = send(third, False)
        c1_d = send(c1_x, True, only=True)
        high, low = factor_end(place, side, (b, b_x, b_y, b_d))
        top, bottom, block, part = own_rows(
            place, leaf, high, low, a, c1, c2, a_x, c1_x, swapped, rest
        )
        last, third, block = tie(jnp.where(same, c2[n_mid * T :], outer0), third, block)
        last = send(last, False)
        passed = send(third, True)
        out, block = products(
            place, high, low, top, bottom, block, (a, c1, c2), (a_x, c1_x, third), (a_d, c1_d, passed)
        )
        return finish(
            place, out, high, low, block, part, third, passed, last, swapped, rest, a_d, c1_d
        )

    return jax.shard_map(
        body,
        mesh=mesh,
        in_specs=(P(None, "gy", "gx"),),
        out_specs=P(None, "gy", "gx"),
        check_vma=False,
    )
```

```python
import math

import jax
import jax.numpy as jnp
from jax import lax
from jax.experimental import pallas as pl
from jax.experimental.pallas import tpu as pltpu
from jax.sharding import PartitionSpec as P

F32 = jnp.float32
BF16 = jnp.bfloat16
T = 128
R = 16
FIRST = 1
SECOND = 8
HBM = pl.BlockSpec(memory_space=pl.ANY)
FAR = pl.BlockSpec(memory_space=pltpu.HBM)
VMEM = pl.BlockSpec(memory_space=pltpu.VMEM)
SMEM = pl.BlockSpec(memory_space=pltpu.SMEM)
PARAMS = pltpu.CompilerParams(vmem_limit_bytes=32 * 2**20)


def dot(a, b, dims=((1,), (0,))):
    return lax.dot_general(
        a, b, (dims, ((), ())), precision=lax.Precision.HIGHEST, preferred_element_type=F32
    )


def dot16(a, b, dims=((1,), (0,))):
    return lax.dot_general(a, b, (dims, ((), ())), preferred_element_type=F32)


def split(a):
    high = a.astype(BF16)
    return high, (a - high.astype(F32)).astype(BF16)


def dot3(a, b, dims=((1,), (0,))):
    return dot16(a[0], b[0], dims) + (dot16(a[0], b[1], dims) + dot16(a[1], b[0], dims))


NT = ((1,), (1,))
TN = ((0,), (0,))


def upper(n):
    return [(i, j) for i in range(n) for j in range(i, n)]


def across_lanes(x, k):
    return jnp.broadcast_to(x[:, k : k + 1], x.shape)


def across_rows(x, k):
    return jnp.broadcast_to(x[k : k + 1, :], x.shape)


def panel(rows, c0, lower):
    sub = lax.broadcasted_iota(jnp.int32, rows.shape, 0)
    lane = lax.broadcasted_iota(jnp.int32, rows.shape, 1)
    cols = [across_lanes(rows, c0 + k) for k in range(R)]
    out = jnp.where((lane >= c0) & (lane < c0 + R), (lane - c0 == sub).astype(F32), rows)
    half = out
    scale = jnp.ones_like(rows)
    for k in range(R):
        pivot = across_rows(cols[k], k)
        inv = 1.0 / pivot
        here = sub == k
        mult = cols[k]

        def step(x):
            row = across_rows(x, k) * inv
            return jnp.where(here, row, x - mult * row)

        if lower:
            scale = jnp.where(here, pivot, scale)
            half = half - jnp.where(sub > k, mult, 0.0) * (across_rows(half, k) * inv)
        out = step(out)
        for j in range(k + 1, R):
            cols[j] = step(cols[j])
    return out, half * lax.rsqrt(scale) if lower else None


def put_rows(matrix, rows, r0):
    parts = [matrix[:r0]] if r0 else []
    parts.append(rows)
    if r0 + rows.shape[0] < matrix.shape[0]:
        parts.append(matrix[r0 + rows.shape[0] :])
    return jnp.concatenate(parts, axis=0)


def invert_tile(m, lower=False):
    lane = lax.broadcasted_iota(jnp.int32, (T, T), 1)
    sub = lax.broadcasted_iota(jnp.int32, (T, T), 0)
    rows = m[:R]
    for c0 in range(0, T, R):
        swept, half = panel(rows, c0, lower)
        if c0 + R < T:
            old = m[c0 + R : c0 + 2 * R]
            inside = (lane[:R] >= c0) & (lane[:R] < c0 + R)
            sums = [jnp.where(inside, 0.0, old)] + [None] * 3
            for k in range(R):
                term = across_lanes(old, c0 + k) * across_rows(swept, k)
                sums[k % 4] = -term if sums[k % 4] is None else sums[k % 4] - term
            rows = (sums[0] + sums[1]) + (sums[2] + sums[3])
        wide = put_rows(jnp.zeros((T, T), F32), swept, c0)
        rest = jnp.where((lane >= c0) & (lane < c0 + R), 0.0, m) - dot(m, wide)
        if lower:
            rest = jnp.where(sub < c0, m, rest)
        m = put_rows(rest, half if lower else swept, c0)
    return jnp.where(lane > sub, 0.0, m) if lower else m


def sweep(ref, start, stop):
    n = ref.shape[0]
    for p in range(start, stop, T):
        pivot = invert_tile(ref[p : p + T, p : p + T])
        rows = dot(pivot, ref[p : p + T, :])
        parts = ([rows[:, :p]] if p else []) + [pivot]
        if p + T < n:
            parts.append(rows[:, p + T :])
        rows = jnp.concatenate(parts, axis=1)
        for q in range(0, n, T):
            if q != p:
                change = dot(ref[q : q + T, p : p + T], rows)
                ref[q : q + T, p : p + T] = jnp.zeros((T, T), F32)
                ref[q : q + T, :] = ref[q : q + T, :] - change
        ref[p : p + T, :] = rows


def inverse_factor(ref):
    n = ref.shape[0]
    for p in range(0, n, T):
        pivot = invert_tile(ref[p : p + T, p : p + T], lower=True)
        scaled = dot(pivot, ref[p : p + T, :])
        for q in range(p + T, n, T):
            weight = scaled[:, q : q + T]
            ref[q : q + T, :] = ref[q : q + T, :] - dot(weight, scaled, TN)
            ref[q : q + T, p : p + T] = -dot(weight, pivot, TN)
        for q in range(0, n, T):
            if q < p:
                ref[p : p + T, q : q + T] = scaled[:, q : q + T]
            else:
                ref[p : p + T, q : q + T] = pivot if q == p else jnp.zeros((T, T), F32)


def leaf_block(leaf, side_r, side_c, r, c, size):
    e = leaf.shape[1] // 4
    return leaf.at[
        0,
        pl.ds(pl.multiple_of(side_r * e + r * size, T), size),
        pl.ds(pl.multiple_of(side_c * e + c * size, T), size),
    ]


def run_copies(pairs, sem):
    copies = [pltpu.make_async_copy(a, b, sem.at[i]) for i, (a, b) in enumerate(pairs)]
    for copy in copies:
        copy.start()
    for copy in copies:
        copy.wait()


def sides(place):
    v, u = place[0], place[1]
    return [v, 2 + u], [1 - v, 3 - u]


def unpack(ref, at, tiles):
    held = {}
    for r, c in upper(tiles):
        held[r, c] = ref[at : at + T, :]
        if c > r:
            held[c, r] = held[r, c].T
        at += T
    return jnp.concatenate(
        [jnp.concatenate([held[r, c] for c in range(tiles)], axis=1) for r in range(tiles)], axis=0
    )


def call(kernel, name, cost, outs, ins, scratch, **more):
    return pl.pallas_call(
        kernel,
        out_shape=[jax.ShapeDtypeStruct(shape, dtype) for shape, dtype in outs],
        in_specs=[spec for spec, _ in ins],
        out_specs=more.pop("out_specs", [VMEM] * len(outs)),
        scratch_shapes=scratch,
        compiler_params=PARAMS,
        cost_estimate=pl.CostEstimate(flops=cost, bytes_accessed=cost, transcendentals=0),
        name=name,
        **more,
    )(*[value for _, value in ins])


def block_tiles(leaf, side_r, side_c, at):
    tiles = leaf.shape[1] // 4 // T
    return leaf_block(leaf, side_r, side_c, at // tiles, at % tiles, T)


def cross_tile(leaf, ext, inn, at):
    n = (leaf.shape[1] // 4 // T) ** 2
    return block_tiles(leaf, ext[at // n % 2], inn[at // n // 2], at % n)


def cut_first_kernel(place, leaf, a, sem):
    tiles = leaf.shape[1] // 4 // T
    ext, inn = sides(place)
    n_sym = len(upper(tiles))
    pairs = []
    for at, (r, c) in enumerate(upper(tiles)):
        pairs.append((leaf_block(leaf, inn[0], inn[0], r, c, T), a.at[pl.ds(at * T, T)]))
    for at in range(FIRST):
        pairs.append(
            (cross_tile(leaf, ext, inn, at), a.at[pl.ds((n_sym + at) * T, T)])
        )
    run_copies(pairs, sem)


def cut_first(place, leaf):
    n_sym = len(upper(leaf.shape[1] // 4 // T))
    return call(
        cut_first_kernel,
        "cut_first",
        1000 * 10**6,
        [(((n_sym + FIRST) * T, T), F32)],
        [(SMEM, place), (FAR, leaf)],
        [pltpu.SemaphoreType.DMA((n_sym + FIRST,))],
    )[0]


def cut_side_kernel(place, leaf, hh, sem):
    tiles = leaf.shape[1] // 4 // T
    _, inn = sides(place)
    pairs = []
    for at, (r, c) in enumerate(upper(tiles)):
        pairs.append((leaf_block(leaf, inn[1], inn[1], r, c, T), hh.at[pl.ds(at * T, T)]))
    run_copies(pairs, sem)


def cut_side(place, leaf):
    n_sym = len(upper(leaf.shape[1] // 4 // T))
    return call(
        cut_side_kernel,
        "cut_side",
        1000 * 10**6,
        [((n_sym * T, T), F32)],
        [(SMEM, place), (FAR, leaf)],
        [pltpu.SemaphoreType.DMA((n_sym,))],
    )[0]


def cut_second_kernel(place, leaf, swap, outer0, b, c, sem):
    e = leaf.shape[1] // 4
    tiles = e // T
    ext, inn = sides(place)
    n_sym = len(upper(tiles))
    pairs = [
        (leaf_block(leaf, inn[0], inn[1], 0, 0, e), b),
        (leaf_block(leaf, ext[0], inn[0], 0, 0, e), c.at[pl.ds(0, e)]),
        (leaf_block(leaf, ext[1], inn[0], 0, 0, e), c.at[pl.ds(e, e)]),
        (leaf_block(leaf, ext[0], inn[1], 0, 0, e), c.at[pl.ds(2 * e, e)]),
        (leaf_block(leaf, ext[1], inn[1], 0, 0, e), c.at[pl.ds(3 * e, e)]),
    ]
    for at, (r, k) in enumerate(upper(tiles)):
        pairs.append((leaf_block(leaf, inn[0], inn[0], r, k, T), swap.at[pl.ds(at * T, T)]))
    half = outer0.shape[0] // T
    second = []
    for at, (r, k) in enumerate(upper(2 * tiles)):
        source = leaf_block(leaf, ext[r // tiles], ext[k // tiles], r % tiles, k % tiles, T)
        if at < half:
            pairs.append((source, outer0.at[pl.ds(at * T, T)]))
        else:
            second.append((source, swap.at[pl.ds((n_sym + at - half) * T, T)]))
    run_copies(pairs, sem)
    same = place[0] == place[1]

    @pl.when(same)
    def _():
        cross = [
            (cross_tile(leaf, ext, inn, at), swap.at[pl.ds((n_sym + at) * T, T)])
            for at in range(half)
        ]
        run_copies(cross, sem)

    @pl.when(jnp.logical_not(same))
    def _():
        run_copies(second, sem)


def cut_second(place, leaf):
    e = leaf.shape[1] // 4
    n_sym = len(upper(e // T))
    half = len(upper(2 * (e // T))) // 2
    return call(
        cut_second_kernel,
        "cut_second",
        1000 * 10**6,
        [(((n_sym + half) * T, T), F32), ((half * T, T), F32), ((e, e), F32), ((4 * e, e), F32)],
        [(SMEM, place), (HBM, leaf)],
        [pltpu.SemaphoreType.DMA((n_sym + half + 5,))],
    )


def gauge_kernel(mine, along, b, b_out, factor):
    e = factor.shape[0]
    tiles = e // T
    factor[...] = unpack(mine, 0, tiles) + unpack(along, 0, tiles)
    inverse_factor(factor)
    b_out[...] = dot(b[...], factor[...], NT)


def gauge(mine, along, b):
    e = b.shape[0]
    return call(
        gauge_kernel,
        "gauge_side",
        8000 * 10**6,
        [((e, e), F32), ((e, e), F32)],
        [(VMEM, x) for x in (mine, along, b)],
        [],
    )


def scale_kernel(factor, c, c1, c2, rest):
    e = factor.shape[0]
    tiles = e // T
    scaled = dot3(split(c[2 * e :, :]), split(factor[...]), NT)
    total = 4 * tiles * tiles
    for at in range(FIRST, total):
        r, k = at // tiles * T, at % tiles * T
        tile = c[r : r + T, k : k + T] if r < 2 * e else scaled[r - 2 * e : r - 2 * e + T, k : k + T]
        if at < FIRST + SECOND:
            c1[(at - FIRST) * T : (at - FIRST + 1) * T, :] = tile
        else:
            c2[(at - FIRST - SECOND) * T : (at - FIRST - SECOND + 1) * T, :] = tile
        spot = at * T - (total * T - rest.shape[0])
        if spot >= 0:
            rest[spot : spot + T, :] = tile


def scale_cross(factor, c, swapped):
    e = factor.shape[0]
    total = 4 * e * e // T
    return call(
        scale_kernel,
        "scale_cross",
        2000 * 10**6,
        [((n, T), F32) for n in (SECOND * T, total - (FIRST + SECOND) * T, total - swapped * T)],
        [(VMEM, x) for x in (factor, c)],
        [],
    )


def couple(b):
    mine, across, along, corner = (ref[...] for ref in b)
    return jnp.concatenate(
        [jnp.concatenate([mine, across], axis=1), jnp.concatenate([along, corner], axis=1)], axis=0
    )


def factor_start_kernel(a0, a1, a2, a3, b0, b1, b2, b3, side):
    e = b0.shape[0]
    tiles = e // T
    coup = couple((b0, b1, b2, b3))
    side[...] = -dot(coup, coup, NT)
    side[:e, :e] = side[:e, :e] + (unpack(a0, 0, tiles) + unpack(a1, 0, tiles))
    side[e:, e:] = side[e:, e:] + (unpack(a2, 0, tiles) + unpack(a3, 0, tiles))
    sweep(side, 0, e)


def factor_start(a, b):
    e = b[0].shape[0]
    return call(
        factor_start_kernel,
        "factor_start",
        1000 * 10**6,
        [((2 * e, 2 * e), F32)],
        [(VMEM, x) for x in (*a, *b)],
        [],
    )[0]


def factor_end_kernel(place, side_in, b0, b1, b2, b3, high, low, side, full):
    e = b0.shape[0]
    side[...] = side_in[...]
    sweep(side, e, 2 * e)
    coup = split(couple((b0, b1, b2, b3)))
    away = dot3(split(side[...]), coup)
    shape = full.shape
    unit = lax.broadcasted_iota(jnp.int32, shape, 0) == lax.broadcasted_iota(jnp.int32, shape, 1)
    full[...] = dot3(coup, split(away), TN) + unit.astype(F32)

    def emit(value, rows, columns):
        high[rows, columns], low[rows, columns] = split(value)

    first, rest = slice(0, e), slice(e, 3 * e)
    emit(full[...], rest, rest)
    emit(-away[:e, :], first, rest)
    same = place[0] == place[1]

    @pl.when(same)
    def _():
        emit(side[:e, :e], first, first)
        emit(-away[:e, :].T, rest, first)

    @pl.when(jnp.logical_not(same))
    def _():
        emit(side[:e, e:], first, first)
        emit(-away[e:, :].T, rest, first)


def factor_end(place, side, b):
    e = b[0].shape[0]
    return call(
        factor_end_kernel,
        "factor_end",
        10000 * 10**6,
        [((3 * e, 3 * e), BF16)] * 2,
        [(SMEM, place), (VMEM, side)] + [(VMEM, x) for x in b],
        [pltpu.VMEM((2 * e, 2 * e), F32), pltpu.VMEM((2 * e, 2 * e), F32)],
    )


def cross_block(*pieces):
    held = []
    for ref, skip in pieces:
        for at in range(skip * T, ref.shape[0], T):
            held.append(ref[at : at + T, :])
    tiles = math.isqrt(len(held) // 4)
    rows = []
    for r in range(2 * tiles):
        side = r // tiles
        row = [held[((side + 2 * c) * tiles + r % tiles) * tiles + k] for c in range(2) for k in range(tiles)]
        rows.append(jnp.concatenate(row, axis=1))
    return jnp.concatenate(rows, axis=0)


def symmetric_tiles(e):
    return len(upper(e // T))


def zeros(tiles):
    return jnp.zeros((tiles * T, T), F32), 0


def times_inverse(cross, high, low, inner):
    e = cross.shape[1] // 2
    return dot3(split(cross[:, :e]), (high[:e], low[:e])) + dot3(
        split(cross[:, e:]), (high[inner], low[inner])
    )


def rows_kernel(
    place, leaf, high, low, a0, c01, c02, a1, c11, swapped, rest, top, bottom, block, part, col, own, sem
):
    e = leaf.shape[1] // 4
    n_sym = symmetric_tiles(e)
    ext, _ = sides(place)
    copies = []
    for r in range(2):
        for c in range(2):
            target = own.at[pl.ds(r * e, e), pl.ds(c * e, e)]
            source = leaf_block(leaf, ext[r], ext[c], 0, 0, e)
            copies.append(pltpu.make_async_copy(source, target, sem.at[2 * r + c]))
            copies[-1].start()
    same = place[0] == place[1]
    mine = cross_block((a0, n_sym), (c01, 0), (c02, 0))

    @pl.when(same)
    def _():
        col[...] = mine

    @pl.when(jnp.logical_not(same))
    def _():
        col[...] = cross_block((swapped, n_sym), (rest, 0))
        across = cross_block((a1, n_sym), (c11, 0), zeros(c02.shape[0] // T))
        part[...] = times_inverse(across, high[...], low[...], slice(2 * e, 3 * e))

    left = split(times_inverse(mine, high[...], low[...], slice(e, 2 * e)))
    top[...], bottom[...] = left
    left = [x[:, : 2 * e] for x in left]
    block[...] = -dot3(left, split(col[...]), NT)
    for copy in copies:
        copy.wait()

    @pl.when(same)
    def _():
        block[...] = block[...] + own[...]


def own_rows(place, leaf, high, low, a0, c01, c02, a1, c11, swapped, rest):
    e = leaf.shape[1] // 4
    return call(
        rows_kernel,
        "own_rows",
        500 * 10**6,
        [((2 * e, 3 * e), BF16)] * 2 + [((2 * e, 2 * e), F32), ((2 * e, 3 * e), F32)],
        [(SMEM, place), (HBM, leaf)]
        + [(VMEM, x) for x in (high, low, a0, c01, c02, a1, c11, swapped, rest)],
        [
            pltpu.VMEM((2 * e, 2 * e), F32),
            pltpu.VMEM((2 * e, 2 * e), F32),
            pltpu.SemaphoreType.DMA((4,)),
        ],
    )


def spot(place, e, side, which):
    x = place[0] if which == 0 else 1 - place[0]
    return pl.ds(pl.multiple_of((2 * side + x) * e, T), e)


def put(out, place, held, a, b, sem):
    e = out.shape[1] // 4
    copies = []
    for r in range(2):
        for c in range(2):
            source = held.at[pl.ds(r * e, e), pl.ds(c * e, e)]
            target = out.at[0, spot(place, e, r, a), spot(place, e, c, b)]
            copies.append(pltpu.make_async_copy(source, target, sem.at[2 * r + c]))
            copies[-1].start()
    return copies


def wait(copies):
    for copy in copies:
        copy.wait()


def pick(ref, rows, b):
    e = ref.shape[1] // 3
    return jnp.concatenate([ref[rows, :e], ref[rows, (1 + b) * e : (2 + b) * e]], axis=1)


def products_kernel(
    place, high, low, top, bottom, block, a0, c01, c02, a1, c11, third, a3, c31, passed, out, part, held, scratch, sem
):
    e = out.shape[1] // 4
    n_sym = symmetric_tiles(e)
    same = place[0] == place[1]
    first = put(out, place, block, 0, 0, sem.at[0])
    everything = slice(0, 2 * e)

    @pl.when(same)
    def _():
        across = cross_block((a1, n_sym), (c11, 0), (third, 0))
        right = split(across)
        left = [pick(x, everything, 1) for x in (top, bottom)]
        held[0] = -dot3(left, right, NT)
        copies = put(out, place, held.at[0], 0, 1, sem.at[1])
        scratch[...] = times_inverse(across, high[...], low[...], slice(2 * e, 3 * e))
        left = split(pick(scratch, everything, 0))
        mine = cross_block((a0, n_sym), (c01, 0), (c02, 0))
        held[1] = -dot3(left, split(mine), NT)
        copies += put(out, place, held.at[1], 1, 0, sem.at[2])
        left = split(pick(scratch, everything, 1))
        part[...] = -dot3(left, right, NT)
        wait(copies)

    @pl.when(jnp.logical_not(same))
    def _():
        right = split(cross_block((a3, n_sym), (c31, 0), (passed, 0)))
        left = [pick(x, everything, 1) for x in (top, bottom)]
        held[0] = -dot3(left, right, NT)
        wait(put(out, place, held.at[0], 0, 1, sem.at[1]))

    wait(first)


def products(place, high, low, top, bottom, block, mine, across, corner):
    e = block.shape[0] // 2
    return call(
        products_kernel,
        "products",
        500 * 10**6,
        [((1, 4 * e, 4 * e), F32), ((2 * e, 2 * e), F32)],
        [(SMEM, place)]
        + [(VMEM, x) for x in (high, low, top, bottom, block, *mine, *across, *corner)],
        [
            pltpu.VMEM((2, 2 * e, 2 * e), F32),
            pltpu.VMEM((2 * e, 3 * e), F32),
            pltpu.SemaphoreType.DMA((3, 4)),
        ],
        out_specs=[HBM, VMEM],
    )


def finish_kernel(
    place, before, high, low, block, part, third, passed, last, swapped, rest, a3, c31, out, held, scratch, sem
):
    e = out.shape[1] // 4
    tiles = e // T
    n_sym = symmetric_tiles(e)

    def targets(b):
        return [
            (
                held.at[pl.ds(r * e, e), pl.ds((2 * b + c) * e, e)],
                out.at[0, spot(place, e, r, 1), spot(place, e, c, b)],
            )
            for r in range(2)
            for c in range(2)
        ]

    n_last = last.shape[0] // T

    @pl.when(place[0] == place[1])
    def _():
        skip = passed.shape[0] // T - n_last
        for at, (i, j) in enumerate(upper(2 * tiles)):
            ref, at = (last, at) if at < n_last else (passed, at - n_last + skip)
            piece = ref[at * T : (at + 1) * T, :]
            r, c = slice(i * T, (i + 1) * T), slice(j * T, (j + 1) * T)
            shift = 2 * e
            held[r, j * T + shift : (j + 1) * T + shift] = block[r, c] + piece
            if i != j:
                held[c, i * T + shift : (i + 1) * T + shift] = block[c, r] + piece.T
        run_copies(targets(1), sem)

    @pl.when(place[0] != place[1])
    def _():
        first = third[: third.shape[0] - n_last * T, :]
        late = cross_block(zeros(FIRST + SECOND), (first, 0), (last, 0))[:, e:]
        inner = slice(2 * e, 3 * e)
        scratch[...] = part[...] + dot3(split(late), (high[inner], low[inner]))
        everything = slice(0, 2 * e)
        copies = []
        for b in range(2):
            if b == 0:
                col = cross_block((swapped, n_sym), (rest, 0))
            else:
                col = cross_block((a3, n_sym), (c31, 0), (passed, 0))
            left = split(pick(scratch, everything, b))
            held[:, 2 * e * b : 2 * e * (b + 1)] = -dot3(left, split(col), NT)
            for i, (source, target) in enumerate(targets(b)):
                copies.append(pltpu.make_async_copy(source, target, sem.at[4 * b + i]))
                copies[-1].start()
        for copy in copies:
            copy.wait()


def finish(place, before, high, low, block, part, third, passed, last, swapped, rest, a3, c31):
    e = before.shape[1] // 4
    return call(
        finish_kernel,
        "finish",
        500 * 10**6,
        [(before.shape, F32)],
        [(SMEM, place), (HBM, before)]
        + [
            (VMEM, x)
            for x in (high, low, block, part, third, passed, last, swapped, rest, a3, c31)
        ],
        [
            pltpu.VMEM((2 * e, 4 * e), F32),
            pltpu.VMEM((2 * e, 3 * e), F32),
            pltpu.SemaphoreType.DMA((8,)),
        ],
        out_specs=[HBM],
        input_output_aliases={1: 0},
    )[0]


def tie(*values):
    return lax.optimization_barrier(values)


def solution(mesh):
    nx, ny = mesh.shape["gx"], mesh.shape["gy"]
    devices = [(x, y) for x in range(nx) for y in range(ny)]

    def is_same(x, y):
        return x // (nx // 2) == y // (ny // 2)

    def send(value, along_y, only=None):
        pairs = []
        for x, y in devices:
            if only is None or is_same(x, y) == only:
                to = (x, (y + ny // 2) % ny) if along_y else ((x + nx // 2) % nx, y)
                pairs.append((x * ny + y, to[0] * ny + to[1]))
        return lax.ppermute(value, ("gx", "gy"), pairs)

    def body(leaf):
        e = leaf.shape[1] // 4
        v = lax.axis_index("gx") // (nx // 2)
        u = lax.axis_index("gy") // (ny // 2)
        place = jnp.stack([v, u]).astype(jnp.int32)
        same = u == v
        a = cut_first(place, leaf)
        a_x = send(a, False)
        here, a = tie(place, a)
        hh = cut_side(here, leaf)
        hh_y = send(hh, True)
        swap, outer0, b, c = cut_second(place, leaf)
        swapped = send(swap, True)
        b, factor = gauge(hh, hh_y, b)
        b_x = send(b, False)
        n_last = outer0.shape[0] // T
        c1, c2, rest = scale_cross(factor, c, n_last)
        b, a_x, c1, swapped = tie(b, a_x, c1, swapped)
        b_y = send(b, True)
        a_x, b_y = tie(a_x, b_y)
        a_d = send(a_x, True)
        c1, b_x = tie(c1, b_x)
        c1_x = send(c1, False)
        b_x, b_y = tie(b_x, b_y)
        b_d = send(b_x, True)
        rest, b_d = tie(rest, b_d)
        rest = send(rest, True, only=True)
        side = factor_start((a, a_x, swapped, a_d), (b, b_x, b_y, b_d))
        n_mid = c2.shape[0] // T - n_last
        theirs = jnp.concatenate([c2[: n_mid * T], swapped[-n_last * T :]])
        third, side = tie(jnp.where(same, theirs, c2), side)
        third = send(third, False)
        c1_d = send(c1_x, True, only=True)
        high, low = factor_end(place, side, (b, b_x, b_y, b_d))
        top, bottom, block, part = own_rows(
            place, leaf, high, low, a, c1, c2, a_x, c1_x, swapped, rest
        )
        last, third, block = tie(jnp.where(same, c2[n_mid * T :], outer0), third, block)
        last = send(last, False)
        passed = send(third, True)
        out, block = products(
            place, high, low, top, bottom, block, (a, c1, c2), (a_x, c1_x, third), (a_d, c1_d, passed)
        )
        return finish(
            place, out, high, low, block, part, third, passed, last, swapped, rest, a_d, c1_d
        )

    return jax.shard_map(
        body,
        mesh=mesh,
        in_specs=(P(None, "gy", "gx"),),
        out_specs=P(None, "gy", "gx"),
        check_vma=False,
    )
```

```python
import math

import jax
import jax.numpy as jnp
from jax import lax
from jax.experimental import pallas as pl
from jax.experimental.pallas import tpu as pltpu
from jax.sharding import PartitionSpec as P

F32 = jnp.float32
BF16 = jnp.bfloat16
T = 128
R = 16
FIRST = 2
SECOND = 8
HBM = pl.BlockSpec(memory_space=pl.ANY)
FAR = pl.BlockSpec(memory_space=pltpu.HBM)
VMEM = pl.BlockSpec(memory_space=pltpu.VMEM)
SMEM = pl.BlockSpec(memory_space=pltpu.SMEM)
PARAMS = pltpu.CompilerParams(vmem_limit_bytes=32 * 2**20)


def dot(a, b, dims=((1,), (0,))):
    return lax.dot_general(
        a, b, (dims, ((), ())), precision=lax.Precision.HIGHEST, preferred_element_type=F32
    )


def dot16(a, b, dims=((1,), (0,))):
    return lax.dot_general(a, b, (dims, ((), ())), preferred_element_type=F32)


def split(a):
    high = a.astype(BF16)
    return high, (a - high.astype(F32)).astype(BF16)


def dot3(a, b, dims=((1,), (0,))):
    return dot16(a[0], b[0], dims) + (dot16(a[0], b[1], dims) + dot16(a[1], b[0], dims))


NT = ((1,), (1,))
TN = ((0,), (0,))


def upper(n):
    return [(i, j) for i in range(n) for j in range(i, n)]


def across_lanes(x, k):
    return jnp.broadcast_to(x[:, k : k + 1], x.shape)


def across_rows(x, k):
    return jnp.broadcast_to(x[k : k + 1, :], x.shape)


def panel(rows, c0, lower):
    sub = lax.broadcasted_iota(jnp.int32, rows.shape, 0)
    lane = lax.broadcasted_iota(jnp.int32, rows.shape, 1)
    cols = [across_lanes(rows, c0 + k) for k in range(R)]
    out = jnp.where((lane >= c0) & (lane < c0 + R), (lane - c0 == sub).astype(F32), rows)
    half = out
    scale = jnp.ones_like(rows)
    for k in range(R):
        pivot = across_rows(cols[k], k)
        inv = 1.0 / pivot
        here = sub == k
        mult = cols[k]

        def step(x):
            row = across_rows(x, k) * inv
            return jnp.where(here, row, x - mult * row)

        if lower:
            scale = jnp.where(here, pivot, scale)
            half = half - jnp.where(sub > k, mult, 0.0) * (across_rows(half, k) * inv)
        out = step(out)
        for j in range(k + 1, R):
            cols[j] = step(cols[j])
    return out, half * lax.rsqrt(scale) if lower else None


def put_rows(matrix, rows, r0):
    parts = [matrix[:r0]] if r0 else []
    parts.append(rows)
    if r0 + rows.shape[0] < matrix.shape[0]:
        parts.append(matrix[r0 + rows.shape[0] :])
    return jnp.concatenate(parts, axis=0)


def invert_tile(m, lower=False):
    lane = lax.broadcasted_iota(jnp.int32, (T, T), 1)
    sub = lax.broadcasted_iota(jnp.int32, (T, T), 0)
    rows = m[:R]
    for c0 in range(0, T, R):
        swept, half = panel(rows, c0, lower)
        if c0 + R < T:
            old = m[c0 + R : c0 + 2 * R]
            inside = (lane[:R] >= c0) & (lane[:R] < c0 + R)
            sums = [jnp.where(inside, 0.0, old)] + [None] * 3
            for k in range(R):
                term = across_lanes(old, c0 + k) * across_rows(swept, k)
                sums[k % 4] = -term if sums[k % 4] is None else sums[k % 4] - term
            rows = (sums[0] + sums[1]) + (sums[2] + sums[3])
        wide = put_rows(jnp.zeros((T, T), F32), swept, c0)
        rest = jnp.where((lane >= c0) & (lane < c0 + R), 0.0, m) - dot(m, wide)
        if lower:
            rest = jnp.where(sub < c0, m, rest)
        m = put_rows(rest, half if lower else swept, c0)
    return jnp.where(lane > sub, 0.0, m) if lower else m


def sweep(ref, start, stop):
    n = ref.shape[0]
    for p in range(start, stop, T):
        pivot = invert_tile(ref[p : p + T, p : p + T])
        rows = dot(pivot, ref[p : p + T, :])
        parts = ([rows[:, :p]] if p else []) + [pivot]
        if p + T < n:
            parts.append(rows[:, p + T :])
        rows = jnp.concatenate(parts, axis=1)
        for q in range(0, n, T):
            if q != p:
                change = dot(ref[q : q + T, p : p + T], rows)
                ref[q : q + T, p : p + T] = jnp.zeros((T, T), F32)
                ref[q : q + T, :] = ref[q : q + T, :] - change
        ref[p : p + T, :] = rows


def inverse_factor(ref):
    n = ref.shape[0]
    for p in range(0, n, T):
        pivot = invert_tile(ref[p : p + T, p : p + T], lower=True)
        scaled = dot(pivot, ref[p : p + T, :])
        for q in range(p + T, n, T):
            weight = scaled[:, q : q + T]
            ref[q : q + T, :] = ref[q : q + T, :] - dot(weight, scaled, TN)
            ref[q : q + T, p : p + T] = -dot(weight, pivot, TN)
        for q in range(0, n, T):
            if q < p:
                ref[p : p + T, q : q + T] = scaled[:, q : q + T]
            else:
                ref[p : p + T, q : q + T] = pivot if q == p else jnp.zeros((T, T), F32)


def leaf_block(leaf, side_r, side_c, r, c, size):
    e = leaf.shape[1] // 4
    return leaf.at[
        0,
        pl.ds(pl.multiple_of(side_r * e + r * size, T), size),
        pl.ds(pl.multiple_of(side_c * e + c * size, T), size),
    ]


def run_copies(pairs, sem):
    copies = [pltpu.make_async_copy(a, b, sem.at[i]) for i, (a, b) in enumerate(pairs)]
    for copy in copies:
        copy.start()
    for copy in copies:
        copy.wait()


def sides(place):
    v, u = place[0], place[1]
    return [v, 2 + u], [1 - v, 3 - u]


def unpack(ref, at, tiles):
    held = {}
    for r, c in upper(tiles):
        held[r, c] = ref[at : at + T, :]
        if c > r:
            held[c, r] = held[r, c].T
        at += T
    return jnp.concatenate(
        [jnp.concatenate([held[r, c] for c in range(tiles)], axis=1) for r in range(tiles)], axis=0
    )


def call(kernel, name, cost, outs, ins, scratch, **more):
    return pl.pallas_call(
        kernel,
        out_shape=[jax.ShapeDtypeStruct(shape, dtype) for shape, dtype in outs],
        in_specs=[spec for spec, _ in ins],
        out_specs=more.pop("out_specs", [VMEM] * len(outs)),
        scratch_shapes=scratch,
        compiler_params=PARAMS,
        cost_estimate=pl.CostEstimate(flops=cost, bytes_accessed=cost, transcendentals=0),
        name=name,
        **more,
    )(*[value for _, value in ins])


def block_tiles(leaf, side_r, side_c, at):
    tiles = leaf.shape[1] // 4 // T
    return leaf_block(leaf, side_r, side_c, at // tiles, at % tiles, T)


def cross_tile(leaf, ext, inn, at):
    n = (leaf.shape[1] // 4 // T) ** 2
    return block_tiles(leaf, ext[at // n % 2], inn[at // n // 2], at % n)


def cut_first_kernel(place, leaf, a, sem):
    tiles = leaf.shape[1] // 4 // T
    ext, inn = sides(place)
    n_sym = len(upper(tiles))
    pairs = []
    for at, (r, c) in enumerate(upper(tiles)):
        pairs.append((leaf_block(leaf, inn[0], inn[0], r, c, T), a.at[pl.ds(at * T, T)]))
    for at in range(FIRST):
        pairs.append(
            (cross_tile(leaf, ext, inn, at), a.at[pl.ds((n_sym + at) * T, T)])
        )
    run_copies(pairs, sem)


def cut_first(place, leaf):
    n_sym = len(upper(leaf.shape[1] // 4 // T))
    return call(
        cut_first_kernel,
        "cut_first",
        1000 * 10**6,
        [(((n_sym + FIRST) * T, T), F32)],
        [(SMEM, place), (FAR, leaf)],
        [pltpu.SemaphoreType.DMA((n_sym + FIRST,))],
    )[0]


def cut_side_kernel(place, leaf, hh, sem):
    tiles = leaf.shape[1] // 4 // T
    _, inn = sides(place)
    pairs = []
    for at, (r, c) in enumerate(upper(tiles)):
        pairs.append((leaf_block(leaf, inn[1], inn[1], r, c, T), hh.at[pl.ds(at * T, T)]))
    run_copies(pairs, sem)


def cut_side(place, leaf):
    n_sym = len(upper(leaf.shape[1] // 4 // T))
    return call(
        cut_side_kernel,
        "cut_side",
        1000 * 10**6,
        [((n_sym * T, T), F32)],
        [(SMEM, place), (FAR, leaf)],
        [pltpu.SemaphoreType.DMA((n_sym,))],
    )[0]


def cut_second_kernel(place, leaf, swap, outer0, b, c, sem):
    e = leaf.shape[1] // 4
    tiles = e // T
    ext, inn = sides(place)
    n_sym = len(upper(tiles))
    pairs = [
        (leaf_block(leaf, inn[0], inn[1], 0, 0, e), b),
        (leaf_block(leaf, ext[0], inn[0], 0, 0, e), c.at[pl.ds(0, e)]),
        (leaf_block(leaf, ext[1], inn[0], 0, 0, e), c.at[pl.ds(e, e)]),
        (leaf_block(leaf, ext[0], inn[1], 0, 0, e), c.at[pl.ds(2 * e, e)]),
        (leaf_block(leaf, ext[1], inn[1], 0, 0, e), c.at[pl.ds(3 * e, e)]),
    ]
    for at, (r, k) in enumerate(upper(tiles)):
        pairs.append((leaf_block(leaf, inn[0], inn[0], r, k, T), swap.at[pl.ds(at * T, T)]))
    half = outer0.shape[0] // T
    second = []
    for at, (r, k) in enumerate(upper(2 * tiles)):
        source = leaf_block(leaf, ext[r // tiles], ext[k // tiles], r % tiles, k % tiles, T)
        if at < half:
            pairs.append((source, outer0.at[pl.ds(at * T, T)]))
        else:
            second.append((source, swap.at[pl.ds((n_sym + at - half) * T, T)]))
    run_copies(pairs, sem)
    same = place[0] == place[1]

    @pl.when(same)
    def _():
        cross = [
            (cross_tile(leaf, ext, inn, at), swap.at[pl.ds((n_sym + at) * T, T)])
            for at in range(half)
        ]
        run_copies(cross, sem)

    @pl.when(jnp.logical_not(same))
    def _():
        run_copies(second, sem)


def cut_second(place, leaf):
    e = leaf.shape[1] // 4
    n_sym = len(upper(e // T))
    half = len(upper(2 * (e // T))) // 2
    return call(
        cut_second_kernel,
        "cut_second",
        1000 * 10**6,
        [(((n_sym + half) * T, T), F32), ((half * T, T), F32), ((e, e), F32), ((4 * e, e), F32)],
        [(SMEM, place), (HBM, leaf)],
        [pltpu.SemaphoreType.DMA((n_sym + half + 5,))],
    )


def gauge_kernel(mine, along, b, b_out, factor):
    e = factor.shape[0]
    tiles = e // T
    factor[...] = unpack(mine, 0, tiles) + unpack(along, 0, tiles)
    inverse_factor(factor)
    b_out[...] = dot(b[...], factor[...], NT)


def gauge(mine, along, b):
    e = b.shape[0]
    return call(
        gauge_kernel,
        "gauge_side",
        8000 * 10**6,
        [((e, e), F32), ((e, e), F32)],
        [(VMEM, x) for x in (mine, along, b)],
        [],
    )


def scale_kernel(factor, c, c1, c2, rest):
    e = factor.shape[0]
    tiles = e // T
    scaled = dot3(split(c[2 * e :, :]), split(factor[...]), NT)
    total = 4 * tiles * tiles
    for at in range(FIRST, total):
        r, k = at // tiles * T, at % tiles * T
        tile = c[r : r + T, k : k + T] if r < 2 * e else scaled[r - 2 * e : r - 2 * e + T, k : k + T]
        if at < FIRST + SECOND:
            c1[(at - FIRST) * T : (at - FIRST + 1) * T, :] = tile
        else:
            c2[(at - FIRST - SECOND) * T : (at - FIRST - SECOND + 1) * T, :] = tile
        spot = at * T - (total * T - rest.shape[0])
        if spot >= 0:
            rest[spot : spot + T, :] = tile


def scale_cross(factor, c, swapped):
    e = factor.shape[0]
    total = 4 * e * e // T
    return call(
        scale_kernel,
        "scale_cross",
        2000 * 10**6,
        [((n, T), F32) for n in (SECOND * T, total - (FIRST + SECOND) * T, total - swapped * T)],
        [(VMEM, x) for x in (factor, c)],
        [],
    )


def couple(b):
    mine, across, along, corner = (ref[...] for ref in b)
    return jnp.concatenate(
        [jnp.concatenate([mine, across], axis=1), jnp.concatenate([along, corner], axis=1)], axis=0
    )


def factor_start_kernel(a0, a1, a2, a3, b0, b1, b2, b3, side):
    e = b0.shape[0]
    tiles = e // T
    coup = couple((b0, b1, b2, b3))
    side[...] = -dot(coup, coup, NT)
    side[:e, :e] = side[:e, :e] + (unpack(a0, 0, tiles) + unpack(a1, 0, tiles))
    side[e:, e:] = side[e:, e:] + (unpack(a2, 0, tiles) + unpack(a3, 0, tiles))
    sweep(side, 0, e)


def factor_start(a, b):
    e = b[0].shape[0]
    return call(
        factor_start_kernel,
        "factor_start",
        1000 * 10**6,
        [((2 * e, 2 * e), F32)],
        [(VMEM, x) for x in (*a, *b)],
        [],
    )[0]


def factor_end_kernel(place, side_in, b0, b1, b2, b3, high, low, side, full):
    e = b0.shape[0]
    side[...] = side_in[...]
    sweep(side, e, 2 * e)
    coup = split(couple((b0, b1, b2, b3)))
    away = dot3(split(side[...]), coup)
    shape = full.shape
    unit = lax.broadcasted_iota(jnp.int32, shape, 0) == lax.broadcasted_iota(jnp.int32, shape, 1)
    full[...] = dot3(coup, split(away), TN) + unit.astype(F32)

    def emit(value, rows, columns):
        high[rows, columns], low[rows, columns] = split(value)

    first, rest = slice(0, e), slice(e, 3 * e)
    emit(full[...], rest, rest)
    emit(-away[:e, :], first, rest)
    same = place[0] == place[1]

    @pl.when(same)
    def _():
        emit(side[:e, :e], first, first)
        emit(-away[:e, :].T, rest, first)

    @pl.when(jnp.logical_not(same))
    def _():
        emit(side[:e, e:], first, first)
        emit(-away[e:, :].T, rest, first)


def factor_end(place, side, b):
    e = b[0].shape[0]
    return call(
        factor_end_kernel,
        "factor_end",
        10000 * 10**6,
        [((3 * e, 3 * e), BF16)] * 2,
        [(SMEM, place), (VMEM, side)] + [(VMEM, x) for x in b],
        [pltpu.VMEM((2 * e, 2 * e), F32), pltpu.VMEM((2 * e, 2 * e), F32)],
    )


def cross_block(*pieces):
    held = []
    for ref, skip in pieces:
        for at in range(skip * T, ref.shape[0], T):
            held.append(ref[at : at + T, :])
    tiles = math.isqrt(len(held) // 4)
    rows = []
    for r in range(2 * tiles):
        side = r // tiles
        row = [held[((side + 2 * c) * tiles + r % tiles) * tiles + k] for c in range(2) for k in range(tiles)]
        rows.append(jnp.concatenate(row, axis=1))
    return jnp.concatenate(rows, axis=0)


def symmetric_tiles(e):
    return len(upper(e // T))


def zeros(tiles):
    return jnp.zeros((tiles * T, T), F32), 0


def times_inverse(cross, high, low, inner):
    e = cross.shape[1] // 2
    return dot3(split(cross[:, :e]), (high[:e], low[:e])) + dot3(
        split(cross[:, e:]), (high[inner], low[inner])
    )


def rows_kernel(
    place, leaf, high, low, a0, c01, c02, a1, c11, swapped, rest, top, bottom, block, part, col, own, sem
):
    e = leaf.shape[1] // 4
    n_sym = symmetric_tiles(e)
    ext, _ = sides(place)
    copies = []
    for r in range(2):
        for c in range(2):
            target = own.at[pl.ds(r * e, e), pl.ds(c * e, e)]
            source = leaf_block(leaf, ext[r], ext[c], 0, 0, e)
            copies.append(pltpu.make_async_copy(source, target, sem.at[2 * r + c]))
            copies[-1].start()
    same = place[0] == place[1]
    mine = cross_block((a0, n_sym), (c01, 0), (c02, 0))

    @pl.when(same)
    def _():
        col[...] = mine

    @pl.when(jnp.logical_not(same))
    def _():
        col[...] = cross_block((swapped, n_sym), (rest, 0))
        across = cross_block((a1, n_sym), (c11, 0), zeros(c02.shape[0] // T))
        part[...] = times_inverse(across, high[...], low[...], slice(2 * e, 3 * e))

    left = split(times_inverse(mine, high[...], low[...], slice(e, 2 * e)))
    top[...], bottom[...] = left
    left = [x[:, : 2 * e] for x in left]
    block[...] = -dot3(left, split(col[...]), NT)
    for copy in copies:
        copy.wait()

    @pl.when(same)
    def _():
        block[...] = block[...] + own[...]


def own_rows(place, leaf, high, low, a0, c01, c02, a1, c11, swapped, rest):
    e = leaf.shape[1] // 4
    return call(
        rows_kernel,
        "own_rows",
        500 * 10**6,
        [((2 * e, 3 * e), BF16)] * 2 + [((2 * e, 2 * e), F32), ((2 * e, 3 * e), F32)],
        [(SMEM, place), (HBM, leaf)]
        + [(VMEM, x) for x in (high, low, a0, c01, c02, a1, c11, swapped, rest)],
        [
            pltpu.VMEM((2 * e, 2 * e), F32),
            pltpu.VMEM((2 * e, 2 * e), F32),
            pltpu.SemaphoreType.DMA((4,)),
        ],
    )


def spot(place, e, side, which):
    x = place[0] if which == 0 else 1 - place[0]
    return pl.ds(pl.multiple_of((2 * side + x) * e, T), e)


def put(out, place, held, a, b, sem):
    e = out.shape[1] // 4
    copies = []
    for r in range(2):
        for c in range(2):
            source = held.at[pl.ds(r * e, e), pl.ds(c * e, e)]
            target = out.at[0, spot(place, e, r, a), spot(place, e, c, b)]
            copies.append(pltpu.make_async_copy(source, target, sem.at[2 * r + c]))
            copies[-1].start()
    return copies


def wait(copies):
    for copy in copies:
        copy.wait()


def pick(ref, rows, b):
    e = ref.shape[1] // 3
    return jnp.concatenate([ref[rows, :e], ref[rows, (1 + b) * e : (2 + b) * e]], axis=1)


def products_kernel(
    place, high, low, top, bottom, block, a0, c01, c02, a1, c11, third, a3, c31, passed, out, part, held, scratch, sem
):
    e = out.shape[1] // 4
    n_sym = symmetric_tiles(e)
    same = place[0] == place[1]
    first = put(out, place, block, 0, 0, sem.at[0])
    everything = slice(0, 2 * e)

    @pl.when(same)
    def _():
        across = cross_block((a1, n_sym), (c11, 0), (third, 0))
        right = split(across)
        left = [pick(x, everything, 1) for x in (top, bottom)]
        held[0] = -dot3(left, right, NT)
        copies = put(out, place, held.at[0], 0, 1, sem.at[1])
        scratch[...] = times_inverse(across, high[...], low[...], slice(2 * e, 3 * e))
        left = split(pick(scratch, everything, 0))
        mine = cross_block((a0, n_sym), (c01, 0), (c02, 0))
        held[1] = -dot3(left, split(mine), NT)
        copies += put(out, place, held.at[1], 1, 0, sem.at[2])
        left = split(pick(scratch, everything, 1))
        part[...] = -dot3(left, right, NT)
        wait(copies)

    @pl.when(jnp.logical_not(same))
    def _():
        right = split(cross_block((a3, n_sym), (c31, 0), (passed, 0)))
        left = [pick(x, everything, 1) for x in (top, bottom)]
        held[0] = -dot3(left, right, NT)
        wait(put(out, place, held.at[0], 0, 1, sem.at[1]))

    wait(first)


def products(place, high, low, top, bottom, block, mine, across, corner):
    e = block.shape[0] // 2
    return call(
        products_kernel,
        "products",
        500 * 10**6,
        [((1, 4 * e, 4 * e), F32), ((2 * e, 2 * e), F32)],
        [(SMEM, place)]
        + [(VMEM, x) for x in (high, low, top, bottom, block, *mine, *across, *corner)],
        [
            pltpu.VMEM((2, 2 * e, 2 * e), F32),
            pltpu.VMEM((2 * e, 3 * e), F32),
            pltpu.SemaphoreType.DMA((3, 4)),
        ],
        out_specs=[HBM, VMEM],
    )


def finish_kernel(
    place, before, high, low, block, part, third, passed, last, swapped, rest, a3, c31, out, held, scratch, sem
):
    e = out.shape[1] // 4
    tiles = e // T
    n_sym = symmetric_tiles(e)

    def targets(b):
        return [
            (
                held.at[pl.ds(r * e, e), pl.ds((2 * b + c) * e, e)],
                out.at[0, spot(place, e, r, 1), spot(place, e, c, b)],
            )
            for r in range(2)
            for c in range(2)
        ]

    n_last = last.shape[0] // T

    @pl.when(place[0] == place[1])
    def _():
        skip = passed.shape[0] // T - n_last
        for at, (i, j) in enumerate(upper(2 * tiles)):
            ref, at = (last, at) if at < n_last else (passed, at - n_last + skip)
            piece = ref[at * T : (at + 1) * T, :]
            r, c = slice(i * T, (i + 1) * T), slice(j * T, (j + 1) * T)
            shift = 2 * e
            held[r, j * T + shift : (j + 1) * T + shift] = block[r, c] + piece
            if i != j:
                held[c, i * T + shift : (i + 1) * T + shift] = block[c, r] + piece.T
        run_copies(targets(1), sem)

    @pl.when(place[0] != place[1])
    def _():
        first = third[: third.shape[0] - n_last * T, :]
        late = cross_block(zeros(FIRST + SECOND), (first, 0), (last, 0))[:, e:]
        inner = slice(2 * e, 3 * e)
        scratch[...] = part[...] + dot3(split(late), (high[inner], low[inner]))
        everything = slice(0, 2 * e)
        copies = []
        for b in range(2):
            if b == 0:
                col = cross_block((swapped, n_sym), (rest, 0))
            else:
                col = cross_block((a3, n_sym), (c31, 0), (passed, 0))
            left = split(pick(scratch, everything, b))
            held[:, 2 * e * b : 2 * e * (b + 1)] = -dot3(left, split(col), NT)
            for i, (source, target) in enumerate(targets(b)):
                copies.append(pltpu.make_async_copy(source, target, sem.at[4 * b + i]))
                copies[-1].start()
        for copy in copies:
            copy.wait()


def finish(place, before, high, low, block, part, third, passed, last, swapped, rest, a3, c31):
    e = before.shape[1] // 4
    return call(
        finish_kernel,
        "finish",
        500 * 10**6,
        [(before.shape, F32)],
        [(SMEM, place), (HBM, before)]
        + [
            (VMEM, x)
            for x in (high, low, block, part, third, passed, last, swapped, rest, a3, c31)
        ],
        [
            pltpu.VMEM((2 * e, 4 * e), F32),
            pltpu.VMEM((2 * e, 3 * e), F32),
            pltpu.SemaphoreType.DMA((8,)),
        ],
        out_specs=[HBM],
        input_output_aliases={1: 0},
    )[0]


def tie(*values):
    return lax.optimization_barrier(values)


def solution(mesh):
    nx, ny = mesh.shape["gx"], mesh.shape["gy"]
    devices = [(x, y) for x in range(nx) for y in range(ny)]

    def is_same(x, y):
        return x // (nx // 2) == y // (ny // 2)

    def send(value, along_y, only=None):
        pairs = []
        for x, y in devices:
            if only is None or is_same(x, y) == only:
                to = (x, (y + ny // 2) % ny) if along_y else ((x + nx // 2) % nx, y)
                pairs.append((x * ny + y, to[0] * ny + to[1]))
        return lax.ppermute(value, ("gx", "gy"), pairs)

    def body(leaf):
        e = leaf.shape[1] // 4
        v = lax.axis_index("gx") // (nx // 2)
        u = lax.axis_index("gy") // (ny // 2)
        place = jnp.stack([v, u]).astype(jnp.int32)
        same = u == v
        a = cut_first(place, leaf)
        a_x = send(a, False)
        here, a = tie(place, a)
        hh = cut_side(here, leaf)
        hh_y = send(hh, True)
        swap, outer0, b, c = cut_second(place, leaf)
        swapped = send(swap, True)
        b, factor = gauge(hh, hh_y, b)
        b_x = send(b, False)
        n_last = outer0.shape[0] // T
        c1, c2, rest = scale_cross(factor, c, n_last)
        b, a_x, c1, swapped = tie(b, a_x, c1, swapped)
        b_y = send(b, True)
        a_x, b_y = tie(a_x, b_y)
        a_d = send(a_x[: a_x.shape[0] - T], True)
        c1, b_x = tie(c1, b_x)
        c1_x = send(c1, False)
        b_x, b_y = tie(b_x, b_y)
        b_d = send(b_x, True)
        rest, b_d = tie(rest, b_d)
        rest = send(rest, True, only=True)
        side = factor_start((a, a_x, swapped, a_d), (b, b_x, b_y, b_d))
        n_mid = c2.shape[0] // T - n_last
        theirs = jnp.concatenate([c2[: n_mid * T], swapped[-n_last * T :]])
        third, side = tie(jnp.where(same, theirs, c2), side)
        third = send(third, False)
        c1_x, side = tie(c1_x, side)
        c1_d = send(jnp.concatenate([a_x[-T:], c1_x]), True, only=True)
        high, low = factor_end(place, side, (b, b_x, b_y, b_d))
        top, bottom, block, part = own_rows(
            place, leaf, high, low, a, c1, c2, a_x, c1_x, swapped, rest
        )
        last, third, block = tie(jnp.where(same, c2[n_mid * T :], outer0), third, block)
        last = send(last, False)
        passed = send(third, True)
        out, block = products(
            place, high, low, top, bottom, block, (a, c1, c2), (a_x, c1_x, third), (a_d, c1_d, passed)
        )
        return finish(
            place, out, high, low, block, part, third, passed, last, swapped, rest, a_d, c1_d
        )

    return jax.shard_map(
        body,
        mesh=mesh,
        in_specs=(P(None, "gy", "gx"),),
        out_specs=P(None, "gy", "gx"),
        check_vma=False,
    )
```
